256 devices in a mesh: blk: 64 (over z, y, x_hi), mp: 4 (over x_lo, core).
Axes of the slice: x: 4 (x_hi: 2, x_lo: 2; x = x_hi * 2 + x_lo), y: 4, z: 8, core: 2. Of those that a mesh axis runs over, the one named last changes fastest.
Arguments:
- dna_ids: int32 [24576, 16], P('blk'), may hold values from 0 to 4095
- meth_ids: int32 [24576, 16], P('blk'), may hold values from 0 to 511
- pair_index: int32 [24576], P('blk'), may hold values from 0 to 24575, each once
- dna_table: bfloat16 [4096, 1024], P(None, 'mp'), may hold values from -6 to 6
- meth_table: bfloat16 [512, 768], replicated, may hold values from -6 to 6
- dna_proj: bfloat16 [1024, 512], P('mp'), may hold values from -0.1875 to 0.1875
- meth_proj: bfloat16 [768, 512], replicated, may hold values from -0.21875 to 0.21875
- logit_scale: float32 [1], replicated, may hold values from 40 to 64
- logit_bias: float32 [1], replicated, may hold values from -8 to -6
Outputs:
- grad_dna_proj: float32 [1024, 512], P('mp')
- grad_meth_proj: float32 [768, 512], replicated
The draws below stay inside these ranges and needn't reach their ends.
Inputs may be any that keep to these rules, and one draw needn't show every extreme that they name: `pair_index`: every methylation window is paired with exactly one DNA window.
All inputs are finite; a program needn't handle non-finite values.
Results may differ from the reference program's by a relative error of at most 0.00085.
Values may be sent and summed in bfloat16 or wider, within the bound.
A program may use at most 128 MiB of HBM per device.

```python
import jax
import jax.numpy as jnp
from jax import lax

D_DNA = 1024
D_METH = 768
E = 512
VOCAB_DNA = 4096
VOCAB_METH = 512
TOK_DNA = 16
TOK_METH = 16
PAIR_DEV = 384
PAIRS = 24576
N_BLK = 64


def touch_ends(values, rng, low, largest):
    dims = values.shape
    spot = [jax.random.randint(jax.random.fold_in(rng, axis), (), 0, dims[axis]) for axis in range(len(dims))]
    values = values.at[tuple(spot)].set(low)
    longest = dims.index(max(dims))
    spot[longest] = (spot[longest] + 1) % dims[longest]
    return values.at[tuple(spot)].set(largest)


def block_scale(stream_key, dims, shards, low, top_value):
    level = 1.0
    for dim, blocks in shards:
        steps = jax.random.uniform(jax.random.fold_in(jax.random.fold_in(stream_key, 6), dim), (blocks,), jnp.float32, low / len(shards), top_value / len(shards))
        level = level * jnp.repeat(jnp.exp(steps), dims[dim] // blocks).reshape((-1,) + (1,) * (len(dims) - 1 - dim))
    return level


def centred(own_key, extent, width, limit, shards=(), kind=jnp.bfloat16):
    result = width * jax.random.normal(own_key, extent, jnp.float32)
    if shards:
        result = result * block_scale(own_key, extent, shards, -0.22, 0.18)
    return jnp.clip(result, -limit, limit).astype(kind)


def setup_inputs(seed: int = 0) -> dict:
    arg_keys = jax.random.split(jax.random.key(seed), 10)
    return {
        "dna_ids": touch_ends(jax.random.randint(arg_keys[0], (PAIRS, TOK_DNA), 0, VOCAB_DNA), jax.random.fold_in(arg_keys[0], 1), 0, VOCAB_DNA - 1).astype(jnp.int32),
        "meth_ids": touch_ends(jax.random.randint(arg_keys[1], (PAIRS, TOK_METH), 0, VOCAB_METH), jax.random.fold_in(arg_keys[1], 1), 0, VOCAB_METH - 1).astype(jnp.int32),
        "pair_index": jax.random.permutation(arg_keys[2], PAIRS).astype(jnp.int32),
        "dna_table": centred(arg_keys[3], (VOCAB_DNA, D_DNA), 1.0, 6.0, ((1, 4),)),
        "meth_table": centred(arg_keys[4], (VOCAB_METH, D_METH), 1.0, 6.0),
        "dna_proj": centred(arg_keys[5], (D_DNA, E), D_DNA ** -0.5, 0.1875, ((0, 4),)),
        "meth_proj": centred(arg_keys[6], (D_METH, E), D_METH ** -0.5, 0.21875),
        "logit_scale": jnp.clip(jax.random.uniform(arg_keys[7], (1,), jnp.float32, 40.0, 64.0), 40.0, 64.0),
        "logit_bias": jnp.clip(jax.random.uniform(arg_keys[8], (1,), jnp.float32, -8.0, -6.0), -8.0, -6.0),
    }


epsilon = 1e-06

def pool_rows(lookup, token_ids):
    blocks = token_ids.reshape(N_BLK, PAIR_DEV, token_ids.shape[1])

    def pool_block(block_ids):
        gathered = jnp.take(lookup, block_ids, axis=0).astype(jnp.float32)
        return lax.optimization_barrier(jnp.mean(gathered, axis=1)).astype(jnp.bfloat16)
    return lax.map(pool_block, blocks).reshape(PAIRS, lookup.shape[1])

def normalize_rows(pooled, weight):
    raw_rows = jnp.dot(pooled, weight, preferred_element_type=jnp.float32)
    inverse = lax.rsqrt(lax.optimization_barrier(jnp.sum(raw_rows * raw_rows, axis=1, keepdims=True)) + epsilon)
    return (inverse, raw_rows * inverse)

def normal_grad(inverse, unit_rows, upstream):
    inner = lax.optimization_barrier(jnp.sum(unit_rows * upstream, axis=1, keepdims=True))
    return (inverse * (upstream - unit_rows * inner)).astype(jnp.bfloat16)

def contract_rows(left, right):
    return lax.dot_general(left, right, (((0,), (0,)), ((), ())), preferred_element_type=jnp.float32)

def reference(dna_ids, meth_ids, pair_index, dna_table, meth_table, dna_proj, meth_proj, logit_scale, logit_bias):
    dna_pooled = pool_rows(dna_table, dna_ids)
    meth_pooled = pool_rows(meth_table, meth_ids)
    dna_inverse, dna_unit = normalize_rows(dna_pooled, dna_proj)
    meth_inverse, meth_unit = normalize_rows(meth_pooled, meth_proj)
    dna_rows = dna_unit.astype(jnp.bfloat16)
    meth_rows = meth_unit.astype(jnp.bfloat16)
    scale_value = logit_scale[0]
    bias_value = logit_bias[0]
    columns = jnp.arange(PAIRS, dtype=jnp.int32)

    def row_block(col_total, inputs):
        row_embed, partner = inputs
        logits = scale_value * jnp.dot(row_embed, meth_rows.T, preferred_element_type=jnp.float32) + bias_value
        labels = (partner[:, None] == columns[None, :]).astype(jnp.float32)
        grad_tile = (jax.nn.sigmoid(logits) - labels).astype(jnp.bfloat16)
        row_total = jnp.dot(grad_tile, meth_rows, preferred_element_type=jnp.float32)
        col_total = col_total + contract_rows(grad_tile, row_embed)
        return (col_total, row_total)
    col_total, row_totals = lax.scan(row_block, jnp.zeros((PAIRS, E), jnp.float32), (dna_rows.reshape(N_BLK, PAIR_DEV, E), pair_index.reshape(N_BLK, PAIR_DEV)))
    row_sum = scale_value * row_totals.reshape(PAIRS, E)
    col_sum = scale_value * col_total
    dna_back = normal_grad(dna_inverse, dna_unit, row_sum)
    meth_back = normal_grad(meth_inverse, meth_unit, col_sum)
    grad_dna_proj = contract_rows(dna_pooled, dna_back)
    grad_meth_proj = contract_rows(meth_pooled, meth_back)
    return (grad_dna_proj, grad_meth_proj)
```

```python
import jax
import jax.numpy as jnp
from jax import lax
from jax.experimental import pallas as pl
from jax.experimental.pallas import tpu as pltpu
from jax.sharding import PartitionSpec as P

MESH = pl.DeviceIdType.MESH
F32 = jnp.float32
BF16 = jnp.bfloat16
EPS = 1e-06

PAIR_DEV = 384
ROWS = 2 * PAIR_DEV
COLS = 8 * PAIR_DEV
E = 512
D_SLICE = 256
D_METH = 768
VOCAB_DNA = 4096
VOCAB_METH = 512
CHUNK = 512
M_HALF = 384
N_COPIES = 64

NT = (((1,), (1,)), ((), ()))


def place():
    blk, mp = lax.axis_index("blk"), lax.axis_index("mp")
    z = lax.div(blk, 8)
    y = lax.rem(lax.div(blk, 2), 4)
    x = lax.rem(blk, 2) * 2 + lax.div(mp, 2)
    return blk, mp, z, y, x, lax.rem(mp, 2)


def device_at(z, y, x, core):
    return (z * 8 + y * 2 + lax.div(x, 2), lax.rem(x, 2) * 2 + core)


def signal(device):
    pl.semaphore_signal(
        pltpu.get_barrier_semaphore(), inc=1, device_id=device, device_id_type=MESH
    )


def send(src, dst, send_sem, recv_sem, device):
    return pltpu.make_async_remote_copy(
        src_ref=src,
        dst_ref=dst,
        send_sem=send_sem,
        recv_sem=recv_sem,
        device_id=device,
        device_id_type=MESH,
    )


def step_kernel(
    dna_ids,
    meth_ids,
    pairs,
    dna_table_hbm,
    meth_table_hbm,
    dna_proj,
    meth_proj_hbm,
    scale_ref,
    bias_ref,
    d_out,
    m_out,
    dna_table,
    meth_table,
    meth_proj,
    dna_tokens,
    counts,
    ids_all,
    pair_all,
    pair_wide,
    dna_pooled,
    dna_projt,
    meth_tablet,
    meth_projt,
    meth_counts,
    meth_pooled,
    meth_unit,
    meth_rows,
    meth_inv,
    dna_unit,
    dna_inv,
    dna_rowst,
    dna_rows,
    row_acc,
    m_acc,
    m_sib,
    m_first,
    m_first_in,
    m_second,
    m_second_in,
    back_all,
    back_sib,
    back_half,
    back_in,
    d_first,
    d_first_in,
    third,
    third_in,
    third_all,
    m_all,
    d_slab,
    d_fin,
    ids_send,
    ids_recv,
    send_sems,
    recv_sems,
    local_sems,
):
    blk, mp, z, y, x, core = place()
    x_hi = lax.div(x, 2)
    sibling = device_at(z, y, x, 1 - core)
    ring = [device_at(z, y, lax.rem(x + o, 4), core) for o in range(4)]
    cross = [device_at(z, y, lax.rem(x + o, 4), 1 - core) for o in range(4)]
    along_y = [device_at(z, lax.rem(y + o, 4), x, core) for o in range(4)]
    along_z = [device_at(lax.rem(z + o, 8), y, x, core) for o in range(8)]
    slot = lax.rem(blk, 8)
    block = x_hi * 4 + mp
    taken = []

    def post(src, dst, device):
        n = len(taken)
        copy = send(src, dst, send_sems.at[n], recv_sems.at[n], device)
        taken.append(copy)
        return copy

    fetch = [
        pltpu.make_async_copy(src, dst, local_sems.at[1 + n])
        for n, (src, dst) in enumerate(
            ((dna_table_hbm, dna_table), (meth_table_hbm, meth_table), (meth_proj_hbm, meth_proj))
        )
    ]
    for copy in fetch:
        copy.start()

    targets = [device_at(s, mp, lax.div(z, 2), lax.rem(z, 2)) for s in range(8)]
    sources = [device_at(block, s // 2, (s % 2) * 2 + lax.div(y, 2), lax.rem(y, 2)) for s in range(8)]

    def is_me(device):
        return jnp.logical_and(device[0] == blk, device[1] == mp)

    for s in range(8):

        @pl.when(jnp.logical_not(is_me(sources[s])))
        def _():
            signal(sources[s])

    for o in (1, 2, 3):
        signal(ring[o])
        signal(cross[o])
        signal(along_y[o])
    for o in range(1, 8):
        signal(along_z[o])
    signal(sibling)
    to_self = jnp.logical_and(mp == y, block == z).astype(jnp.int32)
    pl.semaphore_wait(pltpu.get_barrier_semaphore(), 25 - to_self)

    def ids_copy(s):
        lanes = pl.ds(pl.multiple_of(slot * PAIR_DEV, 128), PAIR_DEV)
        return send(meth_ids, ids_all.at[:, lanes], ids_send.at[s], ids_recv.at[slot], targets[s])

    def ids_arrival(s):
        lanes = pl.ds(s * PAIR_DEV, PAIR_DEV)
        return send(meth_ids, ids_all.at[:, lanes], ids_send.at[s], ids_recv.at[s], sources[s])

    for s in range(8):

        @pl.when(jnp.logical_not(is_me(targets[s])))
        def _():
            ids_copy(s).start()

        @pl.when(is_me(targets[s]))
        def _():
            lanes = pl.ds(pl.multiple_of(slot * PAIR_DEV, 128), PAIR_DEV)
            local = pltpu.make_async_copy(meth_ids, ids_all.at[:, lanes], local_sems.at[0])
            local.start()
            local.wait()

    pair_copy = post(pairs, pair_all.at[x_hi], ring[2])
    pair_copy.start()
    pair_all[x_hi] = pairs[...]

    dna_projt[mp] = dna_proj[...].T
    toward = 1 + 2 * core
    far = device_at(z, y, lax.rem(x + toward, 4), core)
    other_mp = lax.rem(mp + 2, 4)
    proj_far = post(dna_projt.at[mp], dna_projt.at[mp], far)
    proj_sib = post(dna_projt.at[mp], dna_projt.at[mp], sibling)
    proj_fwd = post(dna_projt.at[other_mp], dna_projt.at[other_mp], sibling)
    proj_far.start()
    proj_sib.start()

    dna_tokens[...] = dna_ids[...].T

    def count_dna(i, carry):
        rows = pl.ds(pl.multiple_of(i * 16, 16), 16)
        ids = dna_tokens[rows, :]
        place_of = jnp.bitwise_and(ids, VOCAB_DNA // 4 - 1)
        amount = jnp.left_shift(1, jnp.right_shift(ids, 10) * 8)
        lane = lax.broadcasted_iota(jnp.int32, (16, VOCAB_DNA // 4), 1)
        total = jnp.zeros((16, VOCAB_DNA // 4), jnp.int32)
        for t in range(16):
            total = total + jnp.where(lane == place_of[:, t : t + 1], amount[:, t : t + 1], 0)
        for f in range(4):
            field = jnp.bitwise_and(jnp.right_shift(total, 8 * f), 255)
            counts[rows, f * 1024 : (f + 1) * 1024] = field.astype(F32).astype(BF16)
        return carry

    lax.fori_loop(0, PAIR_DEV // 16, count_dna, 0)
    fetch[0].wait()
    pooled = jnp.dot(counts[...], dna_table[...], preferred_element_type=F32) * 0.0625
    own_lanes = pl.ds(pl.multiple_of(x_hi * PAIR_DEV, 128), PAIR_DEV)
    dna_pooled[mp, :, own_lanes] = pooled.T.astype(BF16)

    def pool_block(x_of, core_of):
        lanes = pl.ds(pl.multiple_of(lax.div(x_of, 2) * PAIR_DEV, 128), PAIR_DEV)
        return dna_pooled.at[lax.rem(x_of, 2) * 2 + core_of, :, lanes]

    own = pool_block(x, core)
    pool_far = [post(own, own, ring[o]) for o in (1, 2, 3)]
    pool_sib = post(own, own, sibling)
    for copy in pool_far:
        copy.start()
    pool_sib.start()

    landed = [pool_block(lax.rem(x + 4 - o, 4), core) for o in (1, 2, 3)]
    pool_fwd = [post(part, part, sibling) for part in landed]

    fetch[1].wait()
    fetch[2].wait()
    meth_tablet[...] = meth_table[...].T
    meth_projt[...] = meth_proj[...].T
    for s in range(8):

        @pl.when(jnp.logical_not(is_me(sources[s])))
        def _():
            ids_arrival(s).wait_recv()

    def count_meth(i, carry):
        lanes = pl.ds(pl.multiple_of(i * 128, 128), 128)
        ids = ids_all[:, lanes]
        place_of = jnp.bitwise_and(ids, 127)
        amount = jnp.left_shift(1, jnp.right_shift(ids, 7) * 8)
        row = lax.broadcasted_iota(jnp.int32, (128, 128), 0)
        total = jnp.zeros((128, 128), jnp.int32)
        for t in range(16):
            total = total + jnp.where(row == place_of[t : t + 1, :], amount[t : t + 1, :], 0)
        for f in range(4):
            field = jnp.bitwise_and(jnp.right_shift(total, 8 * f), 255)
            meth_counts[f * 128 : (f + 1) * 128, lanes] = field.astype(F32).astype(BF16)
        return carry

    lax.fori_loop(0, COLS // 128, count_meth, 0)

    def embed_meth(i, carry):
        lanes = pl.ds(pl.multiple_of(i * CHUNK, 128), CHUNK)
        pooled_m = jnp.dot(meth_tablet[...], meth_counts[:, lanes], preferred_element_type=F32)
        pooled_m = (pooled_m * 0.0625).astype(BF16)
        meth_pooled[:, lanes] = pooled_m
        raw = jnp.dot(meth_projt[...], pooled_m, preferred_element_type=F32)
        inverse = lax.rsqrt(jnp.sum(raw * raw, axis=0, keepdims=True) + EPS)
        unit = raw * inverse
        meth_inv[:, lanes] = inverse
        meth_unit[:, lanes] = unit
        meth_rows[:, lanes] = unit.astype(BF16)
        return carry

    half = COLS // CHUNK // 2
    lax.fori_loop(0, half, embed_meth, 0)
    proj_far.wait_recv()
    proj_fwd.start()
    for o in (1, 3):
        pool_far[o - 1].wait_recv()
        pool_fwd[o - 1].start()
    lax.fori_loop(half, 2 * half, embed_meth, 0)
    pool_far[1].wait_recv()
    pool_fwd[1].start()
    proj_sib.wait_recv()
    proj_fwd.wait_recv()
    pair_copy.wait_recv()
    for h in range(2):
        words = pair_all[h]
        for a in range(3):
            wide = jnp.broadcast_to(words[a : a + 1, :], (128, 128))
            first = h * PAIR_DEV + a * 128
            pair_wide[first : first + 128, :] = wide.T
    pool_sib.wait_recv()
    for copy in pool_fwd:
        copy.wait_recv()

    raw = jnp.dot(dna_projt[0], dna_pooled[0], preferred_element_type=F32)
    for s in range(1, 4):
        raw = raw + jnp.dot(dna_projt[s], dna_pooled[s], preferred_element_type=F32)
    inverse = lax.rsqrt(jnp.sum(raw * raw, axis=0, keepdims=True) + EPS)
    unit = raw * inverse
    dna_inv[...] = inverse
    dna_unit[...] = unit
    unit_low = unit.astype(BF16)
    dna_rowst[...] = unit_low
    dna_rows[...] = unit_low.T

    scale = scale_ref[0]
    bias = bias_ref[0]
    row_acc[...] = jnp.zeros_like(row_acc)
    m_acc[...] = jnp.zeros_like(m_out)
    first_col = block * COLS

    def pair_tile(i, carry):
        lanes = pl.ds(pl.multiple_of(i * CHUNK, 128), CHUNK)
        rows_m = meth_rows[:, lanes]
        dots = jnp.dot(dna_rows[...], rows_m, preferred_element_type=F32)
        prob = 1.0 / (1.0 + jnp.exp(-(scale * dots + bias)))
        lane = lax.broadcasted_iota(jnp.int32, (ROWS, 128), 1) + (first_col + i * CHUNK)
        parts = []
        for g in range(CHUNK // 128):
            part = prob[:, g * 128 : (g + 1) * 128]
            hit = pair_wide[...] - g * 128 == lane
            parts.append(jnp.where(hit, part - 1.0, part).astype(BF16))
        tile = jnp.concatenate(parts, axis=1)
        row_acc[...] += lax.dot_general(rows_m, tile, NT, preferred_element_type=F32)
        up = scale * jnp.dot(dna_rowst[...], tile, preferred_element_type=F32)
        unit_m = meth_unit[:, lanes]
        inner = jnp.sum(unit_m * up, axis=0, keepdims=True)
        back = (meth_inv[:, lanes] * (up - unit_m * inner)).astype(BF16)
        m_acc[...] += lax.dot_general(
            meth_pooled[:, lanes], back, NT, preferred_element_type=F32
        )
        return carry

    lax.fori_loop(0, COLS // CHUNK, pair_tile, 0)

    other = 1 - core
    m_swap = post(m_acc.at[pl.ds(pl.multiple_of(other * M_HALF, 8), M_HALF)], m_sib, sibling)
    m_swap.start()

    up = scale * row_acc[...]
    inner = jnp.sum(dna_unit[...] * up, axis=0, keepdims=True)
    back_all[...] = (dna_inv[...] * (up - dna_unit[...] * inner)).astype(BF16)
    back_swap = post(back_all.at[pl.ds(pl.multiple_of(other * 256, 16), 256)], back_sib, sibling)
    back_swap.start()

    swap = core == 1

    def pick(one, two):
        return tuple(jnp.where(swap, q, p) for p, q in zip(one, two))

    axis_a = [pick(p, q) for p, q in zip(ring, along_y)]
    axis_b = [pick(q, p) for p, q in zip(ring, along_y)]
    at_a = jnp.where(swap, y, x)
    at_b = jnp.where(swap, x, y)

    m_swap.wait_recv()
    for a in range(4):
        rows = pl.ds(pl.multiple_of(core * M_HALF + a * 96, 8), 96)
        m_first[a] = m_acc[rows, :] + m_sib[a * 96 : (a + 1) * 96, :]
    m_a = [post(m_first.at[lax.rem(at_a + o, 4)], m_first_in.at[o - 1], axis_a[o]) for o in (1, 2, 3)]
    for copy in m_a:
        copy.start()

    back_swap.wait_recv()
    for a in range(4):
        rows = pl.ds(pl.multiple_of(core * 256 + a * 64, 16), 64)
        both = back_all[rows, :].astype(F32) + back_sib[a * 64 : (a + 1) * 64, :].astype(F32)
        back_half[a] = both.astype(BF16)
    back_x = [post(back_half.at[lax.rem(x + o, 4)], back_in.at[o - 1], ring[o]) for o in (1, 2, 3)]
    for copy in back_x:
        copy.start()
    for copy in back_x:
        copy.wait_recv()
    back = back_half[x].astype(F32)
    for o in range(3):
        back = back + back_in[o].astype(F32)
    back = back.astype(BF16)
    for s in range(4):
        part = lax.dot_general(back, dna_pooled[s], NT, preferred_element_type=F32)
        for a in range(4):
            d_first[a, :, s * D_SLICE : (s + 1) * D_SLICE] = part[a * 16 : (a + 1) * 16, :]
    d_y = [post(d_first.at[lax.rem(y + o, 4)], d_first_in.at[o - 1], along_y[o]) for o in (1, 2, 3)]
    for copy in d_y:
        copy.start()

    for copy in m_a:
        copy.wait_recv()
    for b in range(4):
        part = m_first[at_a, b * 24 : (b + 1) * 24, :]
        for o in range(3):
            part = part + m_first_in[o, b * 24 : (b + 1) * 24, :]
        m_second[b] = part
    m_b = [post(m_second.at[lax.rem(at_b + o, 4)], m_second_in.at[o - 1], axis_b[o]) for o in (1, 2, 3)]
    for copy in m_b:
        copy.start()

    for copy in d_y:
        copy.wait_recv()
    d_sum = d_first[y]
    for o in range(3):
        d_sum = d_sum + d_first_in[o]
    for s in range(8):
        lanes = slice(s * 128, (s + 1) * 128)
        third[s, 8:16, 0:128] = d_sum[0:8, lanes]
        third[s, 8:16, 128:256] = d_sum[8:16, lanes]
    for copy in m_b:
        copy.wait_recv()
    m_sum = m_second[at_b]
    for o in range(3):
        m_sum = m_sum + m_second_in[o]
    for s in range(6):
        third[s, 0:8, :] = m_sum[s // 2 * 8 : s // 2 * 8 + 8, s % 2 * 256 : s % 2 * 256 + 256]
    third[6, 0:8, :] = jnp.zeros((8, 256), F32)
    third[7, 0:8, :] = jnp.zeros((8, 256), F32)

    z_sum = [post(third.at[lax.rem(z + o, 8)], third_in.at[o - 1], along_z[o]) for o in range(1, 8)]
    for copy in z_sum:
        copy.start()
    for copy in z_sum:
        copy.wait_recv()
    total = third[z]
    for o in range(7):
        total = total + third_in[o]
    third_all[z] = total
    z_back = [post(third_all.at[z], third_all.at[z], along_z[o]) for o in range(1, 8)]
    for copy in z_back:
        copy.start()
    for copy in z_back:
        copy.wait_recv()

    for s in range(8):
        lanes = slice(s * 128, (s + 1) * 128)
        d_slab[y, 0:8, lanes] = third_all[s, 8:16, 0:128]
        d_slab[y, 8:16, lanes] = third_all[s, 8:16, 128:256]
    d_back = [post(d_slab.at[y], d_slab.at[y], along_y[o]) for o in (1, 2, 3)]
    for copy in d_back:
        copy.start()
    sub = core * M_HALF + at_a * 96 + at_b * 24
    for s in range(6):
        rows = pl.ds(pl.multiple_of(sub + s // 2 * 8, 8), 8)
        m_all[rows, s % 2 * 256 : s % 2 * 256 + 256] = third_all[s, 0:8, :]
    piece = m_all.at[pl.ds(pl.multiple_of(sub, 8), 24)]
    m_back_b = [post(piece, piece, axis_b[o]) for o in (1, 2, 3)]
    for copy in m_back_b:
        copy.start()
    for copy in m_back_b:
        copy.wait_recv()
    piece = m_all.at[pl.ds(pl.multiple_of(core * M_HALF + at_a * 96, 8), 96)]
    m_back_a = [post(piece, piece, axis_a[o]) for o in (1, 2, 3)]
    for copy in m_back_a:
        copy.start()
    for copy in d_back:
        copy.wait_recv()

    eighth = core * 4 + x

    def slice_for(device):
        return d_slab.at[:, :, pl.ds(pl.multiple_of(device[1] * D_SLICE, 128), D_SLICE)]

    d_ring = [post(slice_for(device), d_fin.at[eighth], device) for device in ring[1:] + cross[1:] + [sibling]]
    for copy in d_ring:
        copy.start()
    own_lanes = pl.ds(pl.multiple_of(mp * D_SLICE, 128), D_SLICE)
    d_fin[eighth] = d_slab[:, :, own_lanes]
    for copy in m_back_a:
        copy.wait_recv()
    half = m_all.at[pl.ds(pl.multiple_of(core * M_HALF, 8), M_HALF)]
    m_last = post(half, half, sibling)
    m_last.start()
    for copy in d_ring:
        copy.wait_recv()
    for s in range(4):
        pair = jnp.concatenate([d_fin[2 * s].reshape(64, D_SLICE), d_fin[2 * s + 1].reshape(64, D_SLICE)], axis=0)
        d_out[:, s * 128 : (s + 1) * 128] = pair.T
    m_last.wait_recv()
    m_out[...] = m_all[...]

    for s in range(8):

        @pl.when(jnp.logical_not(is_me(targets[s])))
        def _():
            ids_copy(s).wait_send()

    for copy in taken:
        copy.wait_send()


def step_call(*args):
    vmem = pl.BlockSpec(memory_space=pltpu.VMEM)
    smem = pl.BlockSpec(memory_space=pltpu.SMEM)
    hbm = pl.BlockSpec(memory_space=pl.ANY)
    dma = pltpu.SemaphoreType.DMA
    f32 = lambda *shape: pltpu.VMEM(shape, F32)
    bf16 = lambda *shape: pltpu.VMEM(shape, BF16)
    i32 = lambda *shape: pltpu.VMEM(shape, jnp.int32)
    return pl.pallas_call(
        step_kernel,
        out_shape=(
            jax.ShapeDtypeStruct((D_SLICE, E), F32),
            jax.ShapeDtypeStruct((D_METH, E), F32),
        ),
        in_specs=[vmem, vmem, vmem, hbm, hbm, vmem, hbm, smem, smem],
        out_specs=(vmem, vmem),
        scratch_shapes=[
            bf16(VOCAB_DNA, D_SLICE),
            bf16(VOCAB_METH, D_METH),
            bf16(D_METH, E),
            i32(PAIR_DEV, 16),
            bf16(PAIR_DEV, VOCAB_DNA),
            i32(16, COLS),
            i32(2, 3, 128),
            i32(ROWS, 128),
            bf16(4, D_SLICE, ROWS),
            bf16(4, E, D_SLICE),
            bf16(D_METH, VOCAB_METH),
            bf16(E, D_METH),
            bf16(VOCAB_METH, COLS),
            bf16(D_METH, COLS),
            f32(E, COLS),
            bf16(E, COLS),
            f32(1, COLS),
            f32(E, ROWS),
            f32(1, ROWS),
            bf16(E, ROWS),
            bf16(ROWS, E),
            f32(E, ROWS),
            f32(D_METH, E),
            f32(M_HALF, E),
            f32(4, 96, E),
            f32(3, 96, E),
            f32(4, 24, E),
            f32(3, 24, E),
            bf16(E, ROWS),
            bf16(256, ROWS),
            bf16(4, 64, ROWS),
            bf16(3, 64, ROWS),
            f32(4, 16, 4 * D_SLICE),
            f32(3, 16, 4 * D_SLICE),
            f32(8, 16, 256),
            f32(7, 16, 256),
            f32(8, 16, 256),
            f32(D_METH, E),
            f32(4, 16, 4 * D_SLICE),
            f32(8, 4, 16, D_SLICE),
            dma((8,)),
            dma((8,)),
            dma((N_COPIES,)),
            dma((N_COPIES,)),
            dma((4,)),
        ],
        compiler_params=pltpu.CompilerParams(
            collective_id=0, has_side_effects=True, vmem_limit_bytes=56 * 1024 * 1024
        ),
        cost_estimate=pl.CostEstimate(flops=19 * 10**9, bytes_accessed=8 * 10**6, transcendentals=5 * 10**6),
        name="contrastive_step",
    )(*args)


def per_device(
    dna_ids,
    meth_ids,
    pair_index,
    dna_table,
    meth_table,
    dna_proj,
    meth_proj,
    logit_scale,
    logit_bias,
):
    return step_call(
        dna_ids.T,
        meth_ids.T,
        pair_index.reshape(3, 128),
        dna_table,
        meth_table,
        dna_proj,
        meth_proj,
        logit_scale,
        logit_bias,
    )


def solution(mesh):
    placed = (
        P("blk", None),
        P("blk", None),
        P("blk"),
        P(None, "mp"),
        P(),
        P("mp", None),
        P(),
        P(),
        P(),
    )
    return jax.shard_map(
        per_device, mesh=mesh, in_specs=placed, out_specs=(P("mp", None), P()), check_vma=False
    )
```

```python
import jax
import jax.numpy as jnp
from jax import lax
from jax.experimental import pallas as pl
from jax.experimental.pallas import tpu as pltpu
from jax.sharding import PartitionSpec as P

MESH = pl.DeviceIdType.MESH
F32 = jnp.float32
BF16 = jnp.bfloat16
EPS = 1e-06

PAIR_DEV = 384
ROWS = 2 * PAIR_DEV
COLS = 8 * PAIR_DEV
E = 512
D_SLICE = 256
D_METH = 768
VOCAB_DNA = 4096
VOCAB_METH = 512
CHUNK = 768
PART = 256
LOG2E = 1.4426950408889634
M_HALF = 384
N_COPIES = 64

NT = (((1,), (1,)), ((), ()))


def place():
    blk, mp = lax.axis_index("blk"), lax.axis_index("mp")
    z = lax.div(blk, 8)
    y = lax.rem(lax.div(blk, 2), 4)
    x = lax.rem(blk, 2) * 2 + lax.div(mp, 2)
    return blk, mp, z, y, x, lax.rem(mp, 2)


def device_at(z, y, x, core):
    return (z * 8 + y * 2 + lax.div(x, 2), lax.rem(x, 2) * 2 + core)


def signal(device):
    pl.semaphore_signal(
        pltpu.get_barrier_semaphore(), inc=1, device_id=device, device_id_type=MESH
    )


def send(src, dst, send_sem, recv_sem, device):
    return pltpu.make_async_remote_copy(
        src_ref=src,
        dst_ref=dst,
        send_sem=send_sem,
        recv_sem=recv_sem,
        device_id=device,
        device_id_type=MESH,
    )


def step_kernel(
    dna_ids,
    meth_ids,
    pairs,
    dna_table_hbm,
    meth_table_hbm,
    dna_proj,
    meth_proj_hbm,
    scale_ref,
    bias_ref,
    d_out,
    m_out,
    dna_table,
    meth_table,
    meth_proj,
    dna_tokens,
    counts,
    ids_all,
    pair_all,
    pair_wide,
    dna_pooled,
    dna_projt,
    meth_tablet,
    meth_projt,
    meth_pooled,
    meth_unit,
    meth_rows,
    meth_inv,
    dna_unit,
    dna_inv,
    dna_rowst,
    dna_rows,
    row_acc,
    tiles,
    m_acc,
    m_sib,
    m_first,
    m_first_in,
    m_second,
    m_second_in,
    back_all,
    back_sib,
    back_half,
    back_in,
    d_first,
    d_first_in,
    third,
    third_in,
    third_all,
    m_all,
    d_slab,
    d_fin,
    ids_send,
    ids_recv,
    send_sems,
    recv_sems,
    local_sems,
):
    blk, mp, z, y, x, core = place()
    x_hi = lax.div(x, 2)
    sibling = device_at(z, y, x, 1 - core)
    ring = [device_at(z, y, lax.rem(x + o, 4), core) for o in range(4)]
    cross = [device_at(z, y, lax.rem(x + o, 4), 1 - core) for o in range(4)]
    along_y = [device_at(z, lax.rem(y + o, 4), x, core) for o in range(4)]
    along_z = [device_at(lax.rem(z + o, 8), y, x, core) for o in range(8)]
    slot = lax.rem(blk, 8)
    block = x_hi * 4 + mp
    taken = []

    def post(src, dst, device):
        n = len(taken)
        copy = send(src, dst, send_sems.at[n], recv_sems.at[n], device)
        taken.append(copy)
        return copy

    fetch = [
        pltpu.make_async_copy(src, dst, local_sems.at[1 + n])
        for n, (src, dst) in enumerate(
            ((dna_table_hbm, dna_table), (meth_table_hbm, meth_table), (meth_proj_hbm, meth_proj))
        )
    ]
    for copy in fetch:
        copy.start()

    targets = [device_at(s, mp, lax.div(z, 2), lax.rem(z, 2)) for s in range(8)]
    sources = [device_at(block, s // 2, (s % 2) * 2 + lax.div(y, 2), lax.rem(y, 2)) for s in range(8)]

    def is_me(device):
        return jnp.logical_and(device[0] == blk, device[1] == mp)

    for s in range(8):

        @pl.when(jnp.logical_not(is_me(sources[s])))
        def _():
            signal(sources[s])

    for o in (1, 2, 3):
        signal(ring[o])
        signal(cross[o])
        signal(along_y[o])
    for o in range(1, 8):
        signal(along_z[o])
    signal(sibling)
    to_self = jnp.logical_and(mp == y, block == z).astype(jnp.int32)
    pl.semaphore_wait(pltpu.get_barrier_semaphore(), 25 - to_self)

    def ids_copy(s):
        lanes = pl.ds(pl.multiple_of(slot * PAIR_DEV, 128), PAIR_DEV)
        return send(meth_ids, ids_all.at[:, lanes], ids_send.at[s], ids_recv.at[slot], targets[s])

    def ids_arrival(s):
        lanes = pl.ds(s * PAIR_DEV, PAIR_DEV)
        return send(meth_ids, ids_all.at[:, lanes], ids_send.at[s], ids_recv.at[s], sources[s])

    for s in range(8):

        @pl.when(jnp.logical_not(is_me(targets[s])))
        def _():
            ids_copy(s).start()

        @pl.when(is_me(targets[s]))
        def _():
            lanes = pl.ds(pl.multiple_of(slot * PAIR_DEV, 128), PAIR_DEV)
            local = pltpu.make_async_copy(meth_ids, ids_all.at[:, lanes], local_sems.at[0])
            local.start()
            local.wait()

    pair_copy = post(pairs, pair_all.at[x_hi], ring[2])
    pair_copy.start()
    pair_all[x_hi] = pairs[...]

    dna_projt[mp] = dna_proj[...].T
    toward = 1 + 2 * core
    far = device_at(z, y, lax.rem(x + toward, 4), core)
    other_mp = lax.rem(mp + 2, 4)
    proj_far = post(dna_projt.at[mp], dna_projt.at[mp], far)
    proj_sib = post(dna_projt.at[mp], dna_projt.at[mp], sibling)
    proj_fwd = post(dna_projt.at[other_mp], dna_projt.at[other_mp], sibling)
    proj_far.start()
    proj_sib.start()

    dna_tokens[...] = dna_ids[...].T

    def count_dna(i, carry):
        rows = pl.ds(pl.multiple_of(i * 16, 16), 16)
        ids = dna_tokens[rows, :]
        place_of = jnp.bitwise_and(ids, VOCAB_DNA // 4 - 1)
        amount = jnp.left_shift(1, jnp.right_shift(ids, 10) * 8)
        lane = lax.broadcasted_iota(jnp.int32, (16, VOCAB_DNA // 4), 1)
        total = jnp.zeros((16, VOCAB_DNA // 4), jnp.int32)
        for t in range(16):
            total = total + jnp.where(lane == place_of[:, t : t + 1], amount[:, t : t + 1], 0)
        for f in range(4):
            field = jnp.bitwise_and(jnp.right_shift(total, 8 * f), 255)
            counts[rows, f * 1024 : (f + 1) * 1024] = field.astype(F32).astype(BF16)
        return carry

    lax.fori_loop(0, PAIR_DEV // 16, count_dna, 0)
    fetch[0].wait()
    pooled = jnp.dot(counts[...], dna_table[...], preferred_element_type=F32) * 0.0625
    own_lanes = pl.ds(pl.multiple_of(x_hi * PAIR_DEV, 128), PAIR_DEV)
    dna_pooled[mp, :, own_lanes] = pooled.T.astype(BF16)

    def pool_block(x_of, core_of):
        lanes = pl.ds(pl.multiple_of(lax.div(x_of, 2) * PAIR_DEV, 128), PAIR_DEV)
        return dna_pooled.at[lax.rem(x_of, 2) * 2 + core_of, :, lanes]

    own = pool_block(x, core)
    def rows_of(part, h):
        return part.at[h * 128 : (h + 1) * 128]

    from_left = pool_block(lax.rem(x + 3, 4), core)
    from_right = pool_block(lax.rem(x + 1, 4), core)
    from_across = pool_block(lax.rem(x + 2, 4), core)
    pool_right = post(own, own, ring[1])
    pool_left = post(own, own, ring[3])
    pool_sib = post(own, own, sibling)
    pool_right.start()
    pool_left.start()
    pool_sib.start()
    relay_right = post(rows_of(from_left, 0), rows_of(from_left, 0), ring[1])
    relay_left = post(rows_of(from_right, 1), rows_of(from_right, 1), ring[3])
    pool_fwd = [post(part, part, sibling) for part in (from_left, from_right, from_across)]

    fetch[1].wait()
    fetch[2].wait()
    meth_tablet[...] = meth_table[...].T
    meth_projt[...] = meth_proj[...].T
    for s in range(8):

        @pl.when(jnp.logical_not(is_me(sources[s])))
        def _():
            ids_arrival(s).wait_recv()

    def count_meth(ids):
        place_of = jnp.bitwise_and(ids, 127)
        amount = jnp.left_shift(1, jnp.right_shift(ids, 7) * 8)
        row = lax.broadcasted_iota(jnp.int32, (128, 128), 0)
        total = jnp.zeros((128, 128), jnp.int32)
        for t in range(16):
            total = total + jnp.where(row == place_of[t : t + 1, :], amount[t : t + 1, :], 0)
        fields = [jnp.bitwise_and(jnp.right_shift(total, 8 * f), 255) for f in range(4)]
        return jnp.concatenate([field.astype(F32).astype(BF16) for field in fields], axis=0)

    def embed_meth(i, carry):
        for p in range(CHUNK // PART):
            first = pl.multiple_of(i * CHUNK + p * PART, 128)
            lanes = pl.ds(first, PART)
            ids = [ids_all[:, pl.ds(pl.multiple_of(first + 128 * g, 128), 128)] for g in range(PART // 128)]
            tokens = jnp.concatenate([count_meth(part) for part in ids], axis=1)
            pooled_m = jnp.dot(meth_tablet[...], tokens, preferred_element_type=F32)
            pooled_m = (pooled_m * 0.0625).astype(BF16)
            meth_pooled[:, lanes] = pooled_m
            raw = jnp.dot(meth_projt[...], pooled_m, preferred_element_type=F32)
            inverse = lax.rsqrt(jnp.sum(raw * raw, axis=0, keepdims=True) + EPS)
            unit = raw * inverse
            meth_inv[:, lanes] = inverse
            meth_unit[:, lanes] = unit
            meth_rows[:, lanes] = unit.astype(BF16)
        return carry

    half = COLS // CHUNK // 2
    lax.fori_loop(0, half, embed_meth, 0)
    pool_right.wait_recv()
    relay_right.start()
    pool_left.wait_recv()
    relay_left.start()
    pool_fwd[0].start()
    pool_fwd[1].start()
    proj_far.wait_recv()
    proj_fwd.start()
    lax.fori_loop(half, 2 * half, embed_meth, 0)
    relay_right.wait_recv()
    relay_left.wait_recv()
    pool_fwd[2].start()
    proj_sib.wait_recv()
    proj_fwd.wait_recv()
    pair_copy.wait_recv()
    for h in range(2):
        words = pair_all[h]
        for a in range(3):
            wide = jnp.broadcast_to(words[a : a + 1, :], (128, 128))
            first = h * PAIR_DEV + a * 128
            pair_wide[first : first + 128, :] = wide.T
    pool_sib.wait_recv()
    for copy in pool_fwd:
        copy.wait_recv()

    raw = jnp.dot(dna_projt[0], dna_pooled[0], preferred_element_type=F32)
    for s in range(1, 4):
        raw = raw + jnp.dot(dna_projt[s], dna_pooled[s], preferred_element_type=F32)
    inverse = lax.rsqrt(jnp.sum(raw * raw, axis=0, keepdims=True) + EPS)
    unit = raw * inverse
    dna_inv[...] = inverse
    dna_unit[...] = unit
    unit_low = unit.astype(BF16)
    dna_rowst[...] = unit_low
    dna_rows[...] = unit_low.T

    scale = scale_ref[0]
    bias = bias_ref[0]
    row_acc[...] = jnp.zeros_like(row_acc)
    m_acc[...] = jnp.zeros_like(m_acc)
    slope, offset = scale * -LOG2E, bias * -LOG2E
    first_col = block * COLS

    def pair_tile(i, carry):
        first = pl.multiple_of(i * CHUNK, 128)
        partner = pair_wide[...] - (first_col + first)
        parts = []
        for p in range(CHUNK // PART):
            rows_m = meth_rows[:, pl.ds(pl.multiple_of(first + p * PART, 128), PART)]
            dots = jnp.dot(dna_rows[...], rows_m, preferred_element_type=F32)
            lower = 1.0 + jnp.exp2(slope * dots + offset)
            prob = pl.reciprocal(lower, approx=True)
            prob = prob * (2.0 - lower * prob)
            for g in range(PART // 128):
                part = prob[:, g * 128 : (g + 1) * 128]
                lane = lax.broadcasted_iota(jnp.int32, (ROWS, 128), 1) + (p * PART + g * 128)
                parts.append(jnp.where(partner == lane, part - 1.0, part).astype(BF16))
        tile = jnp.concatenate(parts, axis=1)
        lanes = pl.ds(first, CHUNK)
        tiles[:, lanes] = tile
        row_acc[...] += lax.dot_general(meth_rows[:, lanes], tile, NT, preferred_element_type=F32)
        return carry

    lax.fori_loop(0, COLS // CHUNK, pair_tile, 0)

    other = 1 - core
    up = scale * row_acc[...]
    inner = jnp.sum(dna_unit[...] * up, axis=0, keepdims=True)
    back_all[...] = (dna_inv[...] * (up - dna_unit[...] * inner)).astype(BF16)
    back_swap = post(back_all.at[pl.ds(pl.multiple_of(other * 256, 16), 256)], back_sib, sibling)
    back_swap.start()

    def col_tile(i, carry):
        first = pl.multiple_of(i * CHUNK, 128)
        parts = []
        for p in range(CHUNK // PART):
            lanes = pl.ds(pl.multiple_of(first + p * PART, 128), PART)
            up = scale * jnp.dot(dna_rowst[...], tiles[:, lanes], preferred_element_type=F32)
            unit_m = meth_unit[:, lanes]
            inner = jnp.sum(unit_m * up, axis=0, keepdims=True)
            parts.append((meth_inv[:, lanes] * (up - unit_m * inner)).astype(BF16))
        back = jnp.concatenate(parts, axis=1)
        m_acc[...] += lax.dot_general(
            meth_pooled[:, pl.ds(first, CHUNK)], back, NT, preferred_element_type=F32
        )
        return carry

    lax.fori_loop(0, half, col_tile, 0)
    back_swap.wait_recv()
    for a in range(4):
        rows = pl.ds(pl.multiple_of(core * 256 + a * 64, 16), 64)
        both = back_all[rows, :].astype(F32) + back_sib[a * 64 : (a + 1) * 64, :].astype(F32)
        back_half[a] = both.astype(BF16)
    back_x = [post(back_half.at[lax.rem(x + o, 4)], back_in.at[o - 1], ring[o]) for o in (1, 2, 3)]
    for copy in back_x:
        copy.start()
    lax.fori_loop(half, 2 * half, col_tile, 0)

    m_swap = post(m_acc.at[pl.ds(pl.multiple_of(other * M_HALF, 8), M_HALF)], m_sib, sibling)
    m_swap.start()

    swap = core == 1

    def pick(one, two):
        return tuple(jnp.where(swap, q, p) for p, q in zip(one, two))

    axis_a = [pick(p, q) for p, q in zip(ring, along_y)]
    axis_b = [pick(q, p) for p, q in zip(ring, along_y)]
    at_a = jnp.where(swap, y, x)
    at_b = jnp.where(swap, x, y)

    m_swap.wait_recv()

    def halve(i, carry):
        a, b = lax.div(i, 4), lax.rem(i, 4)
        row = jnp.where(swap, a * 96 + b * 24, b * 96 + a * 24)
        mine = m_acc[pl.ds(pl.multiple_of(core * M_HALF + row, 8), 24), :]
        m_first[a, b] = mine + m_sib[pl.ds(pl.multiple_of(row, 8), 24), :]
        return carry

    lax.fori_loop(0, 16, halve, 0)
    m_a = [post(m_first.at[lax.rem(at_a + o, 4)], m_first_in.at[o - 1], axis_a[o]) for o in (1, 2, 3)]
    for copy in m_a:
        copy.start()

    for copy in back_x:
        copy.wait_recv()
    back = back_half[x].astype(F32)
    for o in range(3):
        back = back + back_in[o].astype(F32)
    back = back.astype(BF16)
    for s in range(4):
        part = lax.dot_general(back, dna_pooled[s], NT, preferred_element_type=F32)
        for a in range(4):
            d_first[a, :, s * D_SLICE : (s + 1) * D_SLICE] = part[a * 16 : (a + 1) * 16, :]
    d_y = [post(d_first.at[lax.rem(y + o, 4)], d_first_in.at[o - 1], along_y[o]) for o in (1, 2, 3)]
    for copy in d_y:
        copy.start()

    for copy in m_a:
        copy.wait_recv()
    for b in range(4):
        part = m_first[at_a, b]
        for o in range(3):
            part = part + m_first_in[o, b]
        m_second[b] = part
    m_b = [post(m_second.at[lax.rem(at_b + o, 4)], m_second_in.at[o - 1], axis_b[o]) for o in (1, 2, 3)]
    for copy in m_b:
        copy.start()

    for copy in d_y:
        copy.wait_recv()
    d_sum = d_first[y]
    for o in range(3):
        d_sum = d_sum + d_first_in[o]
    for s in range(8):
        lanes = slice(s * 128, (s + 1) * 128)
        third[s, 8:16, 0:128] = d_sum[0:8, lanes]
        third[s, 8:16, 128:256] = d_sum[8:16, lanes]
    for copy in m_b:
        copy.wait_recv()
    m_sum = m_second[at_b]
    for o in range(3):
        m_sum = m_sum + m_second_in[o]
    for s in range(6):
        third[s, 0:8, :] = m_sum[s // 2 * 8 : s // 2 * 8 + 8, s % 2 * 256 : s % 2 * 256 + 256]
    third[6, 0:8, :] = jnp.zeros((8, 256), F32)
    third[7, 0:8, :] = jnp.zeros((8, 256), F32)

    z_sum = [post(third.at[lax.rem(z + o, 8)], third_in.at[o - 1], along_z[o]) for o in range(1, 8)]
    for copy in z_sum:
        copy.start()
    for copy in z_sum:
        copy.wait_recv()
    total = third[z]
    for o in range(7):
        total = total + third_in[o]
    third_all[z] = total
    z_back = [post(third_all.at[z], third_all.at[z], along_z[o]) for o in range(1, 8)]
    for copy in z_back:
        copy.start()
    for copy in z_back:
        copy.wait_recv()

    for s in range(8):
        lanes = slice(s * 128, (s + 1) * 128)
        d_slab[y, 0:8, lanes] = third_all[s, 8:16, 0:128]
        d_slab[y, 8:16, lanes] = third_all[s, 8:16, 128:256]
    d_back = [post(d_slab.at[y], d_slab.at[y], along_y[o]) for o in (1, 2, 3)]
    for copy in d_back:
        copy.start()
    sub = core * M_HALF + y * 96 + x * 24
    for s in range(6):
        rows = pl.ds(pl.multiple_of(sub + s // 2 * 8, 8), 8)
        m_all[rows, s % 2 * 256 : s % 2 * 256 + 256] = third_all[s, 0:8, :]
    piece = m_all.at[pl.ds(pl.multiple_of(sub, 8), 24)]
    m_back_x = [post(piece, piece, ring[o]) for o in (1, 2, 3)]
    for copy in m_back_x:
        copy.start()

    def band(y_of, low, rows):
        first = core * M_HALF + lax.rem(y_of, 4) * 96 + low
        return m_all.at[pl.ds(pl.multiple_of(first, 8), rows)]

    def to(part, device):
        copy = post(part, part, device)
        copy.start()
        return copy

    for copy in m_back_x:
        copy.wait_recv()
    own_band = band(y, 0, 96)
    up_copy = to(own_band, along_y[1])
    down_copy = to(own_band, along_y[3])
    m_last = [to(own_band, sibling)]

    for copy in d_back:
        copy.wait_recv()
    eighth = core * 4 + x

    def slice_for(device):
        return d_slab.at[:, :, pl.ds(pl.multiple_of(device[1] * D_SLICE, 128), D_SLICE)]

    d_ring = [post(slice_for(device), d_fin.at[eighth], device) for device in ring[1:] + cross[1:] + [sibling]]
    for copy in d_ring:
        copy.start()
    own_lanes = pl.ds(pl.multiple_of(mp * D_SLICE, 128), D_SLICE)
    d_fin[eighth] = d_slab[:, :, own_lanes]

    up_copy.wait_recv()
    relay_up = to(band(y + 3, 0, 48), along_y[1])
    m_last.append(to(band(y + 3, 0, 96), sibling))
    down_copy.wait_recv()
    relay_down = to(band(y + 1, 48, 48), along_y[3])
    m_last.append(to(band(y + 1, 0, 96), sibling))

    for copy in d_ring:
        copy.wait_recv()
    for s in range(4):
        pair = jnp.concatenate([d_fin[2 * s].reshape(64, D_SLICE), d_fin[2 * s + 1].reshape(64, D_SLICE)], axis=0)
        d_out[:, s * 128 : (s + 1) * 128] = pair.T
    relay_up.wait_recv()
    relay_down.wait_recv()
    m_last.append(to(band(y + 2, 0, 96), sibling))
    for copy in m_last:
        copy.wait_recv()
    m_out[...] = m_all[...]

    for s in range(8):

        @pl.when(jnp.logical_not(is_me(targets[s])))
        def _():
            ids_copy(s).wait_send()

    for copy in taken:
        copy.wait_send()


def step_call(*args):
    vmem = pl.BlockSpec(memory_space=pltpu.VMEM)
    smem = pl.BlockSpec(memory_space=pltpu.SMEM)
    hbm = pl.BlockSpec(memory_space=pl.ANY)
    dma = pltpu.SemaphoreType.DMA
    f32 = lambda *shape: pltpu.VMEM(shape, F32)
    bf16 = lambda *shape: pltpu.VMEM(shape, BF16)
    i32 = lambda *shape: pltpu.VMEM(shape, jnp.int32)
    return pl.pallas_call(
        step_kernel,
        out_shape=(
            jax.ShapeDtypeStruct((D_SLICE, E), F32),
            jax.ShapeDtypeStruct((D_METH, E), F32),
        ),
        in_specs=[vmem, vmem, vmem, hbm, hbm, vmem, hbm, smem, smem],
        out_specs=(vmem, vmem),
        scratch_shapes=[
            bf16(VOCAB_DNA, D_SLICE),
            bf16(VOCAB_METH, D_METH),
            bf16(D_METH, E),
            i32(PAIR_DEV, 16),
            bf16(PAIR_DEV, VOCAB_DNA),
            i32(16, COLS),
            i32(2, 3, 128),
            i32(ROWS, 128),
            bf16(4, D_SLICE, ROWS),
            bf16(4, E, D_SLICE),
            bf16(D_METH, VOCAB_METH),
            bf16(E, D_METH),
            bf16(D_METH, COLS),
            f32(E, COLS),
            bf16(E, COLS),
            f32(1, COLS),
            f32(E, ROWS),
            f32(1, ROWS),
            bf16(E, ROWS),
            bf16(ROWS, E),
            f32(E, ROWS),
            bf16(ROWS, COLS),
            f32(D_METH, E),
            f32(M_HALF, E),
            f32(4, 4, 24, E),
            f32(3, 4, 24, E),
            f32(4, 24, E),
            f32(3, 24, E),
            bf16(E, ROWS),
            bf16(256, ROWS),
            bf16(4, 64, ROWS),
            bf16(3, 64, ROWS),
            f32(4, 16, 4 * D_SLICE),
            f32(3, 16, 4 * D_SLICE),
            f32(8, 16, 256),
            f32(7, 16, 256),
            f32(8, 16, 256),
            f32(D_METH, E),
            f32(4, 16, 4 * D_SLICE),
            f32(8, 4, 16, D_SLICE),
            dma((8,)),
            dma((8,)),
            dma((N_COPIES,)),
            dma((N_COPIES,)),
            dma((4,)),
        ],
        compiler_params=pltpu.CompilerParams(
            collective_id=0, has_side_effects=True, vmem_limit_bytes=56 * 1024 * 1024
        ),
        cost_estimate=pl.CostEstimate(flops=19 * 10**9, bytes_accessed=8 * 10**6, transcendentals=5 * 10**6),
        name="contrastive_step",
    )(*args)


def per_device(
    dna_ids,
    meth_ids,
    pair_index,
    dna_table,
    meth_table,
    dna_proj,
    meth_proj,
    logit_scale,
    logit_bias,
):
    return step_call(
        dna_ids.T,
        meth_ids.T,
        pair_index.reshape(3, 128),
        dna_table,
        meth_table,
        dna_proj,
        meth_proj,
        logit_scale,
        logit_bias,
    )


def solution(mesh):
    placed = (
        P("blk", None),
        P("blk", None),
        P("blk"),
        P(None, "mp"),
        P(),
        P("mp", None),
        P(),
        P(),
        P(),
    )
    return jax.shard_map(
        per_device, mesh=mesh, in_specs=placed, out_specs=(P("mp", None), P()), check_vma=False
    )
```

```python
import jax
import jax.numpy as jnp
from jax import lax
from jax.experimental import pallas as pl
from jax.experimental.pallas import tpu as pltpu
from jax.sharding import PartitionSpec as P

MESH = pl.DeviceIdType.MESH
F32 = jnp.float32
BF16 = jnp.bfloat16
EPS = 1e-06

PAIR_DEV = 384
ROWS = 2 * PAIR_DEV
COLS = 8 * PAIR_DEV
E = 512
D_SLICE = 256
D_METH = 768
VOCAB_DNA = 4096
VOCAB_METH = 512
CHUNK = 768
PART = 256
LOG2E = 1.4426950408889634
M_HALF = 384
N_COPIES = 64

NT = (((1,), (1,)), ((), ()))


def place():
    blk, mp = lax.axis_index("blk"), lax.axis_index("mp")
    z = lax.div(blk, 8)
    y = lax.rem(lax.div(blk, 2), 4)
    x = lax.rem(blk, 2) * 2 + lax.div(mp, 2)
    return blk, mp, z, y, x, lax.rem(mp, 2)


def device_at(z, y, x, core):
    return (z * 8 + y * 2 + lax.div(x, 2), lax.rem(x, 2) * 2 + core)


def signal(device):
    pl.semaphore_signal(
        pltpu.get_barrier_semaphore(), inc=1, device_id=device, device_id_type=MESH
    )


def send(src, dst, send_sem, recv_sem, device):
    return pltpu.make_async_remote_copy(
        src_ref=src,
        dst_ref=dst,
        send_sem=send_sem,
        recv_sem=recv_sem,
        device_id=device,
        device_id_type=MESH,
    )


def step_kernel(
    dna_ids,
    meth_ids,
    pairs,
    dna_table_hbm,
    meth_table_hbm,
    dna_proj,
    meth_proj_hbm,
    scale_ref,
    bias_ref,
    d_out,
    m_out,
    dna_table,
    meth_table,
    meth_proj,
    dna_tokens,
    counts,
    ids_all,
    pair_all,
    pair_wide,
    dna_pooled,
    dna_projt,
    meth_tablet,
    meth_projt,
    meth_pooled,
    meth_unit,
    meth_rows,
    meth_inv,
    dna_unit,
    dna_inv,
    dna_rowst,
    dna_rows,
    row_acc,
    tiles,
    meth_back,
    m_acc,
    m_sib,
    m_first,
    m_first_in,
    m_second,
    m_second_in,
    back_all,
    back_sib,
    back_half,
    back_in,
    d_first,
    d_first_in,
    third,
    third_in,
    third_all,
    m_all,
    d_slab,
    d_fin,
    ids_send,
    ids_recv,
    send_sems,
    recv_sems,
    local_sems,
):
    blk, mp, z, y, x, core = place()
    x_hi = lax.div(x, 2)
    sibling = device_at(z, y, x, 1 - core)
    ring = [device_at(z, y, lax.rem(x + o, 4), core) for o in range(4)]
    cross = [device_at(z, y, lax.rem(x + o, 4), 1 - core) for o in range(4)]
    along_y = [device_at(z, lax.rem(y + o, 4), x, core) for o in range(4)]
    along_z = [device_at(lax.rem(z + o, 8), y, x, core) for o in range(8)]
    slot = lax.rem(blk, 8)
    block = x_hi * 4 + mp
    taken = []

    def post(src, dst, device):
        n = len(taken)
        copy = send(src, dst, send_sems.at[n], recv_sems.at[n], device)
        taken.append(copy)
        return copy

    fetch = [
        pltpu.make_async_copy(src, dst, local_sems.at[1 + n])
        for n, (src, dst) in enumerate(
            ((dna_table_hbm, dna_table), (meth_table_hbm, meth_table), (meth_proj_hbm, meth_proj))
        )
    ]
    for copy in fetch:
        copy.start()

    targets = [device_at(s, mp, lax.div(z, 2), lax.rem(z, 2)) for s in range(8)]
    sources = [device_at(block, s // 2, (s % 2) * 2 + lax.div(y, 2), lax.rem(y, 2)) for s in range(8)]

    def is_me(device):
        return jnp.logical_and(device[0] == blk, device[1] == mp)

    for s in range(8):

        @pl.when(jnp.logical_not(is_me(sources[s])))
        def _():
            signal(sources[s])

    for o in (1, 2, 3):
        signal(ring[o])
        signal(cross[o])
        signal(along_y[o])
    for o in range(1, 8):
        signal(along_z[o])
    signal(sibling)
    to_self = jnp.logical_and(mp == y, block == z).astype(jnp.int32)
    pl.semaphore_wait(pltpu.get_barrier_semaphore(), 25 - to_self)

    def ids_copy(s):
        lanes = pl.ds(pl.multiple_of(slot * PAIR_DEV, 128), PAIR_DEV)
        return send(meth_ids, ids_all.at[:, lanes], ids_send.at[s], ids_recv.at[slot], targets[s])

    def ids_arrival(s):
        lanes = pl.ds(s * PAIR_DEV, PAIR_DEV)
        return send(meth_ids, ids_all.at[:, lanes], ids_send.at[s], ids_recv.at[s], sources[s])

    for s in range(8):

        @pl.when(jnp.logical_not(is_me(targets[s])))
        def _():
            ids_copy(s).start()

        @pl.when(is_me(targets[s]))
        def _():
            lanes = pl.ds(pl.multiple_of(slot * PAIR_DEV, 128), PAIR_DEV)
            local = pltpu.make_async_copy(meth_ids, ids_all.at[:, lanes], local_sems.at[0])
            local.start()
            local.wait()

    pair_copy = post(pairs, pair_all.at[x_hi], ring[2])
    pair_copy.start()
    pair_all[x_hi] = pairs[...]

    dna_projt[:, pl.ds(pl.multiple_of(mp * D_SLICE, 128), D_SLICE)] = dna_proj[...].T
    toward = 1 + 2 * core
    far = device_at(z, y, lax.rem(x + toward, 4), core)
    other_mp = lax.rem(mp + 2, 4)

    def quarter(of):
        return dna_projt.at[:, pl.ds(pl.multiple_of(of * D_SLICE, 128), D_SLICE)]

    proj_far = post(quarter(mp), quarter(mp), far)
    proj_sib = post(quarter(mp), quarter(mp), sibling)
    proj_fwd = post(quarter(other_mp), quarter(other_mp), sibling)
    proj_far.start()
    proj_sib.start()

    dna_tokens[...] = dna_ids[...].T

    def count_dna(i, carry):
        rows = pl.ds(pl.multiple_of(i * 16, 16), 16)
        ids = dna_tokens[rows, :]
        place_of = jnp.bitwise_and(ids, VOCAB_DNA // 4 - 1)
        amount = jnp.left_shift(1, jnp.right_shift(ids, 10) * 8)
        lane = lax.broadcasted_iota(jnp.int32, (16, VOCAB_DNA // 4), 1)
        total = jnp.zeros((16, VOCAB_DNA // 4), jnp.int32)
        for t in range(16):
            total = total + jnp.where(lane == place_of[:, t : t + 1], amount[:, t : t + 1], 0)
        for f in range(4):
            field = jnp.bitwise_and(jnp.right_shift(total, 8 * f), 255)
            counts[rows, f * 1024 : (f + 1) * 1024] = field.astype(F32).astype(BF16)
        return carry

    lax.fori_loop(0, PAIR_DEV // 16, count_dna, 0)
    fetch[0].wait()
    pooled = jnp.dot(counts[...], dna_table[...], preferred_element_type=F32) * 0.0625
    own_lanes = pl.ds(pl.multiple_of(x_hi * PAIR_DEV, 128), PAIR_DEV)
    dna_pooled[pl.ds(pl.multiple_of(mp * D_SLICE, 16), D_SLICE), own_lanes] = pooled.T.astype(BF16)

    def pool_block(x_of, core_of, low=0, count=D_SLICE):
        first = (lax.rem(x_of, 2) * 2 + core_of) * D_SLICE + low
        lanes = pl.ds(pl.multiple_of(lax.div(x_of, 2) * PAIR_DEV, 128), PAIR_DEV)
        return dna_pooled.at[pl.ds(pl.multiple_of(first, 16), count), lanes]

    own = pool_block(x, core)
    from_left = pool_block(lax.rem(x + 3, 4), core)
    from_right = pool_block(lax.rem(x + 1, 4), core)
    from_across = pool_block(lax.rem(x + 2, 4), core)
    pool_right = post(own, own, ring[1])
    pool_left = post(own, own, ring[3])
    pool_sib = post(own, own, sibling)
    pool_right.start()
    pool_left.start()
    pool_sib.start()
    half_left = pool_block(lax.rem(x + 3, 4), core, 0, 128)
    half_right = pool_block(lax.rem(x + 1, 4), core, 128, 128)
    relay_right = post(half_left, half_left, ring[1])
    relay_left = post(half_right, half_right, ring[3])
    pool_fwd = [post(part, part, sibling) for part in (from_left, from_right, from_across)]

    fetch[1].wait()
    fetch[2].wait()
    meth_tablet[...] = meth_table[...].T
    meth_projt[...] = meth_proj[...].T
    for s in range(8):

        @pl.when(jnp.logical_not(is_me(sources[s])))
        def _():
            ids_arrival(s).wait_recv()

    def count_meth(ids):
        place_of = jnp.bitwise_and(ids, 127)
        amount = jnp.left_shift(1, jnp.right_shift(ids, 7) * 8)
        row = lax.broadcasted_iota(jnp.int32, (128, 128), 0)
        total = jnp.zeros((128, 128), jnp.int32)
        for t in range(16):
            total = total + jnp.where(row == place_of[t : t + 1, :], amount[t : t + 1, :], 0)
        fields = [jnp.bitwise_and(jnp.right_shift(total, 8 * f), 255) for f in range(4)]
        return jnp.concatenate([field.astype(F32).astype(BF16) for field in fields], axis=0)

    def embed_meth(i, carry):
        for p in range(CHUNK // PART):
            first = pl.multiple_of(i * CHUNK + p * PART, 128)
            lanes = pl.ds(first, PART)
            ids = [ids_all[:, pl.ds(pl.multiple_of(first + 128 * g, 128), 128)] for g in range(PART // 128)]
            tokens = jnp.concatenate([count_meth(part) for part in ids], axis=1)
            pooled_m = jnp.dot(meth_tablet[...], tokens, preferred_element_type=F32)
            pooled_m = (pooled_m * 0.0625).astype(BF16)
            meth_pooled[:, lanes] = pooled_m
            raw = jnp.dot(meth_projt[...], pooled_m, preferred_element_type=F32)
            inverse = lax.rsqrt(jnp.sum(raw * raw, axis=0, keepdims=True) + EPS)
            unit = raw * inverse
            meth_inv[:, lanes] = inverse
            meth_unit[:, lanes] = unit
            meth_rows[:, lanes] = unit.astype(BF16)
        return carry

    half = COLS // CHUNK // 2
    lax.fori_loop(0, half, embed_meth, 0)
    pool_right.wait_recv()
    relay_right.start()
    pool_left.wait_recv()
    relay_left.start()
    pool_fwd[0].start()
    pool_fwd[1].start()
    proj_far.wait_recv()
    proj_fwd.start()
    lax.fori_loop(half, 2 * half, embed_meth, 0)
    relay_right.wait_recv()
    relay_left.wait_recv()
    pool_fwd[2].start()
    proj_sib.wait_recv()
    proj_fwd.wait_recv()
    pair_copy.wait_recv()
    for h in range(2):
        words = pair_all[h]
        for a in range(3):
            wide = jnp.broadcast_to(words[a : a + 1, :], (128, 128))
            first = h * PAIR_DEV + a * 128
            pair_wide[first : first + 128, :] = wide.T
    pool_sib.wait_recv()
    for copy in pool_fwd:
        copy.wait_recv()

    raw = jnp.dot(dna_projt[...], dna_pooled[...], preferred_element_type=F32)
    inverse = lax.rsqrt(jnp.sum(raw * raw, axis=0, keepdims=True) + EPS)
    unit = raw * inverse
    dna_inv[...] = inverse
    dna_unit[...] = unit
    unit_low = unit.astype(BF16)
    dna_rowst[...] = unit_low
    dna_rows[...] = unit_low.T

    scale = scale_ref[0]
    bias = bias_ref[0]
    slope, offset = scale * -LOG2E, bias * -LOG2E
    first_col = block * COLS

    def pair_tile(i, carry):
        first = pl.multiple_of(i * CHUNK, 128)
        partner = pair_wide[...] - (first_col + first)
        parts = []
        for p in range(CHUNK // PART):
            rows_m = meth_rows[:, pl.ds(pl.multiple_of(first + p * PART, 128), PART)]
            dots = jnp.dot(dna_rows[...], rows_m, preferred_element_type=F32)
            lower = 1.0 + jnp.exp2(slope * dots + offset)
            prob = pl.reciprocal(lower, approx=True)
            prob = prob * (2.0 - lower * prob)
            for g in range(PART // 128):
                part = prob[:, g * 128 : (g + 1) * 128]
                lane = lax.broadcasted_iota(jnp.int32, (ROWS, 128), 1) + (p * PART + g * 128)
                parts.append(jnp.where(partner == lane, part - 1.0, part).astype(BF16))
        tile = jnp.concatenate(parts, axis=1)
        tiles[:, pl.ds(first, CHUNK)] = tile
        return carry

    lax.fori_loop(0, COLS // CHUNK, pair_tile, 0)

    def row_sums(i, carry):
        rows = pl.ds(pl.multiple_of(i * PART, 128), PART)
        row_acc[:, rows] = lax.dot_general(meth_rows[...], tiles[rows, :], NT, preferred_element_type=F32)
        return carry

    lax.fori_loop(0, ROWS // PART, row_sums, 0)

    other = 1 - core
    up = scale * row_acc[...]
    inner = jnp.sum(dna_unit[...] * up, axis=0, keepdims=True)
    back_all[...] = (dna_inv[...] * (up - dna_unit[...] * inner)).astype(BF16)
    back_swap = post(back_all.at[pl.ds(pl.multiple_of(other * 256, 16), 256)], back_sib, sibling)
    back_swap.start()

    def col_tile(i, carry):
        first = pl.multiple_of(i * CHUNK, 128)
        for p in range(CHUNK // PART):
            lanes = pl.ds(pl.multiple_of(first + p * PART, 128), PART)
            up = scale * jnp.dot(dna_rowst[...], tiles[:, lanes], preferred_element_type=F32)
            unit_m = meth_unit[:, lanes]
            inner = jnp.sum(unit_m * up, axis=0, keepdims=True)
            meth_back[:, lanes] = (meth_inv[:, lanes] * (up - unit_m * inner)).astype(BF16)
        return carry

    lax.fori_loop(0, half, col_tile, 0)
    back_swap.wait_recv()
    for a in range(4):
        rows = pl.ds(pl.multiple_of(core * 256 + a * 64, 16), 64)
        both = back_all[rows, :].astype(F32) + back_sib[a * 64 : (a + 1) * 64, :].astype(F32)
        back_half[a] = both.astype(BF16)
    back_x = [post(back_half.at[lax.rem(x + o, 4)], back_in.at[o - 1], ring[o]) for o in (1, 2, 3)]
    for copy in back_x:
        copy.start()
    lax.fori_loop(half, 2 * half, col_tile, 0)

    def head_tile(i, carry):
        wide = pl.ds(pl.multiple_of(i * PART, 128), PART)
        m_acc[:, wide] = lax.dot_general(meth_pooled[...], meth_back[wide, :], NT, preferred_element_type=F32)
        return carry

    lax.fori_loop(0, E // PART, head_tile, 0)

    m_swap = post(m_acc.at[pl.ds(pl.multiple_of(other * M_HALF, 8), M_HALF)], m_sib, sibling)
    m_swap.start()

    swap = core == 1

    def pick(one, two):
        return tuple(jnp.where(swap, q, p) for p, q in zip(one, two))

    axis_a = [pick(p, q) for p, q in zip(ring, along_y)]
    axis_b = [pick(q, p) for p, q in zip(ring, along_y)]
    at_a = jnp.where(swap, y, x)
    at_b = jnp.where(swap, x, y)

    m_swap.wait_recv()

    def halve(i, carry):
        a, b = lax.div(i, 4), lax.rem(i, 4)
        row = jnp.where(swap, a * 96 + b * 24, b * 96 + a * 24)
        mine = m_acc[pl.ds(pl.multiple_of(core * M_HALF + row, 8), 24), :]
        m_first[a, b] = mine + m_sib[pl.ds(pl.multiple_of(row, 8), 24), :]
        return carry

    lax.fori_loop(0, 16, halve, 0)
    m_a = [post(m_first.at[lax.rem(at_a + o, 4)], m_first_in.at[o - 1], axis_a[o]) for o in (1, 2, 3)]
    for copy in m_a:
        copy.start()

    for copy in back_x:
        copy.wait_recv()
    back = back_half[x].astype(F32)
    for o in range(3):
        back = back + back_in[o].astype(F32)
    back = back.astype(BF16)
    for s in range(4):
        features = dna_pooled[s * D_SLICE : (s + 1) * D_SLICE, :]
        part = lax.dot_general(back, features, NT, preferred_element_type=F32)
        for a in range(4):
            d_first[a, :, s * D_SLICE : (s + 1) * D_SLICE] = part[a * 16 : (a + 1) * 16, :]
    d_y = [post(d_first.at[lax.rem(y + o, 4)], d_first_in.at[o - 1], along_y[o]) for o in (1, 2, 3)]
    for copy in d_y:
        copy.start()

    for copy in m_a:
        copy.wait_recv()
    for b in range(4):
        part = m_first[at_a, b]
        for o in range(3):
            part = part + m_first_in[o, b]
        m_second[b] = part
    m_b = [post(m_second.at[lax.rem(at_b + o, 4)], m_second_in.at[o - 1], axis_b[o]) for o in (1, 2, 3)]
    for copy in m_b:
        copy.start()

    for copy in d_y:
        copy.wait_recv()
    d_sum = d_first[y]
    for o in range(3):
        d_sum = d_sum + d_first_in[o]
    for s in range(8):
        lanes = slice(s * 128, (s + 1) * 128)
        third[s, 8:16, 0:128] = d_sum[0:8, lanes]
        third[s, 8:16, 128:256] = d_sum[8:16, lanes]
    for copy in m_b:
        copy.wait_recv()
    m_sum = m_second[at_b]
    for o in range(3):
        m_sum = m_sum + m_second_in[o]
    for s in range(6):
        third[s, 0:8, :] = m_sum[s // 2 * 8 : s // 2 * 8 + 8, s % 2 * 256 : s % 2 * 256 + 256]
    third[6, 0:8, :] = jnp.zeros((8, 256), F32)
    third[7, 0:8, :] = jnp.zeros((8, 256), F32)

    z_sum = [post(third.at[lax.rem(z + o, 8)], third_in.at[o - 1], along_z[o]) for o in range(1, 8)]
    for copy in z_sum:
        copy.start()
    for copy in z_sum:
        copy.wait_recv()
    total = third[z]
    for o in range(7):
        total = total + third_in[o]
    third_all[z] = total
    z_back = [post(third_all.at[z], third_all.at[z], along_z[o]) for o in range(1, 8)]
    for copy in z_back:
        copy.start()
    for copy in z_back:
        copy.wait_recv()

    for s in range(8):
        lanes = slice(s * 128, (s + 1) * 128)
        d_slab[y, 0:8, lanes] = third_all[s, 8:16, 0:128]
        d_slab[y, 8:16, lanes] = third_all[s, 8:16, 128:256]
    d_back = [post(d_slab.at[y], d_slab.at[y], along_y[o]) for o in (1, 2, 3)]
    for copy in d_back:
        copy.start()
    sub = core * M_HALF + y * 96 + x * 24
    for s in range(6):
        rows = pl.ds(pl.multiple_of(sub + s // 2 * 8, 8), 8)
        m_all[rows, s % 2 * 256 : s % 2 * 256 + 256] = third_all[s, 0:8, :]
    piece = m_all.at[pl.ds(pl.multiple_of(sub, 8), 24)]
    m_back_x = [post(piece, piece, ring[o]) for o in (1, 2, 3)]
    for copy in m_back_x:
        copy.start()

    def band(y_of, low, rows):
        first = core * M_HALF + lax.rem(y_of, 4) * 96 + low
        return m_all.at[pl.ds(pl.multiple_of(first, 8), rows)]

    def to(part, device):
        copy = post(part, part, device)
        copy.start()
        return copy

    for copy in m_back_x:
        copy.wait_recv()
    own_band = band(y, 0, 96)
    up_copy = to(own_band, along_y[1])
    down_copy = to(own_band, along_y[3])
    m_last = [to(own_band, sibling)]

    for copy in d_back:
        copy.wait_recv()
    eighth = core * 4 + x

    def slice_for(device):
        return d_slab.at[:, :, pl.ds(pl.multiple_of(device[1] * D_SLICE, 128), D_SLICE)]

    d_ring = [post(slice_for(device), d_fin.at[eighth], device) for device in ring[1:] + cross[1:] + [sibling]]
    for copy in d_ring:
        copy.start()
    own_lanes = pl.ds(pl.multiple_of(mp * D_SLICE, 128), D_SLICE)
    d_fin[eighth] = d_slab[:, :, own_lanes]

    up_copy.wait_recv()
    relay_up = to(band(y + 3, 0, 48), along_y[1])
    m_last.append(to(band(y + 3, 0, 96), sibling))
    down_copy.wait_recv()
    relay_down = to(band(y + 1, 48, 48), along_y[3])
    m_last.append(to(band(y + 1, 0, 96), sibling))

    for copy in d_ring:
        copy.wait_recv()
    d_out[...] = d_fin[...].reshape(E, D_SLICE)
    relay_up.wait_recv()
    relay_down.wait_recv()
    m_last.append(to(band(y + 2, 0, 96), sibling))
    for copy in m_last:
        copy.wait_recv()
    m_out[...] = m_all[...]

    for s in range(8):

        @pl.when(jnp.logical_not(is_me(targets[s])))
        def _():
            ids_copy(s).wait_send()

    for copy in taken:
        copy.wait_send()


def step_call(*args):
    vmem = pl.BlockSpec(memory_space=pltpu.VMEM)
    smem = pl.BlockSpec(memory_space=pltpu.SMEM)
    hbm = pl.BlockSpec(memory_space=pl.ANY)
    dma = pltpu.SemaphoreType.DMA
    f32 = lambda *shape: pltpu.VMEM(shape, F32)
    bf16 = lambda *shape: pltpu.VMEM(shape, BF16)
    i32 = lambda *shape: pltpu.VMEM(shape, jnp.int32)
    return pl.pallas_call(
        step_kernel,
        out_shape=(
            jax.ShapeDtypeStruct((E, D_SLICE), F32),
            jax.ShapeDtypeStruct((D_METH, E), F32),
        ),
        in_specs=[vmem, vmem, vmem, hbm, hbm, vmem, hbm, smem, smem],
        out_specs=(vmem, vmem),
        scratch_shapes=[
            bf16(VOCAB_DNA, D_SLICE),
            bf16(VOCAB_METH, D_METH),
            bf16(D_METH, E),
            i32(PAIR_DEV, 16),
            bf16(PAIR_DEV, VOCAB_DNA),
            i32(16, COLS),
            i32(2, 3, 128),
            i32(ROWS, 128),
            bf16(4 * D_SLICE, ROWS),
            bf16(E, 4 * D_SLICE),
            bf16(D_METH, VOCAB_METH),
            bf16(E, D_METH),
            bf16(D_METH, COLS),
            f32(E, COLS),
            bf16(E, COLS),
            f32(1, COLS),
            f32(E, ROWS),
            f32(1, ROWS),
            bf16(E, ROWS),
            bf16(ROWS, E),
            f32(E, ROWS),
            bf16(ROWS, COLS),
            bf16(E, COLS),
            f32(D_METH, E),
            f32(M_HALF, E),
            f32(4, 4, 24, E),
            f32(3, 4, 24, E),
            f32(4, 24, E),
            f32(3, 24, E),
            bf16(E, ROWS),
            bf16(256, ROWS),
            bf16(4, 64, ROWS),
            bf16(3, 64, ROWS),
            f32(4, 16, 4 * D_SLICE),
            f32(3, 16, 4 * D_SLICE),
            f32(8, 16, 256),
            f32(7, 16, 256),
            f32(8, 16, 256),
            f32(D_METH, E),
            f32(4, 16, 4 * D_SLICE),
            f32(8, 4, 16, D_SLICE),
            dma((8,)),
            dma((8,)),
            dma((N_COPIES,)),
            dma((N_COPIES,)),
            dma((4,)),
        ],
        compiler_params=pltpu.CompilerParams(
            collective_id=0, has_side_effects=True, vmem_limit_bytes=56 * 1024 * 1024
        ),
        cost_estimate=pl.CostEstimate(flops=19 * 10**9, bytes_accessed=8 * 10**6, transcendentals=5 * 10**6),
        name="contrastive_step",
    )(*args)


def hand_over_kernel(d_in, m_in, d_out, m_out):
    for s in range(E // 128):
        d_out[:, s * 128 : (s + 1) * 128] = d_in[s * 128 : (s + 1) * 128, :].T
    m_out[...] = m_in[...]


def hand_over(d_part, m_part):
    vmem = pl.BlockSpec(memory_space=pltpu.VMEM)
    return pl.pallas_call(
        hand_over_kernel,
        out_shape=(
            jax.ShapeDtypeStruct((D_SLICE, E), F32),
            jax.ShapeDtypeStruct((D_METH, E), F32),
        ),
        in_specs=[vmem, vmem],
        out_specs=(vmem, vmem),
        compiler_params=pltpu.CompilerParams(vmem_limit_bytes=8 * 1024 * 1024),
        name="hand_over",
    )(d_part, m_part)


def per_device(
    dna_ids,
    meth_ids,
    pair_index,
    dna_table,
    meth_table,
    dna_proj,
    meth_proj,
    logit_scale,
    logit_bias,
):
    d_part, m_part = step_call(
        dna_ids.T,
        meth_ids.T,
        pair_index.reshape(3, 128),
        dna_table,
        meth_table,
        dna_proj,
        meth_proj,
        logit_scale,
        logit_bias,
    )
    return hand_over(d_part, m_part)


def solution(mesh):
    placed = (
        P("blk", None),
        P("blk", None),
        P("blk"),
        P(None, "mp"),
        P(),
        P("mp", None),
        P(),
        P(),
        P(),
    )
    return jax.shard_map(
        per_device, mesh=mesh, in_specs=placed, out_specs=(P("mp", None), P()), check_vma=False
    )
```

```python
import jax
import jax.numpy as jnp
from jax import lax
from jax.experimental import pallas as pl
from jax.experimental.pallas import tpu as pltpu
from jax.sharding import PartitionSpec as P

MESH = pl.DeviceIdType.MESH
F32 = jnp.float32
BF16 = jnp.bfloat16
EPS = 1e-06

PAIR_DEV = 384
ROWS = 2 * PAIR_DEV
COLS = 8 * PAIR_DEV
E = 512
D_SLICE = 256
D_METH = 768
VOCAB_DNA = 4096
VOCAB_METH = 512
CHUNK = 1536
PART = 512
LOG2E = 1.4426950408889634
M_HALF = 384
N_COPIES = 64

NT = (((1,), (1,)), ((), ()))


def place():
    blk, mp = lax.axis_index("blk"), lax.axis_index("mp")
    z = lax.div(blk, 8)
    y = lax.rem(lax.div(blk, 2), 4)
    x = lax.rem(blk, 2) * 2 + lax.div(mp, 2)
    return blk, mp, z, y, x, lax.rem(mp, 2)


def device_at(z, y, x, core):
    return (z * 8 + y * 2 + lax.div(x, 2), lax.rem(x, 2) * 2 + core)


def signal(device):
    pl.semaphore_signal(
        pltpu.get_barrier_semaphore(), inc=1, device_id=device, device_id_type=MESH
    )


def send(src, dst, send_sem, recv_sem, device):
    return pltpu.make_async_remote_copy(
        src_ref=src,
        dst_ref=dst,
        send_sem=send_sem,
        recv_sem=recv_sem,
        device_id=device,
        device_id_type=MESH,
    )


def step_kernel(
    dna_ids,
    meth_ids,
    pairs,
    dna_table_hbm,
    meth_table_hbm,
    dna_proj,
    meth_proj_hbm,
    scale_ref,
    bias_ref,
    d_out,
    m_out,
    dna_table,
    meth_table,
    meth_proj,
    dna_tokens,
    counts,
    ids_all,
    pair_all,
    pair_wide,
    dna_pooled,
    dna_projt,
    meth_tablet,
    meth_projt,
    meth_pooled,
    meth_unit,
    meth_rows,
    meth_inv,
    dna_unit,
    dna_inv,
    dna_rowst,
    dna_rows,
    row_acc,
    tiles,
    meth_back,
    m_acc,
    m_sib,
    m_first,
    m_first_in,
    m_second,
    m_second_in,
    back_all,
    back_sib,
    back_half,
    back_in,
    d_first,
    d_first_in,
    third,
    third_in,
    third_all,
    m_all,
    d_slab,
    d_fin,
    ids_send,
    ids_recv,
    send_sems,
    recv_sems,
    local_sems,
):
    blk, mp, z, y, x, core = place()
    x_hi = lax.div(x, 2)
    sibling = device_at(z, y, x, 1 - core)
    ring = [device_at(z, y, lax.rem(x + o, 4), core) for o in range(4)]
    cross = [device_at(z, y, lax.rem(x + o, 4), 1 - core) for o in range(4)]
    along_y = [device_at(z, lax.rem(y + o, 4), x, core) for o in range(4)]
    along_z = [device_at(lax.rem(z + o, 8), y, x, core) for o in range(8)]
    slot = lax.rem(blk, 8)
    block = x_hi * 4 + mp
    taken = []

    def post(src, dst, device):
        n = len(taken)
        copy = send(src, dst, send_sems.at[n], recv_sems.at[n], device)
        taken.append(copy)
        return copy

    fetch = [
        pltpu.make_async_copy(src, dst, local_sems.at[1 + n])
        for n, (src, dst) in enumerate(
            ((dna_table_hbm, dna_table), (meth_table_hbm, meth_table), (meth_proj_hbm, meth_proj))
        )
    ]
    for copy in fetch:
        copy.start()

    targets = [device_at(s, mp, lax.div(z, 2), lax.rem(z, 2)) for s in range(8)]
    sources = [device_at(block, s // 2, (s % 2) * 2 + lax.div(y, 2), lax.rem(y, 2)) for s in range(8)]

    def is_me(device):
        return jnp.logical_and(device[0] == blk, device[1] == mp)

    for s in range(8):

        @pl.when(jnp.logical_not(is_me(sources[s])))
        def _():
            signal(sources[s])

    for o in (1, 2, 3):
        signal(ring[o])
        signal(cross[o])
        signal(along_y[o])
    for o in range(1, 8):
        signal(along_z[o])
    signal(sibling)
    to_self = jnp.logical_and(mp == y, block == z).astype(jnp.int32)
    pl.semaphore_wait(pltpu.get_barrier_semaphore(), 25 - to_self)

    def ids_copy(s):
        lanes = pl.ds(pl.multiple_of(slot * PAIR_DEV, 128), PAIR_DEV)
        return send(meth_ids, ids_all.at[:, lanes], ids_send.at[s], ids_recv.at[slot], targets[s])

    def ids_arrival(s):
        lanes = pl.ds(s * PAIR_DEV, PAIR_DEV)
        return send(meth_ids, ids_all.at[:, lanes], ids_send.at[s], ids_recv.at[s], sources[s])

    for s in range(8):

        @pl.when(jnp.logical_not(is_me(targets[s])))
        def _():
            ids_copy(s).start()

        @pl.when(is_me(targets[s]))
        def _():
            lanes = pl.ds(pl.multiple_of(slot * PAIR_DEV, 128), PAIR_DEV)
            local = pltpu.make_async_copy(meth_ids, ids_all.at[:, lanes], local_sems.at[0])
            local.start()
            local.wait()

    pair_copy = post(pairs, pair_all.at[x_hi], ring[2])
    pair_copy.start()
    pair_all[x_hi] = pairs[...]

    dna_projt[:, pl.ds(pl.multiple_of(mp * D_SLICE, 128), D_SLICE)] = dna_proj[...].T
    toward = 1 + 2 * core
    far = device_at(z, y, lax.rem(x + toward, 4), core)
    other_mp = lax.rem(mp + 2, 4)

    def quarter(of):
        return dna_projt.at[:, pl.ds(pl.multiple_of(of * D_SLICE, 128), D_SLICE)]

    proj_far = post(quarter(mp), quarter(mp), far)
    proj_sib = post(quarter(mp), quarter(mp), sibling)
    proj_fwd = post(quarter(other_mp), quarter(other_mp), sibling)
    proj_far.start()
    proj_sib.start()

    dna_tokens[...] = dna_ids[...].T

    def count_dna(i, carry):
        rows = pl.ds(pl.multiple_of(i * 16, 16), 16)
        ids = dna_tokens[rows, :]
        place_of = jnp.bitwise_and(ids, VOCAB_DNA // 4 - 1)
        amount = jnp.left_shift(1, jnp.right_shift(ids, 10) * 8)
        lane = lax.broadcasted_iota(jnp.int32, (16, VOCAB_DNA // 4), 1)
        total = jnp.zeros((16, VOCAB_DNA // 4), jnp.int32)
        for t in range(16):
            total = total + jnp.where(lane == place_of[:, t : t + 1], amount[:, t : t + 1], 0)
        for f in range(4):
            field = jnp.bitwise_and(jnp.right_shift(total, 8 * f), 255)
            counts[rows, f * 1024 : (f + 1) * 1024] = field.astype(F32).astype(BF16)
        return carry

    lax.fori_loop(0, PAIR_DEV // 16, count_dna, 0)
    fetch[0].wait()
    pooled = jnp.dot(counts[...], dna_table[...], preferred_element_type=F32) * 0.0625
    own_lanes = pl.ds(pl.multiple_of(x_hi * PAIR_DEV, 128), PAIR_DEV)
    dna_pooled[pl.ds(pl.multiple_of(mp * D_SLICE, 16), D_SLICE), own_lanes] = pooled.T.astype(BF16)

    def pool_block(x_of, core_of, low=0, count=D_SLICE):
        first = (lax.rem(x_of, 2) * 2 + core_of) * D_SLICE + low
        lanes = pl.ds(pl.multiple_of(lax.div(x_of, 2) * PAIR_DEV, 128), PAIR_DEV)
        return dna_pooled.at[pl.ds(pl.multiple_of(first, 16), count), lanes]

    own = pool_block(x, core)
    from_left = pool_block(lax.rem(x + 3, 4), core)
    from_right = pool_block(lax.rem(x + 1, 4), core)
    from_across = pool_block(lax.rem(x + 2, 4), core)
    pool_right = post(own, own, ring[1])
    pool_left = post(own, own, ring[3])
    pool_sib = post(own, own, sibling)
    pool_right.start()
    pool_left.start()
    pool_sib.start()
    half_left = pool_block(lax.rem(x + 3, 4), core, 0, 128)
    half_right = pool_block(lax.rem(x + 1, 4), core, 128, 128)
    relay_right = post(half_left, half_left, ring[1])
    relay_left = post(half_right, half_right, ring[3])
    pool_fwd = [post(part, part, sibling) for part in (from_left, from_right, from_across)]

    fetch[1].wait()
    fetch[2].wait()
    meth_tablet[...] = meth_table[...].T
    meth_projt[...] = meth_proj[...].T
    for s in range(8):

        @pl.when(jnp.logical_not(is_me(sources[s])))
        def _():
            ids_arrival(s).wait_recv()

    def count_meth(ids):
        place_of = jnp.bitwise_and(ids, 127)
        amount = jnp.left_shift(1, jnp.right_shift(ids, 7) * 8)
        row = lax.broadcasted_iota(jnp.int32, (128, 128), 0)
        total = jnp.zeros((128, 128), jnp.int32)
        for t in range(16):
            total = total + jnp.where(row == place_of[t : t + 1, :], amount[t : t + 1, :], 0)
        fields = [jnp.bitwise_and(jnp.right_shift(total, 8 * f), 255) for f in range(4)]
        return jnp.concatenate([field.astype(F32).astype(BF16) for field in fields], axis=0)

    def embed_meth(i, carry):
        for p in range(CHUNK // PART):
            first = pl.multiple_of(i * CHUNK + p * PART, 128)
            lanes = pl.ds(first, PART)
            ids = [ids_all[:, pl.ds(pl.multiple_of(first + 128 * g, 128), 128)] for g in range(PART // 128)]
            tokens = jnp.concatenate([count_meth(part) for part in ids], axis=1)
            pooled_m = jnp.dot(meth_tablet[...], tokens, preferred_element_type=F32)
            pooled_m = (pooled_m * 0.0625).astype(BF16)
            meth_pooled[:, lanes] = pooled_m
            raw = jnp.dot(meth_projt[...], pooled_m, preferred_element_type=F32)
            inverse = lax.rsqrt(jnp.sum(raw * raw, axis=0, keepdims=True) + EPS)
            unit = raw * inverse
            meth_inv[:, lanes] = inverse
            meth_unit[:, lanes] = unit
            meth_rows[:, lanes] = unit.astype(BF16)
        return carry

    half = COLS // CHUNK // 2
    lax.fori_loop(0, half, embed_meth, 0)
    pool_right.wait_recv()
    relay_right.start()
    pool_left.wait_recv()
    relay_left.start()
    pool_fwd[0].start()
    pool_fwd[1].start()
    proj_far.wait_recv()
    proj_fwd.start()
    lax.fori_loop(half, 2 * half, embed_meth, 0)
    relay_right.wait_recv()
    relay_left.wait_recv()
    pool_fwd[2].start()
    proj_sib.wait_recv()
    proj_fwd.wait_recv()
    pair_copy.wait_recv()
    for h in range(2):
        words = pair_all[h]
        for a in range(3):
            wide = jnp.broadcast_to(words[a : a + 1, :], (128, 128))
            first = h * PAIR_DEV + a * 128
            pair_wide[first : first + 128, :] = wide.T
    pool_sib.wait_recv()
    for copy in pool_fwd:
        copy.wait_recv()

    raw = jnp.dot(dna_projt[...], dna_pooled[...], preferred_element_type=F32)
    inverse = lax.rsqrt(jnp.sum(raw * raw, axis=0, keepdims=True) + EPS)
    unit = raw * inverse
    dna_inv[...] = inverse
    dna_unit[...] = unit
    unit_low = unit.astype(BF16)
    dna_rowst[...] = unit_low
    dna_rows[...] = unit_low.T

    scale = scale_ref[0]
    bias = bias_ref[0]
    slope, offset = scale * -LOG2E, bias * -LOG2E
    first_col = block * COLS

    def pair_tile(i, carry):
        first = pl.multiple_of(i * CHUNK, 128)
        partner = pair_wide[...] - (first_col + first)
        parts = []
        for p in range(CHUNK // PART):
            rows_m = meth_rows[:, pl.ds(pl.multiple_of(first + p * PART, 128), PART)]
            dots = jnp.dot(dna_rows[...], rows_m, preferred_element_type=F32)
            lower = 1.0 + jnp.exp2(slope * dots + offset)
            prob = pl.reciprocal(lower, approx=True)
            prob = prob * (2.0 - lower * prob)
            for g in range(PART // 128):
                part = prob[:, g * 128 : (g + 1) * 128]
                lane = lax.broadcasted_iota(jnp.int32, (ROWS, 128), 1) + (p * PART + g * 128)
                parts.append(jnp.where(partner == lane, part - 1.0, part).astype(BF16))
        tile = jnp.concatenate(parts, axis=1)
        tiles[:, pl.ds(first, CHUNK)] = tile
        return carry

    lax.fori_loop(0, COLS // CHUNK, pair_tile, 0)

    row_acc[...] = lax.dot_general(meth_rows[...], tiles[...], NT, preferred_element_type=F32)

    other = 1 - core
    up = scale * row_acc[...]
    inner = jnp.sum(dna_unit[...] * up, axis=0, keepdims=True)
    back_all[...] = (dna_inv[...] * (up - dna_unit[...] * inner)).astype(BF16)
    back_swap = post(back_all.at[pl.ds(pl.multiple_of(other * 256, 16), 256)], back_sib, sibling)
    back_swap.start()

    def col_tile(i, carry):
        first = pl.multiple_of(i * CHUNK, 128)
        for p in range(CHUNK // PART):
            lanes = pl.ds(pl.multiple_of(first + p * PART, 128), PART)
            up = scale * jnp.dot(dna_rowst[...], tiles[:, lanes], preferred_element_type=F32)
            unit_m = meth_unit[:, lanes]
            inner = jnp.sum(unit_m * up, axis=0, keepdims=True)
            meth_back[:, lanes] = (meth_inv[:, lanes] * (up - unit_m * inner)).astype(BF16)
        return carry

    lax.fori_loop(0, half, col_tile, 0)
    back_swap.wait_recv()
    for a in range(4):
        rows = pl.ds(pl.multiple_of(core * 256 + a * 64, 16), 64)
        both = back_all[rows, :].astype(F32) + back_sib[a * 64 : (a + 1) * 64, :].astype(F32)
        back_half[a] = both.astype(BF16)
    back_x = [post(back_half.at[lax.rem(x + o, 4)], back_in.at[o - 1], ring[o]) for o in (1, 2, 3)]
    for copy in back_x:
        copy.start()
    lax.fori_loop(half, 2 * half, col_tile, 0)

    m_acc[...] = lax.dot_general(meth_pooled[...], meth_back[...], NT, preferred_element_type=F32)

    m_swap = post(m_acc.at[pl.ds(pl.multiple_of(other * M_HALF, 8), M_HALF)], m_sib, sibling)
    m_swap.start()

    swap = core == 1

    def pick(one, two):
        return tuple(jnp.where(swap, q, p) for p, q in zip(one, two))

    axis_a = [pick(p, q) for p, q in zip(ring, along_y)]
    axis_b = [pick(q, p) for p, q in zip(ring, along_y)]
    at_a = jnp.where(swap, y, x)
    at_b = jnp.where(swap, x, y)

    m_swap.wait_recv()

    def halve(i, carry):
        a, b = lax.div(i, 4), lax.rem(i, 4)
        row = jnp.where(swap, a * 96 + b * 24, b * 96 + a * 24)
        mine = m_acc[pl.ds(pl.multiple_of(core * M_HALF + row, 8), 24), :]
        m_first[a, b] = mine + m_sib[pl.ds(pl.multiple_of(row, 8), 24), :]
        return carry

    lax.fori_loop(0, 16, halve, 0)
    m_a = [post(m_first.at[lax.rem(at_a + o, 4)], m_first_in.at[o - 1], axis_a[o]) for o in (1, 2, 3)]
    for copy in m_a:
        copy.start()

    for copy in back_x:
        copy.wait_recv()
    back = back_half[x].astype(F32)
    for o in range(3):
        back = back + back_in[o].astype(F32)
    back = back.astype(BF16)
    for s in range(4):
        features = dna_pooled[s * D_SLICE : (s + 1) * D_SLICE, :]
        part = lax.dot_general(back, features, NT, preferred_element_type=F32)
        for a in range(4):
            d_first[a, :, s * D_SLICE : (s + 1) * D_SLICE] = part[a * 16 : (a + 1) * 16, :]
    d_y = [post(d_first.at[lax.rem(y + o, 4)], d_first_in.at[o - 1], along_y[o]) for o in (1, 2, 3)]
    for copy in d_y:
        copy.start()

    for copy in m_a:
        copy.wait_recv()
    for b in range(4):
        part = m_first[at_a, b]
        for o in range(3):
            part = part + m_first_in[o, b]
        m_second[b] = part
    m_b = [post(m_second.at[lax.rem(at_b + o, 4)], m_second_in.at[o - 1], axis_b[o]) for o in (1, 2, 3)]
    for copy in m_b:
        copy.start()

    for copy in d_y:
        copy.wait_recv()
    d_sum = d_first[y]
    for o in range(3):
        d_sum = d_sum + d_first_in[o]
    for s in range(8):
        lanes = slice(s * 128, (s + 1) * 128)
        third[s, 8:16, 0:128] = d_sum[0:8, lanes]
        third[s, 8:16, 128:256] = d_sum[8:16, lanes]
    for copy in m_b:
        copy.wait_recv()
    m_sum = m_second[at_b]
    for o in range(3):
        m_sum = m_sum + m_second_in[o]
    for s in range(6):
        third[s, 0:8, :] = m_sum[s // 2 * 8 : s // 2 * 8 + 8, s % 2 * 256 : s % 2 * 256 + 256]
    third[6, 0:8, :] = jnp.zeros((8, 256), F32)
    third[7, 0:8, :] = jnp.zeros((8, 256), F32)

    z_sum = [post(third.at[lax.rem(z + o, 8)], third_in.at[o - 1], along_z[o]) for o in range(1, 8)]
    for copy in z_sum:
        copy.start()
    for copy in z_sum:
        copy.wait_recv()
    total = third[z]
    for o in range(7):
        total = total + third_in[o]
    third_all[z] = total
    z_back = [post(third_all.at[z], third_all.at[z], along_z[o]) for o in range(1, 8)]
    for copy in z_back:
        copy.start()
    for copy in z_back:
        copy.wait_recv()

    for s in range(8):
        lanes = slice(s * 128, (s + 1) * 128)
        d_slab[y, 0:8, lanes] = third_all[s, 8:16, 0:128]
        d_slab[y, 8:16, lanes] = third_all[s, 8:16, 128:256]
    d_back = [post(d_slab.at[y], d_slab.at[y], along_y[o]) for o in (1, 2, 3)]
    for copy in d_back:
        copy.start()
    sub = core * M_HALF + y * 96 + x * 24
    for s in range(6):
        rows = pl.ds(pl.multiple_of(sub + s // 2 * 8, 8), 8)
        m_all[rows, s % 2 * 256 : s % 2 * 256 + 256] = third_all[s, 0:8, :]
    piece = m_all.at[pl.ds(pl.multiple_of(sub, 8), 24)]
    m_back_x = [post(piece, piece, ring[o]) for o in (1, 2, 3)]
    for copy in m_back_x:
        copy.start()

    def band(y_of, low, rows):
        first = core * M_HALF + lax.rem(y_of, 4) * 96 + low
        return m_all.at[pl.ds(pl.multiple_of(first, 8), rows)]

    def to(part, device):
        copy = post(part, part, device)
        copy.start()
        return copy

    for copy in m_back_x:
        copy.wait_recv()
    own_band = band(y, 0, 96)
    up_copy = to(own_band, along_y[1])
    down_copy = to(own_band, along_y[3])
    m_last = [to(own_band, sibling)]

    for copy in d_back:
        copy.wait_recv()
    eighth = core * 4 + x

    def slice_for(device):
        return d_slab.at[:, :, pl.ds(pl.multiple_of(device[1] * D_SLICE, 128), D_SLICE)]

    d_ring = [post(slice_for(device), d_fin.at[eighth], device) for device in ring[1:] + cross[1:] + [sibling]]
    for copy in d_ring:
        copy.start()
    own_lanes = pl.ds(pl.multiple_of(mp * D_SLICE, 128), D_SLICE)
    d_fin[eighth] = d_slab[:, :, own_lanes]

    up_copy.wait_recv()
    relay_up = to(band(y + 3, 0, 48), along_y[1])
    m_last.append(to(band(y + 3, 0, 96), sibling))
    down_copy.wait_recv()
    relay_down = to(band(y + 1, 48, 48), along_y[3])
    m_last.append(to(band(y + 1, 0, 96), sibling))

    for copy in d_ring:
        copy.wait_recv()
    d_out[...] = d_fin[...].reshape(E, D_SLICE)
    relay_up.wait_recv()
    relay_down.wait_recv()
    m_last.append(to(band(y + 2, 0, 96), sibling))
    for copy in m_last:
        copy.wait_recv()
    m_out[...] = m_all[...]

    for s in range(8):

        @pl.when(jnp.logical_not(is_me(targets[s])))
        def _():
            ids_copy(s).wait_send()

    for copy in taken:
        copy.wait_send()


def step_call(*args):
    vmem = pl.BlockSpec(memory_space=pltpu.VMEM)
    smem = pl.BlockSpec(memory_space=pltpu.SMEM)
    hbm = pl.BlockSpec(memory_space=pl.ANY)
    dma = pltpu.SemaphoreType.DMA
    f32 = lambda *shape: pltpu.VMEM(shape, F32)
    bf16 = lambda *shape: pltpu.VMEM(shape, BF16)
    i32 = lambda *shape: pltpu.VMEM(shape, jnp.int32)
    return pl.pallas_call(
        step_kernel,
        out_shape=(
            jax.ShapeDtypeStruct((E, D_SLICE), F32),
            jax.ShapeDtypeStruct((D_METH, E), F32),
        ),
        in_specs=[vmem, vmem, vmem, hbm, hbm, vmem, hbm, smem, smem],
        out_specs=(vmem, vmem),
        scratch_shapes=[
            bf16(VOCAB_DNA, D_SLICE),
            bf16(VOCAB_METH, D_METH),
            bf16(D_METH, E),
            i32(PAIR_DEV, 16),
            bf16(PAIR_DEV, VOCAB_DNA),
            i32(16, COLS),
            i32(2, 3, 128),
            i32(ROWS, 128),
            bf16(4 * D_SLICE, ROWS),
            bf16(E, 4 * D_SLICE),
            bf16(D_METH, VOCAB_METH),
            bf16(E, D_METH),
            bf16(D_METH, COLS),
            f32(E, COLS),
            bf16(E, COLS),
            f32(1, COLS),
            f32(E, ROWS),
            f32(1, ROWS),
            bf16(E, ROWS),
            bf16(ROWS, E),
            f32(E, ROWS),
            bf16(ROWS, COLS),
            bf16(E, COLS),
            f32(D_METH, E),
            f32(M_HALF, E),
            f32(4, 4, 24, E),
            f32(3, 4, 24, E),
            f32(4, 24, E),
            f32(3, 24, E),
            bf16(E, ROWS),
            bf16(256, ROWS),
            bf16(4, 64, ROWS),
            bf16(3, 64, ROWS),
            f32(4, 16, 4 * D_SLICE),
            f32(3, 16, 4 * D_SLICE),
            f32(8, 16, 256),
            f32(7, 16, 256),
            f32(8, 16, 256),
            f32(D_METH, E),
            f32(4, 16, 4 * D_SLICE),
            f32(8, 4, 16, D_SLICE),
            dma((8,)),
            dma((8,)),
            dma((N_COPIES,)),
            dma((N_COPIES,)),
            dma((4,)),
        ],
        compiler_params=pltpu.CompilerParams(
            collective_id=0, has_side_effects=True, vmem_limit_bytes=56 * 1024 * 1024
        ),
        cost_estimate=pl.CostEstimate(flops=19 * 10**9, bytes_accessed=8 * 10**6, transcendentals=5 * 10**6),
        name="contrastive_step",
    )(*args)


def hand_over_kernel(d_in, m_in, d_out, m_out):
    for s in range(E // 128):
        d_out[:, s * 128 : (s + 1) * 128] = d_in[s * 128 : (s + 1) * 128, :].T
    m_out[...] = m_in[...]


def hand_over(d_part, m_part):
    vmem = pl.BlockSpec(memory_space=pltpu.VMEM)
    return pl.pallas_call(
        hand_over_kernel,
        out_shape=(
            jax.ShapeDtypeStruct((D_SLICE, E), F32),
            jax.ShapeDtypeStruct((D_METH, E), F32),
        ),
        in_specs=[vmem, vmem],
        out_specs=(vmem, vmem),
        compiler_params=pltpu.CompilerParams(vmem_limit_bytes=8 * 1024 * 1024),
        name="hand_over",
    )(d_part, m_part)


def per_device(
    dna_ids,
    meth_ids,
    pair_index,
    dna_table,
    meth_table,
    dna_proj,
    meth_proj,
    logit_scale,
    logit_bias,
):
    d_part, m_part = step_call(
        dna_ids.T,
        meth_ids.T,
        pair_index.reshape(3, 128),
        dna_table,
        meth_table,
        dna_proj,
        meth_proj,
        logit_scale,
        logit_bias,
    )
    return hand_over(d_part, m_part)


def solution(mesh):
    placed = (
        P("blk", None),
        P("blk", None),
        P("blk"),
        P(None, "mp"),
        P(),
        P("mp", None),
        P(),
        P(),
        P(),
    )
    return jax.shard_map(
        per_device, mesh=mesh, in_specs=placed, out_specs=(P("mp", None), P()), check_vma=False
    )
```

```python
import jax
import jax.numpy as jnp
from jax import lax
from jax.experimental import pallas as pl
from jax.experimental.pallas import tpu as pltpu
from jax.sharding import PartitionSpec as P

MESH = pl.DeviceIdType.MESH
F32 = jnp.float32
BF16 = jnp.bfloat16
EPS = 1e-06

PAIR_DEV = 384
ROWS = 2 * PAIR_DEV
COLS = 8 * PAIR_DEV
E = 512
D_SLICE = 256
D_METH = 768
VOCAB_DNA = 4096
VOCAB_METH = 512
CHUNK = 1536
PART = 512
LOG2E = 1.4426950408889634
M_HALF = 384
N_COPIES = 64

NT = (((1,), (1,)), ((), ()))


def place():
    blk, mp = lax.axis_index("blk"), lax.axis_index("mp")
    z = lax.div(blk, 8)
    y = lax.rem(lax.div(blk, 2), 4)
    x = lax.rem(blk, 2) * 2 + lax.div(mp, 2)
    return blk, mp, z, y, x, lax.rem(mp, 2)


def device_at(z, y, x, core):
    return (z * 8 + y * 2 + lax.div(x, 2), lax.rem(x, 2) * 2 + core)


def signal(device):
    pl.semaphore_signal(
        pltpu.get_barrier_semaphore(), inc=1, device_id=device, device_id_type=MESH
    )


def send(src, dst, send_sem, recv_sem, device):
    return pltpu.make_async_remote_copy(
        src_ref=src,
        dst_ref=dst,
        send_sem=send_sem,
        recv_sem=recv_sem,
        device_id=device,
        device_id_type=MESH,
    )


def pool_kernel(dna_ids, dna_table, dna_proj, pooled_out, projt_out, dna_tokens, counts):
    projt_out[...] = dna_proj[...].T
    dna_tokens[...] = dna_ids[...].T

    def count_dna(i, carry):
        rows = pl.ds(pl.multiple_of(i * 16, 16), 16)
        ids = dna_tokens[rows, :]
        place_of = jnp.bitwise_and(ids, VOCAB_DNA // 4 - 1)
        amount = jnp.left_shift(1, jnp.right_shift(ids, 10) * 8)
        lane = lax.broadcasted_iota(jnp.int32, (16, VOCAB_DNA // 4), 1)
        total = jnp.zeros((16, VOCAB_DNA // 4), jnp.int32)
        for t in range(16):
            total = total + jnp.where(lane == place_of[:, t : t + 1], amount[:, t : t + 1], 0)
        for f in range(4):
            field = jnp.bitwise_and(jnp.right_shift(total, 8 * f), 255)
            counts[rows, f * 1024 : (f + 1) * 1024] = field.astype(F32).astype(BF16)
        return carry

    lax.fori_loop(0, PAIR_DEV // 16, count_dna, 0)
    pooled = jnp.dot(counts[...], dna_table[...], preferred_element_type=F32) * 0.0625
    pooled_out[...] = pooled.T.astype(BF16)


def pool_call(*args):
    vmem = pl.BlockSpec(memory_space=pltpu.VMEM)
    return pl.pallas_call(
        pool_kernel,
        out_shape=(
            jax.ShapeDtypeStruct((D_SLICE, PAIR_DEV), BF16),
            jax.ShapeDtypeStruct((E, D_SLICE), BF16),
        ),
        in_specs=[vmem] * 3,
        out_specs=(vmem, vmem),
        scratch_shapes=[
            pltpu.VMEM((PAIR_DEV, 16), jnp.int32),
            pltpu.VMEM((PAIR_DEV, VOCAB_DNA), BF16),
        ],
        compiler_params=pltpu.CompilerParams(vmem_limit_bytes=16 * 1024 * 1024),
        name="pool_dna",
    )(*args)


def step_kernel(
    dna_part,
    dna_projt_part,
    meth_ids,
    pairs,
    meth_table_hbm,
    meth_proj_hbm,
    scale_ref,
    bias_ref,
    d_first,
    m_acc,
    meth_table,
    meth_proj,
    ids_all,
    pair_all,
    pair_wide,
    dna_pooled,
    dna_projt,
    meth_tablet,
    meth_projt,
    meth_pooled,
    meth_unit,
    meth_rows,
    meth_inv,
    dna_unit,
    dna_inv,
    dna_rowst,
    dna_rows,
    row_acc,
    tiles,
    meth_back,
    back_all,
    back_sib,
    back_half,
    back_in,
    ids_send,
    ids_recv,
    send_sems,
    recv_sems,
    local_sems,
):
    blk, mp, z, y, x, core = place()
    x_hi = lax.div(x, 2)
    sibling = device_at(z, y, x, 1 - core)
    ring = [device_at(z, y, lax.rem(x + o, 4), core) for o in range(4)]
    slot = lax.rem(blk, 8)
    block = x_hi * 4 + mp
    taken = []

    def post(src, dst, device):
        n = len(taken)
        copy = send(src, dst, send_sems.at[n], recv_sems.at[n], device)
        taken.append(copy)
        return copy

    fetch = [
        pltpu.make_async_copy(src, dst, local_sems.at[1 + n])
        for n, (src, dst) in enumerate(
            ((meth_table_hbm, meth_table), (meth_proj_hbm, meth_proj))
        )
    ]
    for copy in fetch:
        copy.start()

    targets = [device_at(s, mp, lax.div(z, 2), lax.rem(z, 2)) for s in range(8)]
    sources = [device_at(block, s // 2, (s % 2) * 2 + lax.div(y, 2), lax.rem(y, 2)) for s in range(8)]

    def is_me(device):
        return jnp.logical_and(device[0] == blk, device[1] == mp)

    for s in range(8):

        @pl.when(jnp.logical_not(is_me(sources[s])))
        def _():
            signal(sources[s])

    for o in (1, 2, 3):
        signal(ring[o])
    signal(sibling)
    to_self = jnp.logical_and(mp == y, block == z).astype(jnp.int32)
    pl.semaphore_wait(pltpu.get_barrier_semaphore(), 12 - to_self)

    def ids_copy(s):
        lanes = pl.ds(pl.multiple_of(slot * PAIR_DEV, 128), PAIR_DEV)
        return send(meth_ids, ids_all.at[:, lanes], ids_send.at[s], ids_recv.at[slot], targets[s])

    def ids_arrival(s):
        lanes = pl.ds(s * PAIR_DEV, PAIR_DEV)
        return send(meth_ids, ids_all.at[:, lanes], ids_send.at[s], ids_recv.at[s], sources[s])

    for s in range(8):

        @pl.when(jnp.logical_not(is_me(targets[s])))
        def _():
            ids_copy(s).start()

        @pl.when(is_me(targets[s]))
        def _():
            lanes = pl.ds(pl.multiple_of(slot * PAIR_DEV, 128), PAIR_DEV)
            local = pltpu.make_async_copy(meth_ids, ids_all.at[:, lanes], local_sems.at[0])
            local.start()
            local.wait()

    pair_copy = post(pairs, pair_all.at[x_hi], ring[2])
    pair_copy.start()
    pair_all[x_hi] = pairs[...]

    dna_projt[:, pl.ds(pl.multiple_of(mp * D_SLICE, 128), D_SLICE)] = dna_projt_part[...]
    toward = 1 + 2 * core
    far = device_at(z, y, lax.rem(x + toward, 4), core)
    other_mp = lax.rem(mp + 2, 4)

    def quarter(of):
        return dna_projt.at[:, pl.ds(pl.multiple_of(of * D_SLICE, 128), D_SLICE)]

    proj_far = post(quarter(mp), quarter(mp), far)
    proj_sib = post(quarter(mp), quarter(mp), sibling)
    proj_fwd = post(quarter(other_mp), quarter(other_mp), sibling)
    proj_far.start()
    proj_sib.start()

    own_lanes = pl.ds(pl.multiple_of(x_hi * PAIR_DEV, 128), PAIR_DEV)
    dna_pooled[pl.ds(pl.multiple_of(mp * D_SLICE, 16), D_SLICE), own_lanes] = dna_part[...]

    def pool_block(x_of, core_of, low=0, count=D_SLICE):
        first = (lax.rem(x_of, 2) * 2 + core_of) * D_SLICE + low
        lanes = pl.ds(pl.multiple_of(lax.div(x_of, 2) * PAIR_DEV, 128), PAIR_DEV)
        return dna_pooled.at[pl.ds(pl.multiple_of(first, 16), count), lanes]

    own = pool_block(x, core)
    from_left = pool_block(lax.rem(x + 3, 4), core)
    from_right = pool_block(lax.rem(x + 1, 4), core)
    from_across = pool_block(lax.rem(x + 2, 4), core)
    pool_right = post(own, own, ring[1])
    pool_left = post(own, own, ring[3])
    pool_sib = post(own, own, sibling)
    pool_right.start()
    pool_left.start()
    pool_sib.start()
    half_left = pool_block(lax.rem(x + 3, 4), core, 0, 128)
    half_right = pool_block(lax.rem(x + 1, 4), core, 128, 128)
    relay_right = post(half_left, half_left, ring[1])
    relay_left = post(half_right, half_right, ring[3])
    pool_fwd = [post(part, part, sibling) for part in (from_left, from_right, from_across)]

    fetch[0].wait()
    fetch[1].wait()
    meth_tablet[...] = meth_table[...].T
    meth_projt[...] = meth_proj[...].T
    for s in range(8):

        @pl.when(jnp.logical_not(is_me(sources[s])))
        def _():
            ids_arrival(s).wait_recv()

    def count_meth(ids):
        place_of = jnp.bitwise_and(ids, 127)
        amount = jnp.left_shift(1, jnp.right_shift(ids, 7) * 8)
        row = lax.broadcasted_iota(jnp.int32, (128, 128), 0)
        total = jnp.zeros((128, 128), jnp.int32)
        for t in range(16):
            total = total + jnp.where(row == place_of[t : t + 1, :], amount[t : t + 1, :], 0)
        fields = [jnp.bitwise_and(jnp.right_shift(total, 8 * f), 255) for f in range(4)]
        return jnp.concatenate([field.astype(F32).astype(BF16) for field in fields], axis=0)

    def embed_meth(i, carry):
        for p in range(CHUNK // PART):
            first = pl.multiple_of(i * CHUNK + p * PART, 128)
            lanes = pl.ds(first, PART)
            ids = [ids_all[:, pl.ds(pl.multiple_of(first + 128 * g, 128), 128)] for g in range(PART // 128)]
            tokens = jnp.concatenate([count_meth(part) for part in ids], axis=1)
            pooled_m = jnp.dot(meth_tablet[...], tokens, preferred_element_type=F32)
            pooled_m = (pooled_m * 0.0625).astype(BF16)
            meth_pooled[:, lanes] = pooled_m
            raw = jnp.dot(meth_projt[...], pooled_m, preferred_element_type=F32)
            inverse = lax.rsqrt(jnp.sum(raw * raw, axis=0, keepdims=True) + EPS)
            unit = raw * inverse
            meth_inv[:, lanes] = inverse
            meth_unit[:, lanes] = unit
            meth_rows[:, lanes] = unit.astype(BF16)
        return carry

    half = COLS // CHUNK // 2
    lax.fori_loop(0, half, embed_meth, 0)
    pool_right.wait_recv()
    relay_right.start()
    pool_left.wait_recv()
    relay_left.start()
    pool_fwd[0].start()
    pool_fwd[1].start()
    proj_far.wait_recv()
    proj_fwd.start()
    lax.fori_loop(half, 2 * half, embed_meth, 0)
    relay_right.wait_recv()
    relay_left.wait_recv()
    pool_fwd[2].start()
    proj_sib.wait_recv()
    proj_fwd.wait_recv()
    pair_copy.wait_recv()
    for h in range(2):
        words = pair_all[h]
        for a in range(3):
            wide = jnp.broadcast_to(words[a : a + 1, :], (128, 128))
            first = h * PAIR_DEV + a * 128
            pair_wide[first : first + 128, :] = wide.T
    pool_sib.wait_recv()
    for copy in pool_fwd:
        copy.wait_recv()

    raw = jnp.dot(dna_projt[...], dna_pooled[...], preferred_element_type=F32)
    inverse = lax.rsqrt(jnp.sum(raw * raw, axis=0, keepdims=True) + EPS)
    unit = raw * inverse
    dna_inv[...] = inverse
    dna_unit[...] = unit
    unit_low = unit.astype(BF16)
    dna_rowst[...] = unit_low
    dna_rows[...] = unit_low.T

    scale = scale_ref[0]
    bias = bias_ref[0]
    slope, offset = scale * -LOG2E, bias * -LOG2E
    first_col = block * COLS

    def pair_tile(i, carry):
        first = pl.multiple_of(i * CHUNK, 128)
        partner = pair_wide[...] - (first_col + first)
        parts = []
        for p in range(CHUNK // PART):
            rows_m = meth_rows[:, pl.ds(pl.multiple_of(first + p * PART, 128), PART)]
            dots = jnp.dot(dna_rows[...], rows_m, preferred_element_type=F32)
            lower = 1.0 + jnp.exp2(slope * dots + offset)
            prob = pl.reciprocal(lower, approx=True)
            prob = prob * (2.0 - lower * prob)
            for g in range(PART // 128):
                part = prob[:, g * 128 : (g + 1) * 128]
                lane = lax.broadcasted_iota(jnp.int32, (ROWS, 128), 1) + (p * PART + g * 128)
                parts.append(jnp.where(partner == lane, part - 1.0, part).astype(BF16))
        tile = jnp.concatenate(parts, axis=1)
        tiles[:, pl.ds(first, CHUNK)] = tile
        return carry

    lax.fori_loop(0, COLS // CHUNK, pair_tile, 0)

    row_acc[...] = lax.dot_general(meth_rows[...], tiles[...], NT, preferred_element_type=F32)

    other = 1 - core
    up = scale * row_acc[...]
    inner = jnp.sum(dna_unit[...] * up, axis=0, keepdims=True)
    back_all[...] = (dna_inv[...] * (up - dna_unit[...] * inner)).astype(BF16)
    back_swap = post(back_all.at[pl.ds(pl.multiple_of(other * 256, 16), 256)], back_sib, sibling)
    back_swap.start()

    def col_tile(i, carry):
        first = pl.multiple_of(i * CHUNK, 128)
        for p in range(CHUNK // PART):
            lanes = pl.ds(pl.multiple_of(first + p * PART, 128), PART)
            up = scale * jnp.dot(dna_rowst[...], tiles[:, lanes], preferred_element_type=F32)
            unit_m = meth_unit[:, lanes]
            inner = jnp.sum(unit_m * up, axis=0, keepdims=True)
            meth_back[:, lanes] = (meth_inv[:, lanes] * (up - unit_m * inner)).astype(BF16)
        return carry

    lax.fori_loop(0, half, col_tile, 0)
    back_swap.wait_recv()
    for a in range(4):
        rows = pl.ds(pl.multiple_of(core * 256 + a * 64, 16), 64)
        both = back_all[rows, :].astype(F32) + back_sib[a * 64 : (a + 1) * 64, :].astype(F32)
        back_half[a] = both.astype(BF16)
    back_x = [post(back_half.at[lax.rem(x + o, 4)], back_in.at[o - 1], ring[o]) for o in (1, 2, 3)]
    for copy in back_x:
        copy.start()
    lax.fori_loop(half, 2 * half, col_tile, 0)

    m_acc[...] = lax.dot_general(meth_pooled[...], meth_back[...], NT, preferred_element_type=F32)

    for copy in back_x:
        copy.wait_recv()
    back = back_half[x].astype(F32)
    for o in range(3):
        back = back + back_in[o].astype(F32)
    back = back.astype(BF16)
    for s in range(4):
        features = dna_pooled[s * D_SLICE : (s + 1) * D_SLICE, :]
        part = lax.dot_general(back, features, NT, preferred_element_type=F32)
        for a in range(4):
            d_first[a, :, s * D_SLICE : (s + 1) * D_SLICE] = part[a * 16 : (a + 1) * 16, :]
    for s in range(8):

        @pl.when(jnp.logical_not(is_me(targets[s])))
        def _():
            ids_copy(s).wait_send()

    for copy in taken:
        copy.wait_send()


def sum_kernel(
    d_first,
    m_acc,
    d_out,
    m_all,
    m_sib,
    m_first,
    m_first_in,
    m_second,
    m_second_in,
    d_first_in,
    third,
    third_in,
    third_all,
    d_slab,
    d_fin,
    send_sems,
    recv_sems,
):
    blk, mp, z, y, x, core = place()
    sibling = device_at(z, y, x, 1 - core)
    ring = [device_at(z, y, lax.rem(x + o, 4), core) for o in range(4)]
    cross = [device_at(z, y, lax.rem(x + o, 4), 1 - core) for o in range(4)]
    along_y = [device_at(z, lax.rem(y + o, 4), x, core) for o in range(4)]
    along_z = [device_at(lax.rem(z + o, 8), y, x, core) for o in range(8)]
    other = 1 - core
    taken = []

    def post(src, dst, device):
        n = len(taken)
        copy = send(src, dst, send_sems.at[n], recv_sems.at[n], device)
        taken.append(copy)
        return copy

    for o in (1, 2, 3):
        signal(ring[o])
        signal(cross[o])
        signal(along_y[o])
    for o in range(1, 8):
        signal(along_z[o])
    signal(sibling)
    pl.semaphore_wait(pltpu.get_barrier_semaphore(), 17)

    m_swap = post(m_acc.at[pl.ds(pl.multiple_of(other * M_HALF, 8), M_HALF)], m_sib, sibling)
    m_swap.start()
    d_y = [post(d_first.at[lax.rem(y + o, 4)], d_first_in.at[o - 1], along_y[o]) for o in (1, 2, 3)]
    for copy in d_y:
        copy.start()


    swap = core == 1

    def pick(one, two):
        return tuple(jnp.where(swap, q, p) for p, q in zip(one, two))

    axis_a = [pick(p, q) for p, q in zip(ring, along_y)]
    axis_b = [pick(q, p) for p, q in zip(ring, along_y)]
    at_a = jnp.where(swap, y, x)
    at_b = jnp.where(swap, x, y)

    m_swap.wait_recv()

    def halve(i, carry):
        a, b = lax.div(i, 4), lax.rem(i, 4)
        row = jnp.where(swap, a * 96 + b * 24, b * 96 + a * 24)
        mine = m_acc[pl.ds(pl.multiple_of(core * M_HALF + row, 8), 24), :]
        m_first[a, b] = mine + m_sib[pl.ds(pl.multiple_of(row, 8), 24), :]
        return carry

    lax.fori_loop(0, 16, halve, 0)
    m_a = [post(m_first.at[lax.rem(at_a + o, 4)], m_first_in.at[o - 1], axis_a[o]) for o in (1, 2, 3)]
    for copy in m_a:
        copy.start()

    for copy in m_a:
        copy.wait_recv()
    for b in range(4):
        part = m_first[at_a, b]
        for o in range(3):
            part = part + m_first_in[o, b]
        m_second[b] = part
    m_b = [post(m_second.at[lax.rem(at_b + o, 4)], m_second_in.at[o - 1], axis_b[o]) for o in (1, 2, 3)]
    for copy in m_b:
        copy.start()

    for copy in d_y:
        copy.wait_recv()
    d_sum = d_first[y]
    for o in range(3):
        d_sum = d_sum + d_first_in[o]
    for s in range(8):
        lanes = slice(s * 128, (s + 1) * 128)
        third[s, 8:16, 0:128] = d_sum[0:8, lanes]
        third[s, 8:16, 128:256] = d_sum[8:16, lanes]
    for copy in m_b:
        copy.wait_recv()
    m_sum = m_second[at_b]
    for o in range(3):
        m_sum = m_sum + m_second_in[o]
    for s in range(6):
        third[s, 0:8, :] = m_sum[s // 2 * 8 : s // 2 * 8 + 8, s % 2 * 256 : s % 2 * 256 + 256]
    third[6, 0:8, :] = jnp.zeros((8, 256), F32)
    third[7, 0:8, :] = jnp.zeros((8, 256), F32)

    z_sum = [post(third.at[lax.rem(z + o, 8)], third_in.at[o - 1], along_z[o]) for o in range(1, 8)]
    for copy in z_sum:
        copy.start()
    for copy in z_sum:
        copy.wait_recv()
    total = third[z]
    for o in range(7):
        total = total + third_in[o]
    third_all[z] = total
    z_back = [post(third_all.at[z], third_all.at[z], along_z[o]) for o in range(1, 8)]
    for copy in z_back:
        copy.start()
    for copy in z_back:
        copy.wait_recv()

    for s in range(8):
        lanes = slice(s * 128, (s + 1) * 128)
        d_slab[y, 0:8, lanes] = third_all[s, 8:16, 0:128]
        d_slab[y, 8:16, lanes] = third_all[s, 8:16, 128:256]
    d_back = [post(d_slab.at[y], d_slab.at[y], along_y[o]) for o in (1, 2, 3)]
    for copy in d_back:
        copy.start()
    sub = core * M_HALF + y * 96 + x * 24
    for s in range(6):
        rows = pl.ds(pl.multiple_of(sub + s // 2 * 8, 8), 8)
        m_all[rows, s % 2 * 256 : s % 2 * 256 + 256] = third_all[s, 0:8, :]
    piece = m_all.at[pl.ds(pl.multiple_of(sub, 8), 24)]
    m_back_x = [post(piece, piece, ring[o]) for o in (1, 2, 3)]
    for copy in m_back_x:
        copy.start()

    def band(y_of, low, rows):
        first = core * M_HALF + lax.rem(y_of, 4) * 96 + low
        return m_all.at[pl.ds(pl.multiple_of(first, 8), rows)]

    def to(part, device):
        copy = post(part, part, device)
        copy.start()
        return copy

    for copy in m_back_x:
        copy.wait_recv()
    own_band = band(y, 0, 96)
    up_copy = to(own_band, along_y[1])
    down_copy = to(own_band, along_y[3])
    m_last = [to(own_band, sibling)]

    for copy in d_back:
        copy.wait_recv()
    eighth = core * 4 + x

    def slice_for(device):
        return d_slab.at[:, :, pl.ds(pl.multiple_of(device[1] * D_SLICE, 128), D_SLICE)]

    d_ring = [post(slice_for(device), d_fin.at[eighth], device) for device in ring[1:] + cross[1:] + [sibling]]
    for copy in d_ring:
        copy.start()
    own_lanes = pl.ds(pl.multiple_of(mp * D_SLICE, 128), D_SLICE)
    d_fin[eighth] = d_slab[:, :, own_lanes]

    up_copy.wait_recv()
    relay_up = to(band(y + 3, 0, 48), along_y[1])
    m_last.append(to(band(y + 3, 0, 96), sibling))
    down_copy.wait_recv()
    relay_down = to(band(y + 1, 48, 48), along_y[3])
    m_last.append(to(band(y + 1, 0, 96), sibling))

    for copy in d_ring:
        copy.wait_recv()
    d_out[...] = d_fin[...].reshape(E, D_SLICE)
    relay_up.wait_recv()
    relay_down.wait_recv()
    m_last.append(to(band(y + 2, 0, 96), sibling))
    for copy in m_last:
        copy.wait_recv()

    for copy in taken:
        copy.wait_send()


def sum_call(*args):
    vmem = pl.BlockSpec(memory_space=pltpu.VMEM)
    dma = pltpu.SemaphoreType.DMA
    f32 = lambda *shape: pltpu.VMEM(shape, F32)
    return pl.pallas_call(
        sum_kernel,
        out_shape=(
            jax.ShapeDtypeStruct((E, D_SLICE), F32),
            jax.ShapeDtypeStruct((D_METH, E), F32),
        ),
        in_specs=[vmem, vmem],
        out_specs=(vmem, vmem),
        scratch_shapes=[
            f32(M_HALF, E),
            f32(4, 4, 24, E),
            f32(3, 4, 24, E),
            f32(4, 24, E),
            f32(3, 24, E),
            f32(3, 16, 4 * D_SLICE),
            f32(8, 16, 256),
            f32(7, 16, 256),
            f32(8, 16, 256),
            f32(4, 16, 4 * D_SLICE),
            f32(8, 4, 16, D_SLICE),
            dma((N_COPIES,)),
            dma((N_COPIES,)),
        ],
        compiler_params=pltpu.CompilerParams(
            collective_id=1, has_side_effects=True, vmem_limit_bytes=20 * 1024 * 1024
        ),
        cost_estimate=pl.CostEstimate(flops=10**7, bytes_accessed=8 * 10**6, transcendentals=0),
        name="sum_heads",
    )(*args)


def step_call(*args):
    vmem = pl.BlockSpec(memory_space=pltpu.VMEM)
    smem = pl.BlockSpec(memory_space=pltpu.SMEM)
    hbm = pl.BlockSpec(memory_space=pl.ANY)
    dma = pltpu.SemaphoreType.DMA
    f32 = lambda *shape: pltpu.VMEM(shape, F32)
    bf16 = lambda *shape: pltpu.VMEM(shape, BF16)
    i32 = lambda *shape: pltpu.VMEM(shape, jnp.int32)
    return pl.pallas_call(
        step_kernel,
        out_shape=(
            jax.ShapeDtypeStruct((4, 16, 4 * D_SLICE), F32),
            jax.ShapeDtypeStruct((D_METH, E), F32),
        ),
        in_specs=[vmem, vmem, vmem, vmem, hbm, hbm, smem, smem],
        out_specs=(vmem, vmem),
        scratch_shapes=[
            bf16(VOCAB_METH, D_METH),
            bf16(D_METH, E),
            i32(16, COLS),
            i32(2, 3, 128),
            i32(ROWS, 128),
            bf16(4 * D_SLICE, ROWS),
            bf16(E, 4 * D_SLICE),
            bf16(D_METH, VOCAB_METH),
            bf16(E, D_METH),
            bf16(D_METH, COLS),
            f32(E, COLS),
            bf16(E, COLS),
            f32(1, COLS),
            f32(E, ROWS),
            f32(1, ROWS),
            bf16(E, ROWS),
            bf16(ROWS, E),
            f32(E, ROWS),
            bf16(ROWS, COLS),
            bf16(E, COLS),
            bf16(E, ROWS),
            bf16(256, ROWS),
            bf16(4, 64, ROWS),
            bf16(3, 64, ROWS),
            dma((8,)),
            dma((8,)),
            dma((N_COPIES,)),
            dma((N_COPIES,)),
            dma((4,)),
        ],
        compiler_params=pltpu.CompilerParams(
            collective_id=0, has_side_effects=True, vmem_limit_bytes=52 * 1024 * 1024
        ),
        cost_estimate=pl.CostEstimate(flops=17 * 10**9, bytes_accessed=4 * 10**6, transcendentals=5 * 10**6),
        name="pair_tiles",
    )(*args)


def hand_over_kernel(d_in, m_in, d_out, m_out):
    for s in range(E // 128):
        d_out[:, s * 128 : (s + 1) * 128] = d_in[s * 128 : (s + 1) * 128, :].T
    m_out[...] = m_in[...]


def hand_over(d_part, m_part):
    vmem = pl.BlockSpec(memory_space=pltpu.VMEM)
    return pl.pallas_call(
        hand_over_kernel,
        out_shape=(
            jax.ShapeDtypeStruct((D_SLICE, E), F32),
            jax.ShapeDtypeStruct((D_METH, E), F32),
        ),
        in_specs=[vmem, vmem],
        out_specs=(vmem, vmem),
        compiler_params=pltpu.CompilerParams(vmem_limit_bytes=8 * 1024 * 1024),
        name="hand_over",
    )(d_part, m_part)


def per_device(
    dna_ids,
    meth_ids,
    pair_index,
    dna_table,
    meth_table,
    dna_proj,
    meth_proj,
    logit_scale,
    logit_bias,
):
    dna_part, projt_part = pool_call(dna_ids.T, dna_table, dna_proj)
    d_part, m_part = step_call(
        dna_part,
        projt_part,
        meth_ids.T,
        pair_index.reshape(3, 128),
        meth_table,
        meth_proj,
        logit_scale,
        logit_bias,
    )
    return hand_over(*sum_call(d_part, m_part))


def solution(mesh):
    placed = (
        P("blk", None),
        P("blk", None),
        P("blk"),
        P(None, "mp"),
        P(),
        P("mp", None),
        P(),
        P(),
        P(),
    )
    return jax.shard_map(
        per_device, mesh=mesh, in_specs=placed, out_specs=(P("mp", None), P()), check_vma=False
    )
```

```python
import jax
import jax.numpy as jnp
from jax import lax
from jax.experimental import pallas as pl
from jax.experimental.pallas import tpu as pltpu
from jax.sharding import PartitionSpec as P

MESH = pl.DeviceIdType.MESH
F32 = jnp.float32
BF16 = jnp.bfloat16
EPS = 1e-06

PAIR_DEV = 384
ROWS = 2 * PAIR_DEV
COLS = 8 * PAIR_DEV
E = 512
D_SLICE = 256
D_METH = 768
VOCAB_DNA = 4096
VOCAB_METH = 512
CHUNK = 1536
PART = 512
LOG2E = 1.4426950408889634
E_HALF = 256
N_COPIES = 80

NT = (((1,), (1,)), ((), ()))


def place():
    blk, mp = lax.axis_index("blk"), lax.axis_index("mp")
    z = lax.div(blk, 8)
    y = lax.rem(lax.div(blk, 2), 4)
    x = lax.rem(blk, 2) * 2 + lax.div(mp, 2)
    return blk, mp, z, y, x, lax.rem(mp, 2)


def device_at(z, y, x, core):
    return (z * 8 + y * 2 + lax.div(x, 2), lax.rem(x, 2) * 2 + core)


def signal(device):
    pl.semaphore_signal(
        pltpu.get_barrier_semaphore(), inc=1, device_id=device, device_id_type=MESH
    )


def send(src, dst, send_sem, recv_sem, device):
    return pltpu.make_async_remote_copy(
        src_ref=src,
        dst_ref=dst,
        send_sem=send_sem,
        recv_sem=recv_sem,
        device_id=device,
        device_id_type=MESH,
    )


def step_kernel(
    dna_ids_hbm,
    meth_ids_hbm,
    pairs_hbm,
    dna_table_hbm,
    meth_table_hbm,
    dna_proj_hbm,
    meth_proj_hbm,
    scale_ref,
    bias_ref,
    d_out,
    m_out,
    dna_ids,
    meth_ids,
    pairs,
    dna_proj,
    dna_table,
    meth_table,
    meth_proj,
    dna_tokens,
    ids_all,
    pair_all,
    pair_wide,
    dna_pooled,
    dna_projt,
    meth_tablet,
    meth_projt,
    meth_pooled,
    meth_unit,
    meth_rows,
    meth_inv,
    dna_unit,
    dna_inv,
    dna_rowst,
    dna_rows,
    row_acc,
    tiles,
    m_give,
    m_keep,
    m_sib,
    m_first_in,
    m_second,
    m_second_in,
    m_third,
    m_third_in,
    m_z_all,
    back_all,
    back_sib,
    back_half,
    back_in,
    d_first,
    d_first_in,
    d_third,
    d_third_in,
    d_all,
    d_slab,
    m_all,
    d_fin,
    ids_send,
    ids_recv,
    send_sems,
    recv_sems,
    local_sems,
    write_sems,
):
    blk, mp, z, y, x, core = place()
    x_hi = lax.div(x, 2)
    sibling = device_at(z, y, x, 1 - core)
    ring = [device_at(z, y, lax.rem(x + o, 4), core) for o in range(4)]
    cross = [device_at(z, y, lax.rem(x + o, 4), 1 - core) for o in range(4)]
    along_y = [device_at(z, lax.rem(y + o, 4), x, core) for o in range(4)]
    along_z = [device_at(lax.rem(z + o, 8), y, x, core) for o in range(8)]
    slot = lax.rem(blk, 8)
    block = x_hi * 4 + mp
    taken = []

    def post(src, dst, device):
        n = len(taken)
        copy = send(src, dst, send_sems.at[n], recv_sems.at[n], device)
        taken.append(copy)
        return copy

    fetch = [
        pltpu.make_async_copy(src, dst, local_sems.at[1 + n])
        for n, (src, dst) in enumerate(
            (
                (dna_table_hbm, dna_table),
                (meth_table_hbm, meth_table),
                (meth_proj_hbm, meth_proj),
                (dna_ids_hbm, dna_ids),
                (meth_ids_hbm, meth_ids),
                (pairs_hbm, pairs),
                (dna_proj_hbm, dna_proj),
            )
        )
    ]
    for n in (4, 5, 6, 3, 0, 1, 2):
        fetch[n].start()

    targets = [device_at(s, mp, lax.div(z, 2), lax.rem(z, 2)) for s in range(8)]
    sources = [device_at(block, s // 2, (s % 2) * 2 + lax.div(y, 2), lax.rem(y, 2)) for s in range(8)]

    def is_me(device):
        return jnp.logical_and(device[0] == blk, device[1] == mp)

    for s in range(8):

        @pl.when(jnp.logical_not(is_me(sources[s])))
        def _():
            signal(sources[s])

    for o in (1, 2, 3):
        signal(ring[o])
        signal(cross[o])
        signal(along_y[o])
    for o in range(1, 8):
        signal(along_z[o])
    signal(sibling)
    for n in (3, 4, 5, 6):
        fetch[n].wait()
    to_self = jnp.logical_and(mp == y, block == z).astype(jnp.int32)
    pl.semaphore_wait(pltpu.get_barrier_semaphore(), 25 - to_self)

    def ids_copy(s):
        lanes = pl.ds(pl.multiple_of(slot * PAIR_DEV, 128), PAIR_DEV)
        return send(meth_ids, ids_all.at[:, lanes], ids_send.at[s], ids_recv.at[slot], targets[s])

    def ids_arrival(s):
        lanes = pl.ds(s * PAIR_DEV, PAIR_DEV)
        return send(meth_ids, ids_all.at[:, lanes], ids_send.at[s], ids_recv.at[s], sources[s])

    for s in range(8):

        @pl.when(jnp.logical_not(is_me(targets[s])))
        def _():
            ids_copy(s).start()

        @pl.when(is_me(targets[s]))
        def _():
            lanes = pl.ds(pl.multiple_of(slot * PAIR_DEV, 128), PAIR_DEV)
            local = pltpu.make_async_copy(meth_ids, ids_all.at[:, lanes], local_sems.at[0])
            local.start()
            local.wait()

    pair_copy = post(pairs, pair_all.at[x_hi], ring[2])
    pair_copy.start()
    pair_all[x_hi] = pairs[...]

    dna_projt[:, pl.ds(pl.multiple_of(mp * D_SLICE, 128), D_SLICE)] = dna_proj[...].T
    toward = 1 + 2 * core
    far = device_at(z, y, lax.rem(x + toward, 4), core)
    other_mp = lax.rem(mp + 2, 4)

    def quarter(of):
        return dna_projt.at[:, pl.ds(pl.multiple_of(of * D_SLICE, 128), D_SLICE)]

    proj_far = post(quarter(mp), quarter(mp), far)
    proj_sib = post(quarter(mp), quarter(mp), sibling)
    proj_fwd = post(quarter(other_mp), quarter(other_mp), sibling)
    proj_far.start()
    proj_sib.start()

    dna_tokens[...] = dna_ids[...].T

    def count_dna(i, carry):
        rows = pl.ds(pl.multiple_of(i * 16, 16), 16)
        ids = dna_tokens[rows, :]
        place_of = jnp.bitwise_and(ids, VOCAB_DNA // 4 - 1)
        amount = jnp.left_shift(1, jnp.right_shift(ids, 10) * 8)
        lane = lax.broadcasted_iota(jnp.int32, (16, VOCAB_DNA // 4), 1)
        total = jnp.zeros((16, VOCAB_DNA // 4), jnp.int32)
        for t in range(16):
            total = total + jnp.where(lane == place_of[:, t : t + 1], amount[:, t : t + 1], 0)
        for f in range(4):
            field = jnp.bitwise_and(jnp.right_shift(total, 8 * f), 255)
            field = field.astype(F32).astype(BF16)
            if f < 3:
                tiles[rows, f * 1024 : (f + 1) * 1024] = field
            else:
                tiles[pl.ds(pl.multiple_of(PAIR_DEV + i * 16, 16), 16), 0:1024] = field
        return carry

    lax.fori_loop(0, PAIR_DEV // 16, count_dna, 0)
    fetch[0].wait()
    pooled = jnp.dot(tiles[0:PAIR_DEV, :], dna_table[0:COLS, :], preferred_element_type=F32)
    pooled = pooled + jnp.dot(
        tiles[PAIR_DEV:ROWS, 0 : VOCAB_DNA - COLS], dna_table[COLS:VOCAB_DNA, :], preferred_element_type=F32
    )
    pooled = pooled * 0.0625
    own_lanes = pl.ds(pl.multiple_of(x_hi * PAIR_DEV, 128), PAIR_DEV)
    dna_pooled[pl.ds(pl.multiple_of(mp * D_SLICE, 16), D_SLICE), own_lanes] = pooled.T.astype(BF16)

    def pool_block(x_of, core_of, low=0, count=D_SLICE):
        first = (lax.rem(x_of, 2) * 2 + core_of) * D_SLICE + low
        lanes = pl.ds(pl.multiple_of(lax.div(x_of, 2) * PAIR_DEV, 128), PAIR_DEV)
        return dna_pooled.at[pl.ds(pl.multiple_of(first, 16), count), lanes]

    own = pool_block(x, core)
    from_left = pool_block(lax.rem(x + 3, 4), core)
    from_right = pool_block(lax.rem(x + 1, 4), core)
    from_across = pool_block(lax.rem(x + 2, 4), core)
    pool_right = post(own, own, ring[1])
    pool_left = post(own, own, ring[3])
    pool_sib = post(own, own, sibling)
    pool_right.start()
    pool_left.start()
    pool_sib.start()
    half_left = pool_block(lax.rem(x + 3, 4), core, 0, 128)
    half_right = pool_block(lax.rem(x + 1, 4), core, 128, 128)
    relay_right = post(half_left, half_left, ring[1])
    relay_left = post(half_right, half_right, ring[3])
    pool_fwd = [post(part, part, sibling) for part in (from_left, from_right, from_across)]

    fetch[1].wait()
    fetch[2].wait()
    meth_tablet[...] = meth_table[...].T
    meth_projt[...] = meth_proj[...].T
    for s in range(8):

        @pl.when(jnp.logical_not(is_me(sources[s])))
        def _():
            ids_arrival(s).wait_recv()

    def count_meth(ids):
        place_of = jnp.bitwise_and(ids, 127)
        amount = jnp.left_shift(1, jnp.right_shift(ids, 7) * 8)
        row = lax.broadcasted_iota(jnp.int32, (128, 128), 0)
        total = jnp.zeros((128, 128), jnp.int32)
        for t in range(16):
            total = total + jnp.where(row == place_of[t : t + 1, :], amount[t : t + 1, :], 0)
        fields = [jnp.bitwise_and(jnp.right_shift(total, 8 * f), 255) for f in range(4)]
        return jnp.concatenate([field.astype(F32).astype(BF16) for field in fields], axis=0)

    def embed_meth(i, carry):
        for p in range(CHUNK // PART):
            first = pl.multiple_of(i * CHUNK + p * PART, 128)
            lanes = pl.ds(first, PART)
            ids = [ids_all[:, pl.ds(pl.multiple_of(first + 128 * g, 128), 128)] for g in range(PART // 128)]
            tokens = jnp.concatenate([count_meth(part) for part in ids], axis=1)
            pooled_m = jnp.dot(meth_tablet[...], tokens, preferred_element_type=F32)
            pooled_m = (pooled_m * 0.0625).astype(BF16)
            meth_pooled[:, lanes] = pooled_m
            raw = jnp.dot(meth_projt[...], pooled_m, preferred_element_type=F32)
            inverse = lax.rsqrt(jnp.sum(raw * raw, axis=0, keepdims=True) + EPS)
            unit = raw * inverse
            meth_inv[:, lanes] = inverse
            meth_unit[:, lanes] = unit
            meth_rows[:, lanes] = unit.astype(BF16)
        return carry

    half = COLS // CHUNK // 2
    lax.fori_loop(0, half, embed_meth, 0)
    pool_right.wait_recv()
    relay_right.start()
    pool_left.wait_recv()
    relay_left.start()
    pool_fwd[0].start()
    pool_fwd[1].start()
    proj_far.wait_recv()
    proj_fwd.start()
    lax.fori_loop(half, 2 * half, embed_meth, 0)
    relay_right.wait_recv()
    relay_left.wait_recv()
    pool_fwd[2].start()
    proj_sib.wait_recv()
    proj_fwd.wait_recv()
    pair_copy.wait_recv()
    for h in range(2):
        words = pair_all[h]
        for a in range(3):
            wide = jnp.broadcast_to(words[a : a + 1, :], (128, 128))
            first = h * PAIR_DEV + a * 128
            pair_wide[first : first + 128, :] = wide.T
    pool_sib.wait_recv()
    for copy in pool_fwd:
        copy.wait_recv()

    raw = jnp.dot(dna_projt[...], dna_pooled[...], preferred_element_type=F32)
    inverse = lax.rsqrt(jnp.sum(raw * raw, axis=0, keepdims=True) + EPS)
    unit = raw * inverse
    dna_inv[...] = inverse
    dna_unit[...] = unit
    unit_low = unit.astype(BF16)
    dna_rowst[...] = unit_low
    dna_rows[...] = unit_low.T

    scale = scale_ref[0]
    bias = bias_ref[0]
    slope, offset = scale * -LOG2E, bias * -LOG2E
    first_col = block * COLS

    def pair_tile(i, carry):
        first = pl.multiple_of(i * CHUNK, 128)
        partner = pair_wide[...] - (first_col + first)
        parts = []
        for p in range(CHUNK // PART):
            rows_m = meth_rows[:, pl.ds(pl.multiple_of(first + p * PART, 128), PART)]
            dots = jnp.dot(dna_rows[...], rows_m, preferred_element_type=F32)
            lower = 1.0 + jnp.exp2(slope * dots + offset)
            prob = pl.reciprocal(lower, approx=True)
            prob = prob * (2.0 - lower * prob)
            for g in range(PART // 128):
                part = prob[:, g * 128 : (g + 1) * 128]
                lane = lax.broadcasted_iota(jnp.int32, (ROWS, 128), 1) + (p * PART + g * 128)
                parts.append(jnp.where(partner == lane, part - 1.0, part).astype(BF16))
        tile = jnp.concatenate(parts, axis=1)
        tiles[:, pl.ds(first, CHUNK)] = tile
        return carry

    lax.fori_loop(0, COLS // CHUNK, pair_tile, 0)

    row_acc[...] = lax.dot_general(meth_rows[...], tiles[...], NT, preferred_element_type=F32)

    other = 1 - core
    up = scale * row_acc[...]
    inner = jnp.sum(dna_unit[...] * up, axis=0, keepdims=True)
    back_all[...] = (dna_inv[...] * (up - dna_unit[...] * inner)).astype(BF16)
    back_swap = post(back_all.at[pl.ds(pl.multiple_of(other * 256, 16), 256)], back_sib, sibling)
    back_swap.start()

    def col_tile(i, carry):
        first = pl.multiple_of(i * CHUNK, 128)
        for p in range(CHUNK // PART):
            lanes = pl.ds(pl.multiple_of(first + p * PART, 128), PART)
            up = scale * jnp.dot(dna_rowst[...], tiles[:, lanes], preferred_element_type=F32)
            unit_m = meth_unit[:, lanes]
            inner = jnp.sum(unit_m * up, axis=0, keepdims=True)
            meth_rows[:, lanes] = (meth_inv[:, lanes] * (up - unit_m * inner)).astype(BF16)
        return carry

    lax.fori_loop(0, half, col_tile, 0)
    back_swap.wait_recv()
    for a in range(4):
        rows = pl.ds(pl.multiple_of(core * 256 + a * 64, 16), 64)
        both = back_all[rows, :].astype(F32) + back_sib[a * 64 : (a + 1) * 64, :].astype(F32)
        back_half[a] = both.astype(BF16)
    back_x = [post(back_half.at[lax.rem(x + o, 4)], back_in.at[o - 1], ring[o]) for o in (1, 2, 3)]
    for copy in back_x:
        copy.start()
    lax.fori_loop(half, 2 * half, col_tile, 0)

    for copy in back_x:
        copy.wait_recv()
    back = back_half[x].astype(F32)
    for o in range(3):
        back = back + back_in[o].astype(F32)
    back = back.astype(BF16)
    for s in range(4):
        features = dna_pooled[s * D_SLICE : (s + 1) * D_SLICE, :]
        part = lax.dot_general(back, features, NT, preferred_element_type=F32)
        for a in range(4):
            d_first[a, :, s * D_SLICE : (s + 1) * D_SLICE] = part[a * 16 : (a + 1) * 16, :]
    d_y = [post(d_first.at[lax.rem(y + o, 4)], d_first_in.at[o - 1], along_y[o]) for o in (1, 2, 3)]
    for copy in d_y:
        copy.start()

    def half_head(which):
        rows = pl.ds(pl.multiple_of(which * E_HALF, 16), E_HALF)
        return lax.dot_general(meth_rows[rows, :], meth_pooled[...], NT, preferred_element_type=F32)

    m_give[...] = half_head(other)
    m_swap = post(m_give, m_sib, sibling)
    m_swap.start()
    m_keep[...] = half_head(core)

    for copy in d_y:
        copy.wait_recv()
    d_sum = d_first[y]
    for o in range(3):
        d_sum = d_sum + d_first_in[o]
    for s in range(8):
        d_third[s] = d_sum[:, s * 128 : (s + 1) * 128]
    d_z = [post(d_third.at[lax.rem(z + o, 8)], d_third_in.at[o - 1], along_z[o]) for o in range(1, 8)]
    for copy in d_z:
        copy.start()

    swap = core == 1

    def pick(one, two):
        return tuple(jnp.where(swap, q, p) for p, q in zip(one, two))

    axis_a = [pick(p, q) for p, q in zip(ring, along_y)]
    axis_b = [pick(q, p) for p, q in zip(ring, along_y)]
    at_a = jnp.where(swap, y, x)
    at_b = jnp.where(swap, x, y)

    def band(of, rows=64):
        return pl.ds(pl.multiple_of(of * rows, 16), rows)

    m_swap.wait_recv()
    m_keep[...] = m_keep[...] + m_sib[...]
    m_a = [post(m_keep.at[band(lax.rem(at_a + o, 4))], m_first_in.at[o - 1], axis_a[o]) for o in (1, 2, 3)]
    for copy in m_a:
        copy.start()

    for copy in d_z:
        copy.wait_recv()
    total = d_third[z]
    for o in range(7):
        total = total + d_third_in[o]
    d_all[z] = total
    d_z_back = [post(d_all.at[z], d_all.at[z], along_z[o]) for o in range(1, 8)]
    for copy in d_z_back:
        copy.start()

    for copy in m_a:
        copy.wait_recv()
    part = m_keep[band(at_a), :]
    for o in range(3):
        part = part + m_first_in[o]
    for b in range(4):
        m_second[b] = part[b * 16 : (b + 1) * 16, :]
    m_b = [post(m_second.at[lax.rem(at_b + o, 4)], m_second_in.at[o - 1], axis_b[o]) for o in (1, 2, 3)]
    for copy in m_b:
        copy.start()

    for copy in d_z_back:
        copy.wait_recv()
    for s in range(8):
        d_slab[y, :, s * 128 : (s + 1) * 128] = d_all[s]
    d_back = [post(d_slab.at[y], d_slab.at[y], along_y[o]) for o in (1, 2, 3)]
    for copy in d_back:
        copy.start()

    for copy in m_b:
        copy.wait_recv()
    m_sum = m_second[at_b]
    for o in range(3):
        m_sum = m_sum + m_second_in[o]
    for s in range(6):
        m_third[s] = m_sum[:, s * 128 : (s + 1) * 128]
    m_third[6] = jnp.zeros((16, 128), F32)
    m_third[7] = jnp.zeros((16, 128), F32)
    m_z = [post(m_third.at[lax.rem(z + o, 8)], m_third_in.at[o - 1], along_z[o]) for o in range(1, 8)]
    for copy in m_z:
        copy.start()

    for copy in d_back:
        copy.wait_recv()
    eighth = core * 4 + x

    def slice_for(device):
        return d_slab.at[:, :, pl.ds(pl.multiple_of(device[1] * D_SLICE, 128), D_SLICE)]

    d_ring = [post(slice_for(device), d_fin.at[eighth], device) for device in ring[1:] + cross[1:] + [sibling]]
    for copy in d_ring:
        copy.start()
    d_fin[eighth] = d_slab[:, :, pl.ds(pl.multiple_of(mp * D_SLICE, 128), D_SLICE)]

    for copy in m_z:
        copy.wait_recv()
    total = m_third[z]
    for o in range(7):
        total = total + m_third_in[o]
    m_z_all[z] = total
    m_z_back = [post(m_z_all.at[z], m_z_all.at[z], along_z[o]) for o in range(1, 8)]
    for copy in m_z_back:
        copy.start()
    for copy in m_z_back:
        copy.wait_recv()

    def rows_at(a, low, rows):
        return m_all.at[pl.ds(pl.multiple_of(core * E_HALF + lax.rem(a, 4) * 64 + low, 16), rows)]

    def to(part, device):
        copy = post(part, part, device)
        copy.start()
        return copy

    sub = pl.ds(pl.multiple_of(core * E_HALF + at_a * 64 + at_b * 16, 16), 16)
    for s in range(6):
        m_all[sub, s * 128 : (s + 1) * 128] = m_z_all[s]
    m_back_b = [to(m_all.at[sub], axis_b[o]) for o in (1, 2, 3)]
    for copy in m_back_b:
        copy.wait_recv()
    own_band = rows_at(at_a, 0, 64)
    up_copy = to(own_band, axis_a[1])
    down_copy = to(own_band, axis_a[3])
    m_last = [to(own_band, sibling)]
    up_copy.wait_recv()
    relay_up = to(rows_at(at_a + 3, 0, 32), axis_a[1])
    m_last.append(to(rows_at(at_a + 3, 0, 64), sibling))
    down_copy.wait_recv()
    relay_down = to(rows_at(at_a + 1, 32, 32), axis_a[3])
    m_last.append(to(rows_at(at_a + 1, 0, 64), sibling))
    written = []

    def write(src, dst):
        copy = pltpu.make_async_copy(src, dst, write_sems.at[len(written)])
        copy.start()
        written.append(copy)

    def write_band(of, half):
        rows = pl.ds(pl.multiple_of(half * E_HALF + lax.rem(of, 4) * 64, 16), 64)
        write(m_all.at[rows], m_out.at[rows])

    for o in (0, 3, 1):
        write_band(at_a + o, core)
    for copy in d_ring:
        copy.wait_recv()
    write(d_fin, d_out)
    relay_up.wait_recv()
    relay_down.wait_recv()
    m_last.append(to(rows_at(at_a + 2, 0, 64), sibling))
    write_band(at_a + 2, core)
    sib_a = jnp.where(swap, x, y)
    for copy, o in zip(m_last, (0, 3, 1, 2)):
        copy.wait_recv()
        write_band(sib_a + o, other)
    for copy in written:
        copy.wait()

    for s in range(8):

        @pl.when(jnp.logical_not(is_me(targets[s])))
        def _():
            ids_copy(s).wait_send()

    for copy in taken:
        copy.wait_send()


def step_call(*args):
    vmem = pl.BlockSpec(memory_space=pltpu.VMEM)
    smem = pl.BlockSpec(memory_space=pltpu.SMEM)
    hbm = pl.BlockSpec(memory_space=pltpu.HBM)
    dma = pltpu.SemaphoreType.DMA
    f32 = lambda *shape: pltpu.VMEM(shape, F32)
    bf16 = lambda *shape: pltpu.VMEM(shape, BF16)
    i32 = lambda *shape: pltpu.VMEM(shape, jnp.int32)
    return pl.pallas_call(
        step_kernel,
        out_shape=(
            jax.ShapeDtypeStruct((8, 4, 16, D_SLICE), F32),
            jax.ShapeDtypeStruct((E, D_METH), F32),
        ),
        in_specs=[hbm] * 7 + [smem] * 2,
        out_specs=(hbm, hbm),
        scratch_shapes=[
            i32(16, PAIR_DEV),
            i32(16, PAIR_DEV),
            i32(3, 128),
            bf16(D_SLICE, E),
            bf16(VOCAB_DNA, D_SLICE),
            bf16(VOCAB_METH, D_METH),
            bf16(D_METH, E),
            i32(PAIR_DEV, 16),
            i32(16, COLS),
            i32(2, 3, 128),
            i32(ROWS, 128),
            bf16(4 * D_SLICE, ROWS),
            bf16(E, 4 * D_SLICE),
            bf16(D_METH, VOCAB_METH),
            bf16(E, D_METH),
            bf16(D_METH, COLS),
            f32(E, COLS),
            bf16(E, COLS),
            f32(1, COLS),
            f32(E, ROWS),
            f32(1, ROWS),
            bf16(E, ROWS),
            bf16(ROWS, E),
            f32(E, ROWS),
            bf16(ROWS, COLS),
            f32(E_HALF, D_METH),
            f32(E_HALF, D_METH),
            f32(E_HALF, D_METH),
            f32(3, 64, D_METH),
            f32(4, 16, D_METH),
            f32(3, 16, D_METH),
            f32(8, 16, 128),
            f32(7, 16, 128),
            f32(8, 16, 128),
            bf16(E, ROWS),
            bf16(256, ROWS),
            bf16(4, 64, ROWS),
            bf16(3, 64, ROWS),
            f32(4, 16, 4 * D_SLICE),
            f32(3, 16, 4 * D_SLICE),
            f32(8, 16, 128),
            f32(7, 16, 128),
            f32(8, 16, 128),
            f32(4, 16, 4 * D_SLICE),
            f32(E, D_METH),
            f32(8, 4, 16, D_SLICE),
            dma((8,)),
            dma((8,)),
            dma((N_COPIES,)),
            dma((N_COPIES,)),
            dma((8,)),
            dma((9,)),
        ],
        compiler_params=pltpu.CompilerParams(
            collective_id=0, has_side_effects=True, vmem_limit_bytes=56 * 1024 * 1024
        ),
        cost_estimate=pl.CostEstimate(flops=19 * 10**9, bytes_accessed=8 * 10**6, transcendentals=5 * 10**6),
        name="contrastive_step",
    )(*args)


def hand_over_kernel(d_in, m_in, d_out, m_out, d_here, m_here, d_turned, m_turned, in_sems, out_sems):
    bands = [slice(s * 128, (s + 1) * 128) for s in range(E // 128)]
    pairs = [(m_in, m_here, m_turned, m_out), (d_in, d_here, d_turned, d_out)]
    parts = [(rows, pair) for pair in pairs for rows in bands]
    fetch = [
        pltpu.make_async_copy(src.at[rows], here.at[rows], in_sems.at[n])
        for n, (rows, (src, here, turned, dst)) in enumerate(parts)
    ]
    store = [
        pltpu.make_async_copy(turned.at[:, rows], dst.at[:, rows], out_sems.at[n])
        for n, (rows, (src, here, turned, dst)) in enumerate(parts)
    ]
    for copy in fetch:
        copy.start()
    for n, (rows, (src, here, turned, dst)) in enumerate(parts):
        fetch[n].wait()
        turned[:, rows] = here[rows, :].T
        store[n].start()
    for copy in store:
        copy.wait()


def hand_over(d_part, m_part):
    hbm = pl.BlockSpec(memory_space=pltpu.HBM)
    return pl.pallas_call(
        hand_over_kernel,
        out_shape=(
            jax.ShapeDtypeStruct((D_SLICE, E), F32),
            jax.ShapeDtypeStruct((D_METH, E), F32),
        ),
        in_specs=[hbm, hbm],
        out_specs=(hbm, hbm),
        scratch_shapes=[
            pltpu.VMEM((E, D_SLICE), F32),
            pltpu.VMEM((E, D_METH), F32),
            pltpu.VMEM((D_SLICE, E), F32),
            pltpu.VMEM((D_METH, E), F32),
            pltpu.SemaphoreType.DMA((8,)),
            pltpu.SemaphoreType.DMA((8,)),
        ],
        compiler_params=pltpu.CompilerParams(vmem_limit_bytes=56 * 1024 * 1024),
        name="hand_over",
    )(d_part, m_part)


def per_device(
    dna_ids,
    meth_ids,
    pair_index,
    dna_table,
    meth_table,
    dna_proj,
    meth_proj,
    logit_scale,
    logit_bias,
):
    d_part, m_part = step_call(
        dna_ids.T,
        meth_ids.T,
        pair_index.reshape(3, 128),
        dna_table,
        meth_table,
        dna_proj,
        meth_proj,
        logit_scale,
        logit_bias,
    )
    return hand_over(d_part.reshape(E, D_SLICE), m_part)


def solution(mesh):
    placed = (
        P("blk", None),
        P("blk", None),
        P("blk"),
        P(None, "mp"),
        P(),
        P("mp", None),
        P(),
        P(),
        P(),
    )
    return jax.shard_map(
        per_device, mesh=mesh, in_specs=placed, out_specs=(P("mp", None), P()), check_vma=False
    )
```

```python
import jax
import jax.numpy as jnp
from jax import lax
from jax.experimental import pallas as pl
from jax.experimental.pallas import tpu as pltpu
from jax.sharding import PartitionSpec as P

MESH = pl.DeviceIdType.MESH
F32 = jnp.float32
BF16 = jnp.bfloat16
EPS = 1e-06

PAIR_DEV = 384
ROWS = 2 * PAIR_DEV
COLS = 8 * PAIR_DEV
E = 512
D_SLICE = 256
D_METH = 768
VOCAB_DNA = 4096
VOCAB_METH = 512
CHUNK = 1536
PART = 512
LOG2E = 1.4426950408889634
E_HALF = 256
N_COPIES = 80

NT = (((1,), (1,)), ((), ()))


def place():
    blk, mp = lax.axis_index("blk"), lax.axis_index("mp")
    z = lax.div(blk, 8)
    y = lax.rem(lax.div(blk, 2), 4)
    x = lax.rem(blk, 2) * 2 + lax.div(mp, 2)
    return blk, mp, z, y, x, lax.rem(mp, 2)


def device_at(z, y, x, core):
    return (z * 8 + y * 2 + lax.div(x, 2), lax.rem(x, 2) * 2 + core)


def signal(device):
    pl.semaphore_signal(
        pltpu.get_barrier_semaphore(), inc=1, device_id=device, device_id_type=MESH
    )


def send(src, dst, send_sem, recv_sem, device):
    return pltpu.make_async_remote_copy(
        src_ref=src,
        dst_ref=dst,
        send_sem=send_sem,
        recv_sem=recv_sem,
        device_id=device,
        device_id_type=MESH,
    )


def step_kernel(
    dna_ids_hbm,
    meth_ids_hbm,
    pairs_hbm,
    dna_table_hbm,
    meth_table_hbm,
    dna_proj_hbm,
    meth_proj_hbm,
    scale_ref,
    bias_ref,
    d_out,
    m_out,
    dna_ids,
    meth_ids,
    pairs,
    dna_proj,
    dna_table,
    meth_table,
    meth_proj,
    dna_tokens,
    ids_all,
    pair_all,
    pair_wide,
    dna_pooled,
    dna_projt,
    meth_tablet,
    meth_projt,
    meth_pooled,
    meth_unit,
    meth_rows,
    meth_inv,
    dna_unit,
    dna_inv,
    dna_rowst,
    dna_rows,
    row_acc,
    tiles,
    m_give,
    m_low,
    m_keep,
    m_sib,
    m_first_in,
    m_second,
    m_second_in,
    m_third,
    m_third_in,
    m_z_all,
    back_all,
    back_sib,
    back_half,
    back_in,
    d_first,
    d_first_low,
    d_first_in,
    d_third,
    d_third_in,
    d_all,
    d_slab,
    m_all,
    d_fin,
    ids_send,
    ids_recv,
    send_sems,
    recv_sems,
    local_sems,
    write_sems,
):
    blk, mp, z, y, x, core = place()
    x_hi = lax.div(x, 2)
    sibling = device_at(z, y, x, 1 - core)
    ring = [device_at(z, y, lax.rem(x + o, 4), core) for o in range(4)]
    cross = [device_at(z, y, lax.rem(x + o, 4), 1 - core) for o in range(4)]
    along_y = [device_at(z, lax.rem(y + o, 4), x, core) for o in range(4)]
    along_z = [device_at(lax.rem(z + o, 8), y, x, core) for o in range(8)]
    slot = lax.rem(blk, 8)
    block = x_hi * 4 + mp
    taken = []

    def post(src, dst, device):
        n = len(taken)
        copy = send(src, dst, send_sems.at[n], recv_sems.at[n], device)
        taken.append(copy)
        return copy

    fetch = [
        pltpu.make_async_copy(src, dst, local_sems.at[1 + n])
        for n, (src, dst) in enumerate(
            (
                (dna_table_hbm, dna_table),
                (meth_table_hbm, meth_table),
                (meth_proj_hbm, meth_proj),
                (dna_ids_hbm, dna_ids),
                (meth_ids_hbm, meth_ids),
                (pairs_hbm, pairs),
                (dna_proj_hbm, dna_proj),
            )
        )
    ]
    for n in (4, 5, 6, 3, 0, 1, 2):
        fetch[n].start()

    targets = [device_at(s, mp, lax.div(z, 2), lax.rem(z, 2)) for s in range(8)]
    sources = [device_at(block, s // 2, (s % 2) * 2 + lax.div(y, 2), lax.rem(y, 2)) for s in range(8)]

    def is_me(device):
        return jnp.logical_and(device[0] == blk, device[1] == mp)

    for s in range(8):

        @pl.when(jnp.logical_not(is_me(sources[s])))
        def _():
            signal(sources[s])

    for o in (1, 2, 3):
        signal(ring[o])
        signal(cross[o])
        signal(along_y[o])
    for o in range(1, 8):
        signal(along_z[o])
    signal(sibling)
    for n in (3, 4, 5, 6):
        fetch[n].wait()
    to_self = jnp.logical_and(mp == y, block == z).astype(jnp.int32)
    pl.semaphore_wait(pltpu.get_barrier_semaphore(), 25 - to_self)

    def ids_copy(s):
        lanes = pl.ds(pl.multiple_of(slot * PAIR_DEV, 128), PAIR_DEV)
        return send(meth_ids, ids_all.at[:, lanes], ids_send.at[s], ids_recv.at[slot], targets[s])

    def ids_arrival(s):
        lanes = pl.ds(s * PAIR_DEV, PAIR_DEV)
        return send(meth_ids, ids_all.at[:, lanes], ids_send.at[s], ids_recv.at[s], sources[s])

    for s in range(8):

        @pl.when(jnp.logical_not(is_me(targets[s])))
        def _():
            ids_copy(s).start()

        @pl.when(is_me(targets[s]))
        def _():
            lanes = pl.ds(pl.multiple_of(slot * PAIR_DEV, 128), PAIR_DEV)
            local = pltpu.make_async_copy(meth_ids, ids_all.at[:, lanes], local_sems.at[0])
            local.start()
            local.wait()

    pair_copy = post(pairs, pair_all.at[x_hi], ring[2])
    pair_copy.start()
    pair_all[x_hi] = pairs[...]

    dna_projt[:, pl.ds(pl.multiple_of(mp * D_SLICE, 128), D_SLICE)] = dna_proj[...].T
    toward = 1 + 2 * core
    far = device_at(z, y, lax.rem(x + toward, 4), core)
    other_mp = lax.rem(mp + 2, 4)

    def quarter(of):
        return dna_projt.at[:, pl.ds(pl.multiple_of(of * D_SLICE, 128), D_SLICE)]

    proj_far = post(quarter(mp), quarter(mp), far)
    proj_sib = post(quarter(mp), quarter(mp), sibling)
    proj_fwd = post(quarter(other_mp), quarter(other_mp), sibling)
    proj_far.start()
    proj_sib.start()

    dna_tokens[...] = dna_ids[...].T

    def count_dna(i, carry):
        rows = pl.ds(pl.multiple_of(i * 16, 16), 16)
        ids = dna_tokens[rows, :]
        place_of = jnp.bitwise_and(ids, VOCAB_DNA // 4 - 1)
        amount = jnp.left_shift(1, jnp.right_shift(ids, 10) * 8)
        lane = lax.broadcasted_iota(jnp.int32, (16, VOCAB_DNA // 4), 1)
        total = jnp.zeros((16, VOCAB_DNA // 4), jnp.int32)
        for t in range(16):
            total = total + jnp.where(lane == place_of[:, t : t + 1], amount[:, t : t + 1], 0)
        for f in range(4):
            field = jnp.bitwise_and(jnp.right_shift(total, 8 * f), 255)
            field = field.astype(F32).astype(BF16)
            if f < 3:
                tiles[rows, f * 1024 : (f + 1) * 1024] = field
            else:
                tiles[pl.ds(pl.multiple_of(PAIR_DEV + i * 16, 16), 16), 0:1024] = field
        return carry

    lax.fori_loop(0, PAIR_DEV // 16, count_dna, 0)
    fetch[0].wait()
    pooled = jnp.dot(tiles[0:PAIR_DEV, :], dna_table[0:COLS, :], preferred_element_type=F32)
    pooled = pooled + jnp.dot(
        tiles[PAIR_DEV:ROWS, 0 : VOCAB_DNA - COLS], dna_table[COLS:VOCAB_DNA, :], preferred_element_type=F32
    )
    pooled = pooled * 0.0625
    own_lanes = pl.ds(pl.multiple_of(x_hi * PAIR_DEV, 128), PAIR_DEV)
    dna_pooled[pl.ds(pl.multiple_of(mp * D_SLICE, 16), D_SLICE), own_lanes] = pooled.T.astype(BF16)

    def pool_block(x_of, core_of, low=0, count=D_SLICE):
        first = (lax.rem(x_of, 2) * 2 + core_of) * D_SLICE + low
        lanes = pl.ds(pl.multiple_of(lax.div(x_of, 2) * PAIR_DEV, 128), PAIR_DEV)
        return dna_pooled.at[pl.ds(pl.multiple_of(first, 16), count), lanes]

    own = pool_block(x, core)
    from_left = pool_block(lax.rem(x + 3, 4), core)
    from_right = pool_block(lax.rem(x + 1, 4), core)
    from_across = pool_block(lax.rem(x + 2, 4), core)
    pool_right = post(own, own, ring[1])
    pool_left = post(own, own, ring[3])
    pool_sib = post(own, own, sibling)
    pool_right.start()
    pool_left.start()
    pool_sib.start()
    half_left = pool_block(lax.rem(x + 3, 4), core, 0, 128)
    half_right = pool_block(lax.rem(x + 1, 4), core, 128, 128)
    relay_right = post(half_left, half_left, ring[1])
    relay_left = post(half_right, half_right, ring[3])
    pool_fwd = [post(part, part, sibling) for part in (from_left, from_right, from_across)]

    fetch[1].wait()
    fetch[2].wait()
    meth_tablet[...] = meth_table[...].T
    meth_projt[...] = meth_proj[...].T
    for s in range(8):

        @pl.when(jnp.logical_not(is_me(sources[s])))
        def _():
            ids_arrival(s).wait_recv()

    def count_meth(ids):
        place_of = jnp.bitwise_and(ids, 127)
        amount = jnp.left_shift(1, jnp.right_shift(ids, 7) * 8)
        row = lax.broadcasted_iota(jnp.int32, (128, 128), 0)
        total = jnp.zeros((128, 128), jnp.int32)
        for t in range(16):
            total = total + jnp.where(row == place_of[t : t + 1, :], amount[t : t + 1, :], 0)
        fields = [jnp.bitwise_and(jnp.right_shift(total, 8 * f), 255) for f in range(4)]
        return jnp.concatenate([field.astype(F32).astype(BF16) for field in fields], axis=0)

    def embed_meth(i, carry):
        for p in range(CHUNK // PART):
            first = pl.multiple_of(i * CHUNK + p * PART, 128)
            lanes = pl.ds(first, PART)
            ids = [ids_all[:, pl.ds(pl.multiple_of(first + 128 * g, 128), 128)] for g in range(PART // 128)]
            tokens = jnp.concatenate([count_meth(part) for part in ids], axis=1)
            pooled_m = jnp.dot(meth_tablet[...], tokens, preferred_element_type=F32)
            pooled_m = (pooled_m * 0.0625).astype(BF16)
            meth_pooled[:, lanes] = pooled_m
            raw = jnp.dot(meth_projt[...], pooled_m, preferred_element_type=F32)
            inverse = lax.rsqrt(jnp.sum(raw * raw, axis=0, keepdims=True) + EPS)
            unit = raw * inverse
            meth_inv[:, lanes] = inverse
            meth_unit[:, lanes] = unit
            meth_rows[:, lanes] = unit.astype(BF16)
        return carry

    half = COLS // CHUNK // 2
    lax.fori_loop(0, half, embed_meth, 0)
    pool_right.wait_recv()
    relay_right.start()
    pool_left.wait_recv()
    relay_left.start()
    pool_fwd[0].start()
    pool_fwd[1].start()
    proj_far.wait_recv()
    proj_fwd.start()
    lax.fori_loop(half, 2 * half, embed_meth, 0)
    relay_right.wait_recv()
    relay_left.wait_recv()
    pool_fwd[2].start()
    proj_sib.wait_recv()
    proj_fwd.wait_recv()
    pair_copy.wait_recv()
    for h in range(2):
        words = pair_all[h]
        for a in range(3):
            wide = jnp.broadcast_to(words[a : a + 1, :], (128, 128))
            first = h * PAIR_DEV + a * 128
            pair_wide[first : first + 128, :] = wide.T
    pool_sib.wait_recv()
    for copy in pool_fwd:
        copy.wait_recv()

    raw = jnp.dot(dna_projt[...], dna_pooled[...], preferred_element_type=F32)
    inverse = lax.rsqrt(jnp.sum(raw * raw, axis=0, keepdims=True) + EPS)
    unit = raw * inverse
    dna_inv[...] = inverse
    dna_unit[...] = unit
    unit_low = unit.astype(BF16)
    dna_rowst[...] = unit_low
    dna_rows[...] = unit_low.T

    scale = scale_ref[0]
    bias = bias_ref[0]
    slope, offset = scale * -LOG2E, bias * -LOG2E
    first_col = block * COLS

    def pair_tile(i, carry):
        first = pl.multiple_of(i * CHUNK, 128)
        partner = pair_wide[...] - (first_col + first)
        parts = []
        for p in range(CHUNK // PART):
            rows_m = meth_rows[:, pl.ds(pl.multiple_of(first + p * PART, 128), PART)]
            dots = jnp.dot(dna_rows[...], rows_m, preferred_element_type=F32)
            lower = 1.0 + jnp.exp2(slope * dots + offset)
            prob = pl.reciprocal(lower, approx=True)
            prob = prob * (2.0 - lower * prob)
            for g in range(PART // 128):
                part = prob[:, g * 128 : (g + 1) * 128]
                lane = lax.broadcasted_iota(jnp.int32, (ROWS, 128), 1) + (p * PART + g * 128)
                parts.append(jnp.where(partner == lane, part - 1.0, part).astype(BF16))
        tile = jnp.concatenate(parts, axis=1)
        tiles[:, pl.ds(first, CHUNK)] = tile
        return carry

    lax.fori_loop(0, COLS // CHUNK, pair_tile, 0)

    row_acc[...] = lax.dot_general(meth_rows[...], tiles[...], NT, preferred_element_type=F32)

    other = 1 - core
    up = scale * row_acc[...]
    inner = jnp.sum(dna_unit[...] * up, axis=0, keepdims=True)
    back_all[...] = (dna_inv[...] * (up - dna_unit[...] * inner)).astype(BF16)
    back_swap = post(back_all.at[pl.ds(pl.multiple_of(other * 256, 16), 256)], back_sib, sibling)
    back_swap.start()

    def col_tile(i, carry):
        first = pl.multiple_of(i * CHUNK, 128)
        for p in range(CHUNK // PART):
            lanes = pl.ds(pl.multiple_of(first + p * PART, 128), PART)
            up = scale * jnp.dot(dna_rowst[...], tiles[:, lanes], preferred_element_type=F32)
            unit_m = meth_unit[:, lanes]
            inner = jnp.sum(unit_m * up, axis=0, keepdims=True)
            meth_rows[:, lanes] = (meth_inv[:, lanes] * (up - unit_m * inner)).astype(BF16)
        return carry

    lax.fori_loop(0, half, col_tile, 0)
    back_swap.wait_recv()
    for a in range(4):
        rows = pl.ds(pl.multiple_of(core * 256 + a * 64, 16), 64)
        both = back_all[rows, :].astype(F32) + back_sib[a * 64 : (a + 1) * 64, :].astype(F32)
        back_half[a] = both.astype(BF16)
    back_x = [post(back_half.at[lax.rem(x + o, 4)], back_in.at[o - 1], ring[o]) for o in (1, 2, 3)]
    for copy in back_x:
        copy.start()
    lax.fori_loop(half, 2 * half, col_tile, 0)

    for copy in back_x:
        copy.wait_recv()
    back = back_half[x].astype(F32)
    for o in range(3):
        back = back + back_in[o].astype(F32)
    back = back.astype(BF16)
    for s in range(4):
        features = dna_pooled[s * D_SLICE : (s + 1) * D_SLICE, :]
        part = lax.dot_general(back, features, NT, preferred_element_type=F32)
        for a in range(4):
            d_first[a, :, s * D_SLICE : (s + 1) * D_SLICE] = part[a * 16 : (a + 1) * 16, :]
            d_first_low[a, :, s * D_SLICE : (s + 1) * D_SLICE] = part[a * 16 : (a + 1) * 16, :].astype(BF16)
    d_y = [post(d_first_low.at[lax.rem(y + o, 4)], d_first_in.at[o - 1], along_y[o]) for o in (1, 2, 3)]
    for copy in d_y:
        copy.start()

    def half_head(which):
        rows = pl.ds(pl.multiple_of(which * E_HALF, 16), E_HALF)
        return lax.dot_general(meth_pooled[...], meth_rows[rows, :], NT, preferred_element_type=F32)

    m_give[...] = half_head(other).astype(BF16)
    m_swap = post(m_give, m_sib, sibling)
    m_swap.start()
    m_keep[...] = half_head(core)

    for copy in d_y:
        copy.wait_recv()
    d_sum = d_first[y]
    for o in range(3):
        d_sum = d_sum + d_first_in[o].astype(F32)
    for s in range(8):
        d_third[s] = d_sum[:, s * 128 : (s + 1) * 128]
    d_z = [post(d_third.at[lax.rem(z + o, 8)], d_third_in.at[o - 1], along_z[o]) for o in range(1, 8)]
    for copy in d_z:
        copy.start()

    swap = core == 1

    def pick(one, two):
        return tuple(jnp.where(swap, q, p) for p, q in zip(one, two))

    axis_a = [pick(p, q) for p, q in zip(ring, along_y)]
    axis_b = [pick(q, p) for p, q in zip(ring, along_y)]
    at_a = jnp.where(swap, y, x)
    at_b = jnp.where(swap, x, y)

    def band(of, rows=192):
        return pl.ds(pl.multiple_of(of * rows, 16), rows)

    m_swap.wait_recv()
    both = m_keep[...] + m_sib[...].astype(F32)
    m_keep[...] = both
    m_low[...] = both.astype(BF16)
    m_a = [post(m_low.at[band(lax.rem(at_a + o, 4))], m_first_in.at[o - 1], axis_a[o]) for o in (1, 2, 3)]
    for copy in m_a:
        copy.start()

    for copy in d_z:
        copy.wait_recv()
    total = d_third[z]
    for o in range(7):
        total = total + d_third_in[o]
    d_all[z] = total
    d_z_back = [post(d_all.at[z], d_all.at[z], along_z[o]) for o in range(1, 8)]
    for copy in d_z_back:
        copy.start()

    for copy in m_a:
        copy.wait_recv()
    part = m_keep[band(at_a), :]
    for o in range(3):
        part = part + m_first_in[o].astype(F32)
    for b in range(4):
        m_second[b] = part[b * 48 : (b + 1) * 48, :]
    m_b = [post(m_second.at[lax.rem(at_b + o, 4)], m_second_in.at[o - 1], axis_b[o]) for o in (1, 2, 3)]
    for copy in m_b:
        copy.start()

    for copy in d_z_back:
        copy.wait_recv()
    for s in range(8):
        d_slab[y, :, s * 128 : (s + 1) * 128] = d_all[s]
    d_back = [post(d_slab.at[y], d_slab.at[y], along_y[o]) for o in (1, 2, 3)]
    for copy in d_back:
        copy.start()

    for copy in m_b:
        copy.wait_recv()
    m_sum = m_second[at_b]
    for o in range(3):
        m_sum = m_sum + m_second_in[o]
    for s in range(6):
        m_third[s] = m_sum[s // 2 * 16 : s // 2 * 16 + 16, s % 2 * 128 : s % 2 * 128 + 128]
    m_third[6] = jnp.zeros((16, 128), F32)
    m_third[7] = jnp.zeros((16, 128), F32)
    m_z = [post(m_third.at[lax.rem(z + o, 8)], m_third_in.at[o - 1], along_z[o]) for o in range(1, 8)]
    for copy in m_z:
        copy.start()

    for copy in d_back:
        copy.wait_recv()
    eighth = core * 4 + x

    def slice_for(device):
        return d_slab.at[:, :, pl.ds(pl.multiple_of(device[1] * D_SLICE, 128), D_SLICE)]

    d_ring = [post(slice_for(device), d_fin.at[eighth], device) for device in ring[1:] + cross[1:] + [sibling]]
    for copy in d_ring:
        copy.start()
    d_fin[eighth] = d_slab[:, :, pl.ds(pl.multiple_of(mp * D_SLICE, 128), D_SLICE)]

    for copy in m_z:
        copy.wait_recv()
    total = m_third[z]
    for o in range(7):
        total = total + m_third_in[o]
    m_z_all[z] = total
    m_z_back = [post(m_z_all.at[z], m_z_all.at[z], along_z[o]) for o in range(1, 8)]
    for copy in m_z_back:
        copy.start()
    for copy in m_z_back:
        copy.wait_recv()

    def rows_at(a, low, rows):
        return m_all.at[core, pl.ds(pl.multiple_of(lax.rem(a, 4) * 192 + low, 16), rows)]

    def to(part, device):
        copy = post(part, part, device)
        copy.start()
        return copy

    sub = at_a * 192 + at_b * 48
    for s in range(6):
        rows = pl.ds(pl.multiple_of(sub + s // 2 * 16, 16), 16)
        m_all[core, rows, s % 2 * 128 : s % 2 * 128 + 128] = m_z_all[s]
    own_block = m_all.at[core, pl.ds(pl.multiple_of(sub, 16), 48)]
    m_back_b = [to(own_block, axis_b[o]) for o in (1, 2, 3)]
    for copy in m_back_b:
        copy.wait_recv()
    own_band = rows_at(at_a, 0, 192)
    up_copy = to(own_band, axis_a[1])
    down_copy = to(own_band, axis_a[3])
    m_last = [to(own_band, sibling)]
    up_copy.wait_recv()
    relay_up = to(rows_at(at_a + 3, 0, 96), axis_a[1])
    m_last.append(to(rows_at(at_a + 3, 0, 192), sibling))
    down_copy.wait_recv()
    relay_down = to(rows_at(at_a + 1, 96, 96), axis_a[3])
    m_last.append(to(rows_at(at_a + 1, 0, 192), sibling))
    written = []

    def write(src, dst):
        copy = pltpu.make_async_copy(src, dst, write_sems.at[len(written)])
        copy.start()
        written.append(copy)

    def write_band(of, half):
        rows = pl.ds(pl.multiple_of(lax.rem(of, 4) * 192, 16), 192)
        write(m_all.at[half, rows], m_out.at[half, rows])

    for o in (0, 3, 1):
        write_band(at_a + o, core)
    for copy in d_ring:
        copy.wait_recv()
    write(d_fin, d_out)
    relay_up.wait_recv()
    relay_down.wait_recv()
    m_last.append(to(rows_at(at_a + 2, 0, 192), sibling))
    write_band(at_a + 2, core)
    sib_a = jnp.where(swap, x, y)
    for copy, o in zip(m_last, (0, 3, 1, 2)):
        copy.wait_recv()
        write_band(sib_a + o, other)
    for copy in written:
        copy.wait()

    for s in range(8):

        @pl.when(jnp.logical_not(is_me(targets[s])))
        def _():
            ids_copy(s).wait_send()

    for copy in taken:
        copy.wait_send()


def step_call(*args):
    vmem = pl.BlockSpec(memory_space=pltpu.VMEM)
    smem = pl.BlockSpec(memory_space=pltpu.SMEM)
    hbm = pl.BlockSpec(memory_space=pltpu.HBM)
    dma = pltpu.SemaphoreType.DMA
    f32 = lambda *shape: pltpu.VMEM(shape, F32)
    bf16 = lambda *shape: pltpu.VMEM(shape, BF16)
    i32 = lambda *shape: pltpu.VMEM(shape, jnp.int32)
    return pl.pallas_call(
        step_kernel,
        out_shape=(
            jax.ShapeDtypeStruct((8, 4, 16, D_SLICE), F32),
            jax.ShapeDtypeStruct((2, D_METH, E_HALF), F32),
        ),
        in_specs=[hbm] * 7 + [smem] * 2,
        out_specs=(hbm, hbm),
        scratch_shapes=[
            i32(16, PAIR_DEV),
            i32(16, PAIR_DEV),
            i32(3, 128),
            bf16(D_SLICE, E),
            bf16(VOCAB_DNA, D_SLICE),
            bf16(VOCAB_METH, D_METH),
            bf16(D_METH, E),
            i32(PAIR_DEV, 16),
            i32(16, COLS),
            i32(2, 3, 128),
            i32(ROWS, 128),
            bf16(4 * D_SLICE, ROWS),
            bf16(E, 4 * D_SLICE),
            bf16(D_METH, VOCAB_METH),
            bf16(E, D_METH),
            bf16(D_METH, COLS),
            f32(E, COLS),
            bf16(E, COLS),
            f32(1, COLS),
            f32(E, ROWS),
            f32(1, ROWS),
            bf16(E, ROWS),
            bf16(ROWS, E),
            f32(E, ROWS),
            bf16(ROWS, COLS),
            bf16(D_METH, E_HALF),
            bf16(D_METH, E_HALF),
            f32(D_METH, E_HALF),
            bf16(D_METH, E_HALF),
            bf16(3, 192, E_HALF),
            f32(4, 48, E_HALF),
            f32(3, 48, E_HALF),
            f32(8, 16, 128),
            f32(7, 16, 128),
            f32(8, 16, 128),
            bf16(E, ROWS),
            bf16(256, ROWS),
            bf16(4, 64, ROWS),
            bf16(3, 64, ROWS),
            f32(4, 16, 4 * D_SLICE),
            bf16(4, 16, 4 * D_SLICE),
            bf16(3, 16, 4 * D_SLICE),
            f32(8, 16, 128),
            f32(7, 16, 128),
            f32(8, 16, 128),
            f32(4, 16, 4 * D_SLICE),
            f32(2, D_METH, E_HALF),
            f32(8, 4, 16, D_SLICE),
            dma((8,)),
            dma((8,)),
            dma((N_COPIES,)),
            dma((N_COPIES,)),
            dma((8,)),
            dma((9,)),
        ],
        compiler_params=pltpu.CompilerParams(
            collective_id=0, has_side_effects=True, vmem_limit_bytes=56 * 1024 * 1024
        ),
        cost_estimate=pl.CostEstimate(flops=19 * 10**9, bytes_accessed=8 * 10**6, transcendentals=5 * 10**6),
        name="contrastive_step",
    )(*args)


def hand_over_kernel(d_in, m_in, d_out, m_out, d_here, m_here, d_turned, in_sems, out_sems):
    m_parts = [(half, pl.ds(first, 192)) for half in range(2) for first in range(0, D_METH, 192)]
    d_parts = [slice(s * 128, (s + 1) * 128) for s in range(E // 128)]
    fetch = [(m_in.at[h, rows], m_here.at[h, rows]) for h, rows in m_parts]
    store = [(m_here.at[h, rows], m_out.at[rows, pl.ds(h * E_HALF, E_HALF)]) for h, rows in m_parts]
    fetch += [(d_in.at[rows], d_here.at[rows]) for rows in d_parts]
    store += [(d_turned.at[:, rows], d_out.at[:, rows]) for rows in d_parts]
    fetch = [pltpu.make_async_copy(*pair, in_sems.at[n]) for n, pair in enumerate(fetch)]
    store = [pltpu.make_async_copy(*pair, out_sems.at[n]) for n, pair in enumerate(store)]
    for copy in fetch:
        copy.start()
    for n in range(len(store)):
        fetch[n].wait()
        if n >= len(m_parts):
            rows = d_parts[n - len(m_parts)]
            d_turned[:, rows] = d_here[rows, :].T
        store[n].start()
    for copy in store:
        copy.wait()


def hand_over(d_part, m_part):
    hbm = pl.BlockSpec(memory_space=pltpu.HBM)
    return pl.pallas_call(
        hand_over_kernel,
        out_shape=(
            jax.ShapeDtypeStruct((D_SLICE, E), F32),
            jax.ShapeDtypeStruct((D_METH, E), F32),
        ),
        in_specs=[hbm, hbm],
        out_specs=(hbm, hbm),
        scratch_shapes=[
            pltpu.VMEM((E, D_SLICE), F32),
            pltpu.VMEM((2, D_METH, E_HALF), F32),
            pltpu.VMEM((D_SLICE, E), F32),
            pltpu.SemaphoreType.DMA((12,)),
            pltpu.SemaphoreType.DMA((12,)),
        ],
        compiler_params=pltpu.CompilerParams(vmem_limit_bytes=56 * 1024 * 1024),
        name="hand_over",
    )(d_part, m_part)


def per_device(
    dna_ids,
    meth_ids,
    pair_index,
    dna_table,
    meth_table,
    dna_proj,
    meth_proj,
    logit_scale,
    logit_bias,
):
    d_part, m_part = step_call(
        dna_ids.T,
        meth_ids.T,
        pair_index.reshape(3, 128),
        dna_table,
        meth_table,
        dna_proj,
        meth_proj,
        logit_scale,
        logit_bias,
    )
    return hand_over(d_part.reshape(E, D_SLICE), m_part)


def solution(mesh):
    placed = (
        P("blk", None),
        P("blk", None),
        P("blk"),
        P(None, "mp"),
        P(),
        P("mp", None),
        P(),
        P(),
        P(),
    )
    return jax.shard_map(
        per_device, mesh=mesh, in_specs=placed, out_specs=(P("mp", None), P()), check_vma=False
    )
```

```python
import jax
import jax.numpy as jnp
from jax import lax
from jax.experimental import pallas as pl
from jax.experimental.pallas import tpu as pltpu
from jax.sharding import PartitionSpec as P

MESH = pl.DeviceIdType.MESH
F32 = jnp.float32
BF16 = jnp.bfloat16
EPS = 1e-06

PAIR_DEV = 384
ROWS = 2 * PAIR_DEV
COLS = 8 * PAIR_DEV
E = 512
D_SLICE = 256
D_METH = 768
VOCAB_DNA = 4096
VOCAB_METH = 512
CHUNK = 768
PART = 256
LOG2E = 1.4426950408889634
E_HALF = 256
N_COPIES = 80

NT = (((1,), (1,)), ((), ()))


def place():
    blk, mp = lax.axis_index("blk"), lax.axis_index("mp")
    z = lax.div(blk, 8)
    y = lax.rem(lax.div(blk, 2), 4)
    x = lax.rem(blk, 2) * 2 + lax.div(mp, 2)
    return blk, mp, z, y, x, lax.rem(mp, 2)


def device_at(z, y, x, core):
    return (z * 8 + y * 2 + lax.div(x, 2), lax.rem(x, 2) * 2 + core)


def signal(device):
    pl.semaphore_signal(
        pltpu.get_barrier_semaphore(), inc=1, device_id=device, device_id_type=MESH
    )


def send(src, dst, send_sem, recv_sem, device):
    return pltpu.make_async_remote_copy(
        src_ref=src,
        dst_ref=dst,
        send_sem=send_sem,
        recv_sem=recv_sem,
        device_id=device,
        device_id_type=MESH,
    )


def step_kernel(
    dna_ids_hbm,
    meth_ids_hbm,
    pairs_hbm,
    dna_table_hbm,
    meth_table_hbm,
    dna_proj_hbm,
    meth_proj_hbm,
    scale_ref,
    bias_ref,
    d_out,
    m_out,
    dna_ids,
    meth_ids,
    pairs,
    dna_proj,
    dna_table,
    meth_table,
    meth_proj,
    dna_tokens,
    ids_all,
    pair_all,
    pair_wide,
    dna_pooled,
    dna_projt,
    meth_tablet,
    meth_projt,
    meth_pooled,
    meth_unit,
    meth_rows,
    meth_inv,
    dna_unit,
    dna_inv,
    dna_rowst,
    dna_rows,
    row_acc,
    tiles,
    m_give,
    m_sib,
    m_keep,
    m_first,
    m_low,
    m_first_in,
    m_second,
    m_second_in,
    third,
    third_in,
    third_all,
    back_all,
    back_sib,
    back_half,
    back_in,
    d_first,
    d_first_low,
    d_first_in,
    d_slab,
    m_all,
    d_fin,
    ids_send,
    ids_recv,
    send_sems,
    recv_sems,
    local_sems,
    write_sems,
):
    blk, mp, z, y, x, core = place()
    x_hi = lax.div(x, 2)
    sibling = device_at(z, y, x, 1 - core)
    ring = [device_at(z, y, lax.rem(x + o, 4), core) for o in range(4)]
    cross = [device_at(z, y, lax.rem(x + o, 4), 1 - core) for o in range(4)]
    along_y = [device_at(z, lax.rem(y + o, 4), x, core) for o in range(4)]
    along_z = [device_at(lax.rem(z + o, 8), y, x, core) for o in range(8)]
    ring_place = x_hi * 4 + mp
    nearest = lax.rem(lax.div(ring_place + 1, 2), 4)

    taken = []

    def post(src, dst, device):
        n = len(taken)
        copy = send(src, dst, send_sems.at[n], recv_sems.at[n], device)
        taken.append(copy)
        return copy

    fetch = [
        pltpu.make_async_copy(src, dst, local_sems.at[1 + n])
        for n, (src, dst) in enumerate(
            (
                (dna_table_hbm, dna_table),
                (meth_table_hbm, meth_table),
                (meth_proj_hbm, meth_proj),
                (dna_ids_hbm, dna_ids),
                (meth_ids_hbm, meth_ids),
                (pairs_hbm, pairs),
                (dna_proj_hbm, dna_proj),
            )
        )
    ]
    for n in (4, 5, 6, 3, 0, 1, 2):
        fetch[n].start()

    def at_ring_place(z_of, y_of, place_of):
        return device_at(lax.rem(z_of, 8), lax.rem(y_of, 4), lax.div(place_of, 2), lax.rem(place_of, 2))

    def group(dy):
        dz = lax.rem(ring_place + 8 - 2 * dy, 8)
        return lax.rem(z + dz, 8), lax.rem(y + dy, 4)

    def source(dy, half):
        z_of, y_of = group(dy)
        return ((z_of * 4 + y_of) * 2 + half, dy)

    targets = [at_ring_place(z + 8 - s, y + 4 - mp, lax.rem(s + 2 * mp, 8)) for s in range(8)]
    sources = [source(s // 2, s % 2) for s in range(8)]

    def is_me(device):
        return jnp.logical_and(device[0] == blk, device[1] == mp)

    for s in range(8):

        @pl.when(jnp.logical_not(is_me(sources[s])))
        def _():
            signal(sources[s])

    for o in (1, 2, 3):
        signal(ring[o])
        signal(cross[o])
        signal(along_y[o])
    for o in range(1, 8):
        signal(along_z[o])
    signal(sibling)
    for n in (3, 4, 5, 6):
        fetch[n].wait()
    dna_tokens[...] = dna_ids[...].T

    def count_dna(i, carry):
        rows = pl.ds(pl.multiple_of(i * 16, 16), 16)
        ids = dna_tokens[rows, :]
        place_of = jnp.bitwise_and(ids, VOCAB_DNA // 4 - 1)
        amount = jnp.left_shift(1, jnp.right_shift(ids, 10) * 8)
        lane = lax.broadcasted_iota(jnp.int32, (16, VOCAB_DNA // 4), 1)
        total = jnp.zeros((16, VOCAB_DNA // 4), jnp.int32)
        for t in range(16):
            total = total + jnp.where(lane == place_of[:, t : t + 1], amount[:, t : t + 1], 0)
        for f in range(4):
            field = jnp.bitwise_and(jnp.right_shift(total, 8 * f), 255)
            field = field.astype(F32).astype(BF16)
            if f < 3:
                tiles[rows, f * 1024 : (f + 1) * 1024] = field
            else:
                tiles[pl.ds(pl.multiple_of(PAIR_DEV + i * 16, 16), 16), 0:1024] = field
        return carry

    lax.fori_loop(0, PAIR_DEV // 16, count_dna, 0)
    to_self = jnp.logical_and(mp == 0, x_hi == 0).astype(jnp.int32)
    pl.semaphore_wait(pltpu.get_barrier_semaphore(), 25 - to_self)

    slot = mp * 2 + x_hi
    slot_lanes = pl.ds(pl.multiple_of(slot * PAIR_DEV, 128), PAIR_DEV)

    def ids_copy(s):
        return send(meth_ids, ids_all.at[:, slot_lanes], ids_send.at[s], ids_recv.at[slot], targets[s])

    for s in range(8):

        @pl.when(jnp.logical_not(is_me(targets[s])))
        def _():
            ids_copy(s).start()

        @pl.when(is_me(targets[s]))
        def _():
            local = pltpu.make_async_copy(meth_ids, ids_all.at[:, slot_lanes], local_sems.at[0])
            local.start()
            local.wait()

    pair_copy = post(pairs, pair_all.at[x_hi], ring[2])
    pair_copy.start()
    pair_all[x_hi] = pairs[...]

    dna_projt[:, pl.ds(pl.multiple_of(mp * D_SLICE, 128), D_SLICE)] = dna_proj[...].T
    toward = 1 + 2 * core
    far = device_at(z, y, lax.rem(x + toward, 4), core)
    other_mp = lax.rem(mp + 2, 4)

    def quarter(of):
        return dna_projt.at[:, pl.ds(pl.multiple_of(of * D_SLICE, 128), D_SLICE)]

    proj_far = post(quarter(mp), quarter(mp), far)
    proj_sib = post(quarter(mp), quarter(mp), sibling)
    proj_fwd = post(quarter(other_mp), quarter(other_mp), sibling)
    proj_far.start()
    proj_sib.start()

    fetch[0].wait()
    pooled = jnp.dot(tiles[0:PAIR_DEV, :], dna_table[0:COLS, :], preferred_element_type=F32)
    pooled = pooled + jnp.dot(
        tiles[PAIR_DEV:ROWS, 0 : VOCAB_DNA - COLS], dna_table[COLS:VOCAB_DNA, :], preferred_element_type=F32
    )
    pooled = pooled * 0.0625
    own_lanes = pl.ds(pl.multiple_of(x_hi * PAIR_DEV, 128), PAIR_DEV)
    dna_pooled[pl.ds(pl.multiple_of(mp * D_SLICE, 16), D_SLICE), own_lanes] = pooled.T.astype(BF16)

    def pool_block(x_of, core_of, low=0, count=D_SLICE):
        first = (lax.rem(x_of, 2) * 2 + core_of) * D_SLICE + low
        lanes = pl.ds(pl.multiple_of(lax.div(x_of, 2) * PAIR_DEV, 128), PAIR_DEV)
        return dna_pooled.at[pl.ds(pl.multiple_of(first, 16), count), lanes]

    own = pool_block(x, core)
    from_left = pool_block(lax.rem(x + 3, 4), core)
    from_right = pool_block(lax.rem(x + 1, 4), core)
    from_across = pool_block(lax.rem(x + 2, 4), core)
    pool_right = post(own, own, ring[1])
    pool_left = post(own, own, ring[3])
    pool_sib = post(own, own, sibling)
    pool_right.start()
    pool_left.start()
    pool_sib.start()
    half_left = pool_block(lax.rem(x + 3, 4), core, 0, 128)
    half_right = pool_block(lax.rem(x + 1, 4), core, 128, 128)
    relay_right = post(half_left, half_left, ring[1])
    relay_left = post(half_right, half_right, ring[3])
    pool_fwd = [post(part, part, sibling) for part in (from_left, from_right, from_across)]

    fetch[1].wait()
    fetch[2].wait()
    meth_tablet[...] = meth_table[...].T
    meth_projt[...] = meth_proj[...].T
    def count_meth(ids):
        place_of = jnp.bitwise_and(ids, 127)
        amount = jnp.left_shift(1, jnp.right_shift(ids, 7) * 8)
        row = lax.broadcasted_iota(jnp.int32, (128, 128), 0)
        total = jnp.zeros((128, 128), jnp.int32)
        for t in range(16):
            total = total + jnp.where(row == place_of[t : t + 1, :], amount[t : t + 1, :], 0)
        fields = [jnp.bitwise_and(jnp.right_shift(total, 8 * f), 255) for f in range(4)]
        return jnp.concatenate([field.astype(F32).astype(BF16) for field in fields], axis=0)

    def embed_meth(i, carry):
        dy = lax.rem(nearest + i + lax.div(i, 2) * (5 - 2 * i), 4)
        for half in range(2):
            lanes = pl.ds(pl.multiple_of((dy * 2 + half) * PAIR_DEV, 128), PAIR_DEV)
            arrival = send(
                meth_ids, ids_all.at[:, lanes], ids_send.at[0], ids_recv.at[dy * 2 + half], source(dy, half)
            )

            @pl.when(jnp.logical_not(is_me(source(dy, half))))
            def _():
                arrival.wait_recv()

        for p in range(CHUNK // PART):
            first = pl.multiple_of(dy * CHUNK + p * PART, 128)
            lanes = pl.ds(first, PART)
            ids = [ids_all[:, pl.ds(pl.multiple_of(first + 128 * g, 128), 128)] for g in range(PART // 128)]
            tokens = jnp.concatenate([count_meth(part) for part in ids], axis=1)
            pooled_m = jnp.dot(meth_tablet[...], tokens, preferred_element_type=F32)
            pooled_m = (pooled_m * 0.0625).astype(BF16)
            meth_pooled[:, lanes] = pooled_m
            raw = jnp.dot(meth_projt[...], pooled_m, preferred_element_type=F32)
            inverse = lax.rsqrt(jnp.sum(raw * raw, axis=0, keepdims=True) + EPS)
            unit = raw * inverse
            meth_inv[:, lanes] = inverse
            meth_unit[:, lanes] = unit
            meth_rows[:, lanes] = unit.astype(BF16)
        return carry

    half = COLS // CHUNK // 2
    lax.fori_loop(0, half, embed_meth, 0)
    pool_right.wait_recv()
    relay_right.start()
    pool_left.wait_recv()
    relay_left.start()
    pool_fwd[0].start()
    pool_fwd[1].start()
    proj_far.wait_recv()
    proj_fwd.start()
    lax.fori_loop(half, 2 * half, embed_meth, 0)
    relay_right.wait_recv()
    relay_left.wait_recv()
    pool_fwd[2].start()
    proj_sib.wait_recv()
    proj_fwd.wait_recv()
    pair_copy.wait_recv()
    for h in range(2):
        words = pair_all[h]
        for a in range(3):
            wide = jnp.broadcast_to(words[a : a + 1, :], (128, 128))
            first = h * PAIR_DEV + a * 128
            pair_wide[first : first + 128, :] = wide.T
    pool_sib.wait_recv()
    for copy in pool_fwd:
        copy.wait_recv()

    raw = jnp.dot(dna_projt[...], dna_pooled[...], preferred_element_type=F32)
    inverse = lax.rsqrt(jnp.sum(raw * raw, axis=0, keepdims=True) + EPS)
    unit = raw * inverse
    dna_inv[...] = inverse
    dna_unit[...] = unit
    unit_low = unit.astype(BF16)
    dna_rowst[...] = unit_low
    dna_rows[...] = unit_low.T

    scale = scale_ref[0]
    bias = bias_ref[0]
    slope, offset = scale * -LOG2E, bias * -LOG2E
    def pair_tile(i, carry):
        first = pl.multiple_of(i * CHUNK, 128)
        z_of, y_of = group(i)
        partner = pair_wide[...] - (z_of * 4 + y_of) * ROWS
        parts = []
        for p in range(CHUNK // PART):
            rows_m = meth_rows[:, pl.ds(pl.multiple_of(first + p * PART, 128), PART)]
            dots = jnp.dot(dna_rows[...], rows_m, preferred_element_type=F32)
            lower = 1.0 + jnp.exp2(slope * dots + offset)
            prob = pl.reciprocal(lower, approx=True)
            prob = prob * (2.0 - lower * prob)
            for g in range(PART // 128):
                part = prob[:, g * 128 : (g + 1) * 128]
                lane = lax.broadcasted_iota(jnp.int32, (ROWS, 128), 1) + (p * PART + g * 128)
                parts.append(jnp.where(partner == lane, part - 1.0, part).astype(BF16))
        tile = jnp.concatenate(parts, axis=1)
        tiles[:, pl.ds(first, CHUNK)] = tile
        return carry

    lax.fori_loop(0, COLS // CHUNK, pair_tile, 0)

    row_acc[...] = lax.dot_general(meth_rows[...], tiles[...], NT, preferred_element_type=F32)

    other = 1 - core
    up = scale * row_acc[...]
    inner = jnp.sum(dna_unit[...] * up, axis=0, keepdims=True)
    back_all[...] = (dna_inv[...] * (up - dna_unit[...] * inner)).astype(BF16)
    back_swap = post(back_all.at[pl.ds(pl.multiple_of(other * 256, 16), 256)], back_sib, sibling)
    back_swap.start()

    def col_tile(i, carry):
        first = pl.multiple_of(i * CHUNK, 128)
        for p in range(CHUNK // PART):
            lanes = pl.ds(pl.multiple_of(first + p * PART, 128), PART)
            up = scale * jnp.dot(dna_rowst[...], tiles[:, lanes], preferred_element_type=F32)
            unit_m = meth_unit[:, lanes]
            inner = jnp.sum(unit_m * up, axis=0, keepdims=True)
            meth_rows[:, lanes] = (meth_inv[:, lanes] * (up - unit_m * inner)).astype(BF16)
        return carry

    lax.fori_loop(0, half, col_tile, 0)
    back_swap.wait_recv()
    for a in range(4):
        rows = pl.ds(pl.multiple_of(core * 256 + a * 64, 16), 64)
        both = back_all[rows, :].astype(F32) + back_sib[a * 64 : (a + 1) * 64, :].astype(F32)
        back_half[a] = both.astype(BF16)
    back_x = [post(back_half.at[lax.rem(x + o, 4)], back_in.at[o - 1], ring[o]) for o in (1, 2, 3)]
    for copy in back_x:
        copy.start()
    lax.fori_loop(half, 2 * half, col_tile, 0)

    for copy in back_x:
        copy.wait_recv()
    back = back_half[x].astype(F32)
    for o in range(3):
        back = back + back_in[o].astype(F32)
    back = back.astype(BF16)
    for s in range(4):
        features = dna_pooled[s * D_SLICE : (s + 1) * D_SLICE, :]
        part = lax.dot_general(back, features, NT, preferred_element_type=F32)
        for a in range(4):
            d_first[a, :, s * D_SLICE : (s + 1) * D_SLICE] = part[a * 16 : (a + 1) * 16, :]
            d_first_low[a, :, s * D_SLICE : (s + 1) * D_SLICE] = part[a * 16 : (a + 1) * 16, :].astype(BF16)
    d_y = [post(d_first_low.at[lax.rem(y + o, 4)], d_first_in.at[o - 1], along_y[o]) for o in (1, 2, 3)]
    for copy in d_y:
        copy.start()

    def half_head(which):
        rows = pl.ds(pl.multiple_of(which * E_HALF, 16), E_HALF)
        return lax.dot_general(meth_pooled[...], meth_rows[rows, :], NT, preferred_element_type=F32)

    m_give[...] = half_head(other).astype(BF16)
    m_swap = post(m_give, m_sib, sibling)
    m_swap.start()
    m_keep[...] = half_head(core)

    swap = core == 1

    def pick(one, two):
        return tuple(jnp.where(swap, q, p) for p, q in zip(one, two))

    axis_a = [pick(p, q) for p, q in zip(ring, along_y)]
    axis_b = [pick(q, p) for p, q in zip(ring, along_y)]
    at_a = jnp.where(swap, y, x)
    at_b = jnp.where(swap, x, y)
    m_swap.wait_recv()

    def halve(i, carry):
        a, b = lax.div(i, 4), lax.rem(i, 4)
        rows = pl.ds(pl.multiple_of(jnp.where(swap, a * 192 + b * 48, b * 192 + a * 48), 16), 48)
        both = m_keep[rows, :] + m_sib[rows, :].astype(F32)
        m_first[a, b] = both
        m_low[a, b] = both.astype(BF16)
        return carry

    lax.fori_loop(0, 16, halve, 0)
    m_a = [post(m_low.at[lax.rem(at_a + o, 4)], m_first_in.at[o - 1], axis_a[o]) for o in (1, 2, 3)]
    for copy in m_a:
        copy.start()

    for copy in d_y:
        copy.wait_recv()
    d_sum = d_first[y]
    for o in range(3):
        d_sum = d_sum + d_first_in[o].astype(F32)
    for s in range(8):
        third[s, 1] = d_sum[:, s * 128 : (s + 1) * 128]

    for copy in m_a:
        copy.wait_recv()
    for b in range(4):
        part = m_first[at_a, b]
        for o in range(3):
            part = part + m_first_in[o, b].astype(F32)
        m_second[b] = part
    m_b = [post(m_second.at[lax.rem(at_b + o, 4)], m_second_in.at[o - 1], axis_b[o]) for o in (1, 2, 3)]
    for copy in m_b:
        copy.start()
    for copy in m_b:
        copy.wait_recv()
    m_sum = m_second[at_b]
    for o in range(3):
        m_sum = m_sum + m_second_in[o]
    for s in range(6):
        third[s, 0] = m_sum[s // 2 * 16 : s // 2 * 16 + 16, s % 2 * 128 : s % 2 * 128 + 128]
    third[6, 0] = jnp.zeros((16, 128), F32)
    third[7, 0] = jnp.zeros((16, 128), F32)

    z_sum = [post(third.at[lax.rem(z + o, 8)], third_in.at[o - 1], along_z[o]) for o in range(1, 8)]
    for copy in z_sum:
        copy.start()
    for copy in z_sum:
        copy.wait_recv()
    total = third[z]
    for o in range(7):
        total = total + third_in[o]
    third_all[z] = total
    z_back = [post(third_all.at[z], third_all.at[z], along_z[o]) for o in range(1, 8)]
    for copy in z_back:
        copy.start()
    for copy in z_back:
        copy.wait_recv()

    for s in range(8):
        d_slab[y, :, s * 128 : (s + 1) * 128] = third_all[s, 1]
    d_back = [post(d_slab.at[y], d_slab.at[y], along_y[o]) for o in (1, 2, 3)]
    for copy in d_back:
        copy.start()

    def rows_at(y_of, low, rows):
        return m_all.at[core, pl.ds(pl.multiple_of(lax.rem(y_of, 4) * 192 + low, 16), rows)]

    def to(part, device):
        copy = post(part, part, device)
        copy.start()
        return copy

    sub = y * 192 + x * 48
    for s in range(6):
        rows = pl.ds(pl.multiple_of(sub + s // 2 * 16, 16), 16)
        m_all[core, rows, s % 2 * 128 : s % 2 * 128 + 128] = third_all[s, 0]
    own_block = m_all.at[core, pl.ds(pl.multiple_of(sub, 16), 48)]
    m_back_x = [to(own_block, ring[o]) for o in (1, 2, 3)]
    for copy in m_back_x:
        copy.wait_recv()
    own_band = rows_at(y, 0, 192)
    up_copy = to(own_band, along_y[1])
    down_copy = to(own_band, along_y[3])
    m_last = [to(own_band, sibling)]

    for copy in d_back:
        copy.wait_recv()
    eighth = core * 4 + x

    def slice_for(device):
        return d_slab.at[:, :, pl.ds(pl.multiple_of(device[1] * D_SLICE, 128), D_SLICE)]

    d_ring = [post(slice_for(device), d_fin.at[eighth], device) for device in ring[1:] + cross[1:] + [sibling]]
    for copy in d_ring:
        copy.start()
    d_fin[eighth] = d_slab[:, :, pl.ds(pl.multiple_of(mp * D_SLICE, 128), D_SLICE)]

    written = []

    def write(src, dst):
        copy = pltpu.make_async_copy(src, dst, write_sems.at[len(written)])
        copy.start()
        written.append(copy)

    def write_band(y_of, half):
        rows = pl.ds(pl.multiple_of(lax.rem(y_of, 4) * 192, 16), 192)
        write(m_all.at[half, rows], m_out.at[half, rows])

    write_band(y, core)
    up_copy.wait_recv()
    relay_up = to(rows_at(y + 3, 0, 96), along_y[1])
    m_last.append(to(rows_at(y + 3, 0, 192), sibling))
    down_copy.wait_recv()
    relay_down = to(rows_at(y + 1, 96, 96), along_y[3])
    m_last.append(to(rows_at(y + 1, 0, 192), sibling))
    write_band(y + 3, core)
    write_band(y + 1, core)
    for copy in d_ring:
        copy.wait_recv()
    write(d_fin, d_out)
    relay_up.wait_recv()
    relay_down.wait_recv()
    m_last.append(to(rows_at(y + 2, 0, 192), sibling))
    write_band(y + 2, core)
    for copy, o in zip(m_last, (0, 3, 1, 2)):
        copy.wait_recv()
        write_band(y + o, other)
    for copy in written:
        copy.wait()

    for s in range(8):

        @pl.when(jnp.logical_not(is_me(targets[s])))
        def _():
            ids_copy(s).wait_send()

    for copy in taken:
        copy.wait_send()


def step_call(*args):
    vmem = pl.BlockSpec(memory_space=pltpu.VMEM)
    smem = pl.BlockSpec(memory_space=pltpu.SMEM)
    hbm = pl.BlockSpec(memory_space=pltpu.HBM)
    dma = pltpu.SemaphoreType.DMA
    f32 = lambda *shape: pltpu.VMEM(shape, F32)
    bf16 = lambda *shape: pltpu.VMEM(shape, BF16)
    i32 = lambda *shape: pltpu.VMEM(shape, jnp.int32)
    return pl.pallas_call(
        step_kernel,
        out_shape=(
            jax.ShapeDtypeStruct((8, 4, 16, D_SLICE), F32),
            jax.ShapeDtypeStruct((2, D_METH, E_HALF), F32),
        ),
        in_specs=[hbm] * 7 + [smem] * 2,
        out_specs=(hbm, hbm),
        scratch_shapes=[
            i32(16, PAIR_DEV),
            i32(16, PAIR_DEV),
            i32(3, 128),
            bf16(D_SLICE, E),
            bf16(VOCAB_DNA, D_SLICE),
            bf16(VOCAB_METH, D_METH),
            bf16(D_METH, E),
            i32(PAIR_DEV, 16),
            i32(16, COLS),
            i32(2, 3, 128),
            i32(ROWS, 128),
            bf16(4 * D_SLICE, ROWS),
            bf16(E, 4 * D_SLICE),
            bf16(D_METH, VOCAB_METH),
            bf16(E, D_METH),
            bf16(D_METH, COLS),
            f32(E, COLS),
            bf16(E, COLS),
            f32(1, COLS),
            f32(E, ROWS),
            f32(1, ROWS),
            bf16(E, ROWS),
            bf16(ROWS, E),
            f32(E, ROWS),
            bf16(ROWS, COLS),
            bf16(D_METH, E_HALF),
            bf16(D_METH, E_HALF),
            f32(D_METH, E_HALF),
            f32(4, 4, 48, E_HALF),
            bf16(4, 4, 48, E_HALF),
            bf16(3, 4, 48, E_HALF),
            f32(4, 48, E_HALF),
            f32(3, 48, E_HALF),
            f32(8, 2, 16, 128),
            f32(7, 2, 16, 128),
            f32(8, 2, 16, 128),
            bf16(E, ROWS),
            bf16(256, ROWS),
            bf16(4, 64, ROWS),
            bf16(3, 64, ROWS),
            f32(4, 16, 4 * D_SLICE),
            bf16(4, 16, 4 * D_SLICE),
            bf16(3, 16, 4 * D_SLICE),
            f32(4, 16, 4 * D_SLICE),
            f32(2, D_METH, E_HALF),
            f32(8, 4, 16, D_SLICE),
            dma((8,)),
            dma((8,)),
            dma((N_COPIES,)),
            dma((N_COPIES,)),
            dma((8,)),
            dma((9,)),
        ],
        compiler_params=pltpu.CompilerParams(
            collective_id=0, has_side_effects=True, vmem_limit_bytes=56 * 1024 * 1024
        ),
        cost_estimate=pl.CostEstimate(flops=19 * 10**9, bytes_accessed=8 * 10**6, transcendentals=5 * 10**6),
        name="contrastive_step",
    )(*args)


def hand_over_kernel(d_in, m_in, d_out, m_out, d_here, m_here, d_turned, in_sems, out_sems):
    m_parts = [(half, pl.ds(first, 192)) for half in range(2) for first in range(0, D_METH, 192)]
    d_parts = [slice(s * 128, (s + 1) * 128) for s in range(E // 128)]
    fetch = [(m_in.at[h, rows], m_here.at[h, rows]) for h, rows in m_parts]
    store = [(m_here.at[h, rows], m_out.at[rows, pl.ds(h * E_HALF, E_HALF)]) for h, rows in m_parts]
    fetch += [(d_in.at[rows], d_here.at[rows]) for rows in d_parts]
    store += [(d_turned.at[:, rows], d_out.at[:, rows]) for rows in d_parts]
    fetch = [pltpu.make_async_copy(*pair, in_sems.at[n]) for n, pair in enumerate(fetch)]
    store = [pltpu.make_async_copy(*pair, out_sems.at[n]) for n, pair in enumerate(store)]
    for copy in fetch:
        copy.start()
    for n in range(len(store)):
        fetch[n].wait()
        if n >= len(m_parts):
            rows = d_parts[n - len(m_parts)]
            d_turned[:, rows] = d_here[rows, :].T
        store[n].start()
    for copy in store:
        copy.wait()


def hand_over(d_part, m_part):
    hbm = pl.BlockSpec(memory_space=pltpu.HBM)
    return pl.pallas_call(
        hand_over_kernel,
        out_shape=(
            jax.ShapeDtypeStruct((D_SLICE, E), F32),
            jax.ShapeDtypeStruct((D_METH, E), F32),
        ),
        in_specs=[hbm, hbm],
        out_specs=(hbm, hbm),
        scratch_shapes=[
            pltpu.VMEM((E, D_SLICE), F32),
            pltpu.VMEM((2, D_METH, E_HALF), F32),
            pltpu.VMEM((D_SLICE, E), F32),
            pltpu.SemaphoreType.DMA((12,)),
            pltpu.SemaphoreType.DMA((12,)),
        ],
        compiler_params=pltpu.CompilerParams(vmem_limit_bytes=56 * 1024 * 1024),
        name="hand_over",
    )(d_part, m_part)


def per_device(
    dna_ids,
    meth_ids,
    pair_index,
    dna_table,
    meth_table,
    dna_proj,
    meth_proj,
    logit_scale,
    logit_bias,
):
    d_part, m_part = step_call(
        dna_ids.T,
        meth_ids.T,
        pair_index.reshape(3, 128),
        dna_table,
        meth_table,
        dna_proj,
        meth_proj,
        logit_scale,
        logit_bias,
    )
    return hand_over(d_part.reshape(E, D_SLICE), m_part)


def solution(mesh):
    placed = (
        P("blk", None),
        P("blk", None),
        P("blk"),
        P(None, "mp"),
        P(),
        P("mp", None),
        P(),
        P(),
        P(),
    )
    return jax.shard_map(
        per_device, mesh=mesh, in_specs=placed, out_specs=(P("mp", None), P()), check_vma=False
    )
```

```python
import jax
import jax.numpy as jnp
from jax import lax
from jax.experimental import pallas as pl
from jax.experimental.pallas import tpu as pltpu
from jax.sharding import PartitionSpec as P

MESH = pl.DeviceIdType.MESH
F32 = jnp.float32
BF16 = jnp.bfloat16
EPS = 1e-06

PAIR_DEV = 384
ROWS = 2 * PAIR_DEV
COLS = 8 * PAIR_DEV
E = 512
D_SLICE = 256
D_METH = 768
VOCAB_DNA = 4096
VOCAB_METH = 512
CHUNK = 1536
PART = 512
EMBED = 256
NIBBLES = 0x0F0F0F0F
LOG2E = 1.4426950408889634
E_HALF = 256
N_COPIES = 80

NT = (((1,), (1,)), ((), ()))


def place():
    blk, mp = lax.axis_index("blk"), lax.axis_index("mp")
    z = lax.div(blk, 8)
    y = lax.rem(lax.div(blk, 2), 4)
    x = lax.rem(blk, 2) * 2 + lax.div(mp, 2)
    return blk, mp, z, y, x, lax.rem(mp, 2)


def device_at(z, y, x, core):
    return (z * 8 + y * 2 + lax.div(x, 2), lax.rem(x, 2) * 2 + core)


def signal(device):
    pl.semaphore_signal(
        pltpu.get_barrier_semaphore(), inc=1, device_id=device, device_id_type=MESH
    )


def send(src, dst, send_sem, recv_sem, device):
    return pltpu.make_async_remote_copy(
        src_ref=src,
        dst_ref=dst,
        send_sem=send_sem,
        recv_sem=recv_sem,
        device_id=device,
        device_id_type=MESH,
    )


def token_counts(ids, bits, axis):
    place_of = jnp.bitwise_and(ids, 2**bits - 1)
    amount = jnp.left_shift(1, jnp.right_shift(ids, bits) * 4)
    shape = (ids.shape[0], 2**bits) if axis else (2**bits, ids.shape[1])
    spot = lax.broadcasted_iota(jnp.int32, shape, axis)
    even = odd = None
    for first in (0, 8):
        total = jnp.zeros(shape, jnp.int32)
        for t in range(first, first + 8):
            take = (slice(None), slice(t, t + 1)) if axis else (slice(t, t + 1), slice(None))
            total = total + jnp.where(spot == place_of[take], amount[take], 0)
        low = jnp.bitwise_and(total, NIBBLES)
        high = jnp.bitwise_and(jnp.right_shift(total, 4), NIBBLES)
        even, odd = (low, high) if even is None else (even + low, odd + high)
    fields = []
    for f in range(8):
        field = jnp.bitwise_and(jnp.right_shift(odd if f % 2 else even, f // 2 * 8), 255)
        fields.append(field.astype(F32).astype(BF16))
    return fields


def step_kernel(
    dna_ids_hbm,
    meth_ids_hbm,
    pairs_hbm,
    dna_table_hbm,
    meth_table_hbm,
    dna_proj_hbm,
    meth_proj_hbm,
    scale_ref,
    bias_ref,
    d_out,
    m_out,
    dna_ids,
    meth_ids,
    pairs,
    dna_proj,
    dna_table,
    meth_table,
    meth_proj,
    dna_tokens,
    ids_all,
    pair_all,
    pair_wide,
    dna_pooled,
    dna_projt,
    meth_tablet,
    meth_projt,
    meth_pooled,
    meth_unit,
    meth_rows,
    meth_inv,
    dna_unit,
    dna_inv,
    dna_rowst,
    dna_rows,
    row_acc,
    tiles,
    m_keep,
    m_low,
    m_first_in,
    m_second,
    m_second_in,
    third,
    third_in,
    third_all,
    back_all,
    back_sib,
    back_half,
    back_in,
    d_first,
    d_first_low,
    d_first_in,
    d_slab,
    m_all,
    d_fin,
    ids_send,
    ids_recv,
    send_sems,
    recv_sems,
    local_sems,
    write_sems,
):
    blk, mp, z, y, x, core = place()
    x_hi = lax.div(x, 2)
    sibling = device_at(z, y, x, 1 - core)
    ring = [device_at(z, y, lax.rem(x + o, 4), core) for o in range(4)]
    cross = [device_at(z, y, lax.rem(x + o, 4), 1 - core) for o in range(4)]
    along_y = [device_at(z, lax.rem(y + o, 4), x, core) for o in range(4)]
    cross_y = [device_at(z, lax.rem(y + o, 4), x, 1 - core) for o in range(4)]
    along_z = [device_at(lax.rem(z + o, 8), y, x, core) for o in range(8)]
    ring_place = x_hi * 4 + mp
    nearest = lax.rem(lax.div(ring_place + 1, 2), 4)

    taken = []

    def post(src, dst, device):
        n = len(taken)
        copy = send(src, dst, send_sems.at[n], recv_sems.at[n], device)
        taken.append(copy)
        return copy

    fetch = [
        pltpu.make_async_copy(src, dst, local_sems.at[1 + n])
        for n, (src, dst) in enumerate(
            (
                (dna_table_hbm, dna_table),
                (meth_table_hbm, meth_table),
                (meth_proj_hbm, meth_proj),
                (dna_ids_hbm, dna_ids),
                (meth_ids_hbm, meth_ids),
                (pairs_hbm, pairs),
                (dna_proj_hbm, dna_proj),
            )
        )
    ]
    for n in (4, 5, 6, 3, 0, 1, 2):
        fetch[n].start()

    def at_ring_place(z_of, y_of, place_of):
        return device_at(lax.rem(z_of, 8), lax.rem(y_of, 4), lax.div(place_of, 2), lax.rem(place_of, 2))

    def group(dy):
        dz = lax.rem(ring_place + 8 - 2 * dy, 8)
        return lax.rem(z + dz, 8), lax.rem(y + dy, 4)

    def source(dy, half):
        z_of, y_of = group(dy)
        return ((z_of * 4 + y_of) * 2 + half, dy)

    targets = [at_ring_place(z + 8 - s, y + 4 - mp, lax.rem(s + 2 * mp, 8)) for s in range(8)]
    sources = [source(s // 2, s % 2) for s in range(8)]

    def is_me(device):
        return jnp.logical_and(device[0] == blk, device[1] == mp)

    for s in range(8):

        @pl.when(jnp.logical_not(is_me(sources[s])))
        def _():
            signal(sources[s])

    for o in (1, 2, 3):
        signal(ring[o])
        signal(cross[o])
        signal(along_y[o])
        signal(cross_y[o])
    for o in range(1, 8):
        signal(along_z[o])
    signal(sibling)
    for n in (3, 4, 5, 6):
        fetch[n].wait()
    dna_tokens[...] = dna_ids[...].T

    def count_dna(i, carry):
        rows = pl.ds(pl.multiple_of(i * 16, 16), 16)
        fields = token_counts(dna_tokens[rows, :], 9, 1)
        for f, field in enumerate(fields):
            if f < 6:
                tiles[rows, f * 512 : (f + 1) * 512] = field
            else:
                low = pl.ds(pl.multiple_of(PAIR_DEV + i * 16, 16), 16)
                tiles[low, (f - 6) * 512 : (f - 5) * 512] = field
        return carry

    lax.fori_loop(0, PAIR_DEV // 16, count_dna, 0)
    to_self = jnp.logical_and(mp == 0, x_hi == 0).astype(jnp.int32)
    pl.semaphore_wait(pltpu.get_barrier_semaphore(), 28 - to_self)

    slot = mp * 2 + x_hi
    slot_lanes = pl.ds(pl.multiple_of(slot * PAIR_DEV, 128), PAIR_DEV)

    def ids_copy(s):
        return send(meth_ids, ids_all.at[:, slot_lanes], ids_send.at[s], ids_recv.at[slot], targets[s])

    for s in range(8):

        @pl.when(jnp.logical_not(is_me(targets[s])))
        def _():
            ids_copy(s).start()

        @pl.when(is_me(targets[s]))
        def _():
            local = pltpu.make_async_copy(meth_ids, ids_all.at[:, slot_lanes], local_sems.at[0])
            local.start()
            local.wait()

    pair_copy = post(pairs, pair_all.at[x_hi], ring[2])
    pair_copy.start()
    pair_all[x_hi] = pairs[...]

    dna_projt[:, pl.ds(pl.multiple_of(mp * D_SLICE, 128), D_SLICE)] = dna_proj[...].T
    toward = 1 + 2 * core
    far = device_at(z, y, lax.rem(x + toward, 4), core)
    other_mp = lax.rem(mp + 2, 4)

    def quarter(of):
        return dna_projt.at[:, pl.ds(pl.multiple_of(of * D_SLICE, 128), D_SLICE)]

    proj_far = post(quarter(mp), quarter(mp), far)
    proj_sib = post(quarter(mp), quarter(mp), sibling)
    proj_fwd = post(quarter(other_mp), quarter(other_mp), sibling)
    proj_far.start()
    proj_sib.start()

    fetch[0].wait()
    pooled = jnp.dot(tiles[0:PAIR_DEV, :], dna_table[0:COLS, :], preferred_element_type=F32)
    pooled = pooled + jnp.dot(
        tiles[PAIR_DEV:ROWS, 0 : VOCAB_DNA - COLS], dna_table[COLS:VOCAB_DNA, :], preferred_element_type=F32
    )
    pooled = pooled * 0.0625
    own_lanes = pl.ds(pl.multiple_of(x_hi * PAIR_DEV, 128), PAIR_DEV)
    dna_pooled[pl.ds(pl.multiple_of(mp * D_SLICE, 16), D_SLICE), own_lanes] = pooled.T.astype(BF16)

    def pool_block(x_of, core_of, low=0, count=D_SLICE):
        first = (lax.rem(x_of, 2) * 2 + core_of) * D_SLICE + low
        lanes = pl.ds(pl.multiple_of(lax.div(x_of, 2) * PAIR_DEV, 128), PAIR_DEV)
        return dna_pooled.at[pl.ds(pl.multiple_of(first, 16), count), lanes]

    own = pool_block(x, core)
    from_left = pool_block(lax.rem(x + 3, 4), core)
    from_right = pool_block(lax.rem(x + 1, 4), core)
    from_across = pool_block(lax.rem(x + 2, 4), core)
    pool_right = post(own, own, ring[1])
    pool_left = post(own, own, ring[3])
    pool_sib = post(own, own, sibling)
    pool_right.start()
    pool_left.start()
    pool_sib.start()
    half_left = pool_block(lax.rem(x + 3, 4), core, 0, 128)
    half_right = pool_block(lax.rem(x + 1, 4), core, 128, 128)
    relay_right = post(half_left, half_left, ring[1])
    relay_left = post(half_right, half_right, ring[3])
    pool_fwd = [post(part, part, sibling) for part in (from_left, from_right, from_across)]

    fetch[1].wait()
    fetch[2].wait()
    meth_tablet[...] = meth_table[...].T
    meth_projt[...] = meth_proj[...].T
    def embed_meth(i, carry):
        dy = lax.rem(nearest + i + lax.div(i, 2) * (5 - 2 * i), 4)
        for half in range(2):
            lanes = pl.ds(pl.multiple_of((dy * 2 + half) * PAIR_DEV, 128), PAIR_DEV)
            arrival = send(
                meth_ids, ids_all.at[:, lanes], ids_send.at[0], ids_recv.at[dy * 2 + half], source(dy, half)
            )

            @pl.when(jnp.logical_not(is_me(source(dy, half))))
            def _():
                arrival.wait_recv()

        for p in range(ROWS // EMBED):
            first = pl.multiple_of(dy * ROWS + p * EMBED, 128)
            lanes = pl.ds(first, EMBED)
            ids = [ids_all[:, pl.ds(pl.multiple_of(first + 128 * g, 128), 128)] for g in range(EMBED // 128)]
            tokens = jnp.concatenate(
                [jnp.concatenate(token_counts(part, 6, 0), axis=0) for part in ids], axis=1
            )
            pooled_m = jnp.dot(meth_tablet[...], tokens, preferred_element_type=F32)
            pooled_m = (pooled_m * 0.0625).astype(BF16)
            meth_pooled[:, lanes] = pooled_m
            raw = jnp.dot(meth_projt[...], pooled_m, preferred_element_type=F32)
            inverse = lax.rsqrt(jnp.sum(raw * raw, axis=0, keepdims=True) + EPS)
            unit = raw * inverse
            meth_inv[:, lanes] = inverse
            meth_unit[:, lanes] = unit
            meth_rows[:, lanes] = unit.astype(BF16)
        return carry

    lax.fori_loop(0, 2, embed_meth, 0)
    pool_right.wait_recv()
    relay_right.start()
    pool_left.wait_recv()
    relay_left.start()
    pool_fwd[0].start()
    pool_fwd[1].start()
    proj_far.wait_recv()
    proj_fwd.start()
    lax.fori_loop(2, 4, embed_meth, 0)
    relay_right.wait_recv()
    relay_left.wait_recv()
    pool_fwd[2].start()
    proj_sib.wait_recv()
    proj_fwd.wait_recv()
    pair_copy.wait_recv()
    for h in range(2):
        words = pair_all[h]
        for a in range(3):
            wide = jnp.broadcast_to(words[a : a + 1, :], (128, 128))
            first = h * PAIR_DEV + a * 128
            pair_wide[first : first + 128, :] = wide.T
    pool_sib.wait_recv()
    for copy in pool_fwd:
        copy.wait_recv()

    raw = jnp.dot(dna_projt[...], dna_pooled[...], preferred_element_type=F32)
    inverse = lax.rsqrt(jnp.sum(raw * raw, axis=0, keepdims=True) + EPS)
    unit = raw * inverse
    dna_inv[...] = inverse
    dna_unit[...] = unit
    unit_low = unit.astype(BF16)
    dna_rowst[...] = unit_low
    dna_rows[...] = unit_low.T

    scale = scale_ref[0]
    bias = bias_ref[0]
    slope, offset = scale * -LOG2E, bias * -LOG2E
    def pair_tile(i, carry):
        first = pl.multiple_of(i * CHUNK, 128)
        partners = []
        for j in range(CHUNK // ROWS):
            z_of, y_of = group(i * (CHUNK // ROWS) + j)
            partners.append(pair_wide[...] - (z_of * 4 + y_of) * ROWS)
        parts = []
        for p in range(CHUNK // PART):
            rows_m = meth_rows[:, pl.ds(pl.multiple_of(first + p * PART, 128), PART)]
            dots = jnp.dot(dna_rows[...], rows_m, preferred_element_type=F32)
            lower = 1.0 + jnp.exp2(slope * dots + offset)
            prob = pl.reciprocal(lower, approx=True)
            prob = prob * (2.0 - lower * prob)
            for g in range(PART // 128):
                part = prob[:, g * 128 : (g + 1) * 128]
                j, low = divmod(p * PART + g * 128, ROWS)
                lane = lax.broadcasted_iota(jnp.int32, (ROWS, 128), 1) + low
                parts.append(jnp.where(partners[j] == lane, part - 1.0, part).astype(BF16))
        tile = jnp.concatenate(parts, axis=1)
        tiles[:, pl.ds(first, CHUNK)] = tile
        return carry

    lax.fori_loop(0, COLS // CHUNK, pair_tile, 0)

    row_acc[...] = lax.dot_general(meth_rows[...], tiles[...], NT, preferred_element_type=F32)

    other = 1 - core
    up = scale * row_acc[...]
    inner = jnp.sum(dna_unit[...] * up, axis=0, keepdims=True)
    back_all[...] = (dna_inv[...] * (up - dna_unit[...] * inner)).astype(BF16)
    back_swap = post(back_all.at[pl.ds(pl.multiple_of(other * 256, 16), 256)], back_sib, sibling)
    back_swap.start()

    def col_tile(i, carry):
        first = pl.multiple_of(i * CHUNK, 128)
        for p in range(CHUNK // PART):
            lanes = pl.ds(pl.multiple_of(first + p * PART, 128), PART)
            up = scale * jnp.dot(dna_rowst[...], tiles[:, lanes], preferred_element_type=F32)
            unit_m = meth_unit[:, lanes]
            inner = jnp.sum(unit_m * up, axis=0, keepdims=True)
            meth_rows[:, lanes] = (meth_inv[:, lanes] * (up - unit_m * inner)).astype(BF16)
        return carry

    lax.fori_loop(0, 1, col_tile, 0)
    back_swap.wait_recv()
    for a in range(4):
        rows = pl.ds(pl.multiple_of(core * 256 + a * 64, 16), 64)
        both = back_all[rows, :].astype(F32) + back_sib[a * 64 : (a + 1) * 64, :].astype(F32)
        back_half[a] = both.astype(BF16)
    back_x = [post(back_half.at[lax.rem(x + o, 4)], back_in.at[o - 1], ring[o]) for o in (1, 2, 3)]
    for copy in back_x:
        copy.start()
    lax.fori_loop(1, 2, col_tile, 0)

    for copy in back_x:
        copy.wait_recv()
    back = back_half[x].astype(F32)
    for o in range(3):
        back = back + back_in[o].astype(F32)
    back = back.astype(BF16)
    for s in range(4):
        features = dna_pooled[s * D_SLICE : (s + 1) * D_SLICE, :]
        part = lax.dot_general(back, features, NT, preferred_element_type=F32)
        for a in range(4):
            d_first[a, :, s * D_SLICE : (s + 1) * D_SLICE] = part[a * 16 : (a + 1) * 16, :]
            d_first_low[a, :, s * D_SLICE : (s + 1) * D_SLICE] = part[a * 16 : (a + 1) * 16, :].astype(BF16)
    d_y = [post(d_first_low.at[lax.rem(y + o, 4)], d_first_in.at[o - 1], along_y[o]) for o in (1, 2, 3)]
    for copy in d_y:
        copy.start()

    swap = core == 1

    def pick(one, two):
        return tuple(jnp.where(swap, q, p) for p, q in zip(one, two))

    axis_a = [pick(p, q) for p, q in zip(ring, along_y)]
    axis_b = [pick(q, p) for p, q in zip(ring, along_y)]
    cross_a = [pick(q, p) for p, q in zip(cross, cross_y)]
    at_a = jnp.where(swap, y, x)
    at_b = jnp.where(swap, x, y)
    at_cross = jnp.where(swap, x, y)

    def half_head(which):
        rows = pl.ds(pl.multiple_of(which * E_HALF, 16), E_HALF)
        return lax.dot_general(meth_pooled[...], meth_rows[rows, :], NT, preferred_element_type=F32)

    def block_rows(which, a, b):
        return pl.ds(pl.multiple_of(jnp.where(which == 1, a * 192 + b * 48, b * 192 + a * 48), 16), 48)

    def pack(which):
        def pack_block(i, carry):
            a, b = lax.div(i, 4), lax.rem(i, 4)
            m_low[which, a, b] = m_keep[block_rows(which, a, b), :].astype(BF16)
            return carry

        lax.fori_loop(0, 16, pack_block, 0)

    m_keep[...] = half_head(other)
    pack(other)
    m_a = [
        post(m_low.at[other, lax.rem(at_cross + o, 4)], m_first_in.at[3 + o], sibling if o == 0 else cross_a[o])
        for o in range(4)
    ]
    for copy in m_a:
        copy.start()
    m_keep[...] = half_head(core)
    pack(core)
    m_own = [post(m_low.at[core, lax.rem(at_a + o, 4)], m_first_in.at[o - 1], axis_a[o]) for o in (1, 2, 3)]
    for copy in m_own:
        copy.start()
    m_a = m_a + m_own

    for copy in d_y:
        copy.wait_recv()
    d_sum = d_first[y]
    for o in range(3):
        d_sum = d_sum + d_first_in[o].astype(F32)
    for s in range(8):
        third[s, 1] = d_sum[:, s * 128 : (s + 1) * 128]

    for copy in m_a:
        copy.wait_recv()
    for b in range(4):
        part = m_keep[block_rows(core, at_a, b), :]
        for o in range(7):
            part = part + m_first_in[o, b].astype(F32)
        m_second[b] = part
    m_b = [post(m_second.at[lax.rem(at_b + o, 4)], m_second_in.at[o - 1], axis_b[o]) for o in (1, 2, 3)]
    for copy in m_b:
        copy.start()
    for copy in m_b:
        copy.wait_recv()
    m_sum = m_second[at_b]
    for o in range(3):
        m_sum = m_sum + m_second_in[o]
    for s in range(6):
        third[s, 0] = m_sum[s // 2 * 16 : s // 2 * 16 + 16, s % 2 * 128 : s % 2 * 128 + 128]
    third[6, 0] = jnp.zeros((16, 128), F32)
    third[7, 0] = jnp.zeros((16, 128), F32)

    z_sum = [post(third.at[lax.rem(z + o, 8)], third_in.at[o - 1], along_z[o]) for o in range(1, 8)]
    for copy in z_sum:
        copy.start()
    for copy in z_sum:
        copy.wait_recv()
    total = third[z]
    for o in range(7):
        total = total + third_in[o]
    third_all[z] = total
    z_back = [post(third_all.at[z], third_all.at[z], along_z[o]) for o in range(1, 8)]
    for copy in z_back:
        copy.start()
    for copy in z_back:
        copy.wait_recv()

    for s in range(8):
        d_slab[y, :, s * 128 : (s + 1) * 128] = third_all[s, 1]
    d_back = [post(d_slab.at[y], d_slab.at[y], along_y[o]) for o in (1, 2, 3)]
    for copy in d_back:
        copy.start()

    def rows_at(y_of, low, rows):
        return m_all.at[core, pl.ds(pl.multiple_of(lax.rem(y_of, 4) * 192 + low, 16), rows)]

    def to(part, device):
        copy = post(part, part, device)
        copy.start()
        return copy

    sub = y * 192 + x * 48
    for s in range(6):
        rows = pl.ds(pl.multiple_of(sub + s // 2 * 16, 16), 16)
        m_all[core, rows, s % 2 * 128 : s % 2 * 128 + 128] = third_all[s, 0]
    own_block = m_all.at[core, pl.ds(pl.multiple_of(sub, 16), 48)]
    m_back_x = [to(own_block, ring[o]) for o in (1, 2, 3)]
    for copy in m_back_x:
        copy.wait_recv()
    own_band = rows_at(y, 0, 192)
    up_copy = to(own_band, along_y[1])
    down_copy = to(own_band, along_y[3])
    m_last = [to(own_band, sibling)]

    for copy in d_back:
        copy.wait_recv()
    eighth = core * 4 + x

    def slice_for(device):
        return d_slab.at[:, :, pl.ds(pl.multiple_of(device[1] * D_SLICE, 128), D_SLICE)]

    d_ring = [post(slice_for(device), d_fin.at[eighth], device) for device in ring[1:] + cross[1:] + [sibling]]
    for copy in d_ring:
        copy.start()
    d_fin[eighth] = d_slab[:, :, pl.ds(pl.multiple_of(mp * D_SLICE, 128), D_SLICE)]

    written = []

    def write(src, dst):
        copy = pltpu.make_async_copy(src, dst, write_sems.at[len(written)])
        copy.start()
        written.append(copy)

    def write_band(y_of, half):
        rows = pl.ds(pl.multiple_of(lax.rem(y_of, 4) * 192, 16), 192)
        write(m_all.at[half, rows], m_out.at[half, rows])

    write_band(y, core)
    up_copy.wait_recv()
    relay_up = to(rows_at(y + 3, 0, 96), along_y[1])
    m_last.append(to(rows_at(y + 3, 0, 192), sibling))
    down_copy.wait_recv()
    relay_down = to(rows_at(y + 1, 96, 96), along_y[3])
    m_last.append(to(rows_at(y + 1, 0, 192), sibling))
    write_band(y + 3, core)
    write_band(y + 1, core)
    for copy in d_ring:
        copy.wait_recv()
    write(d_fin, d_out)
    relay_up.wait_recv()
    relay_down.wait_recv()
    m_last.append(to(rows_at(y + 2, 0, 192), sibling))
    write_band(y + 2, core)
    for copy, o in zip(m_last, (0, 3, 1, 2)):
        copy.wait_recv()
        write_band(y + o, other)
    for copy in written:
        copy.wait()

    for s in range(8):

        @pl.when(jnp.logical_not(is_me(targets[s])))
        def _():
            ids_copy(s).wait_send()

    for copy in taken:
        copy.wait_send()


def step_call(*args):
    vmem = pl.BlockSpec(memory_space=pltpu.VMEM)
    smem = pl.BlockSpec(memory_space=pltpu.SMEM)
    hbm = pl.BlockSpec(memory_space=pltpu.HBM)
    dma = pltpu.SemaphoreType.DMA
    f32 = lambda *shape: pltpu.VMEM(shape, F32)
    bf16 = lambda *shape: pltpu.VMEM(shape, BF16)
    i32 = lambda *shape: pltpu.VMEM(shape, jnp.int32)
    return pl.pallas_call(
        step_kernel,
        out_shape=(
            jax.ShapeDtypeStruct((8, 4, 16, D_SLICE), F32),
            jax.ShapeDtypeStruct((2, D_METH, E_HALF), F32),
        ),
        in_specs=[hbm] * 7 + [smem] * 2,
        out_specs=(hbm, hbm),
        scratch_shapes=[
            i32(16, PAIR_DEV),
            i32(16, PAIR_DEV),
            i32(3, 128),
            bf16(D_SLICE, E),
            bf16(VOCAB_DNA, D_SLICE),
            bf16(VOCAB_METH, D_METH),
            bf16(D_METH, E),
            i32(PAIR_DEV, 16),
            i32(16, COLS),
            i32(2, 3, 128),
            i32(ROWS, 128),
            bf16(4 * D_SLICE, ROWS),
            bf16(E, 4 * D_SLICE),
            bf16(D_METH, VOCAB_METH),
            bf16(E, D_METH),
            bf16(D_METH, COLS),
            f32(E, COLS),
            bf16(E, COLS),
            f32(1, COLS),
            f32(E, ROWS),
            f32(1, ROWS),
            bf16(E, ROWS),
            bf16(ROWS, E),
            f32(E, ROWS),
            bf16(ROWS, COLS),
            f32(D_METH, E_HALF),
            bf16(2, 4, 4, 48, E_HALF),
            bf16(7, 4, 48, E_HALF),
            f32(4, 48, E_HALF),
            f32(3, 48, E_HALF),
            f32(8, 2, 16, 128),
            f32(7, 2, 16, 128),
            f32(8, 2, 16, 128),
            bf16(E, ROWS),
            bf16(256, ROWS),
            bf16(4, 64, ROWS),
            bf16(3, 64, ROWS),
            f32(4, 16, 4 * D_SLICE),
            bf16(4, 16, 4 * D_SLICE),
            bf16(3, 16, 4 * D_SLICE),
            f32(4, 16, 4 * D_SLICE),
            f32(2, D_METH, E_HALF),
            f32(8, 4, 16, D_SLICE),
            dma((8,)),
            dma((8,)),
            dma((N_COPIES,)),
            dma((N_COPIES,)),
            dma((8,)),
            dma((9,)),
        ],
        compiler_params=pltpu.CompilerParams(
            collective_id=0, has_side_effects=True, vmem_limit_bytes=56 * 1024 * 1024
        ),
        cost_estimate=pl.CostEstimate(flops=19 * 10**9, bytes_accessed=8 * 10**6, transcendentals=5 * 10**6),
        name="contrastive_step",
    )(*args)


def hand_over_kernel(d_in, m_in, d_out, m_out, d_here, m_here, d_turned, in_sems, out_sems):
    m_parts = [(half, pl.ds(first, 192)) for half in range(2) for first in range(0, D_METH, 192)]
    d_parts = [slice(s * 128, (s + 1) * 128) for s in range(E // 128)]
    fetch = [(m_in.at[h, rows], m_here.at[h, rows]) for h, rows in m_parts]
    store = [(m_here.at[h, rows], m_out.at[rows, pl.ds(h * E_HALF, E_HALF)]) for h, rows in m_parts]
    fetch += [(d_in.at[rows], d_here.at[rows]) for rows in d_parts]
    store += [(d_turned.at[:, rows], d_out.at[:, rows]) for rows in d_parts]
    fetch = [pltpu.make_async_copy(*pair, in_sems.at[n]) for n, pair in enumerate(fetch)]
    store = [pltpu.make_async_copy(*pair, out_sems.at[n]) for n, pair in enumerate(store)]
    for copy in fetch:
        copy.start()
    for n in range(len(store)):
        fetch[n].wait()
        if n >= len(m_parts):
            rows = d_parts[n - len(m_parts)]
            d_turned[:, rows] = d_here[rows, :].T
        store[n].start()
    for copy in store:
        copy.wait()


def hand_over(d_part, m_part):
    hbm = pl.BlockSpec(memory_space=pltpu.HBM)
    return pl.pallas_call(
        hand_over_kernel,
        out_shape=(
            jax.ShapeDtypeStruct((D_SLICE, E), F32),
            jax.ShapeDtypeStruct((D_METH, E), F32),
        ),
        in_specs=[hbm, hbm],
        out_specs=(hbm, hbm),
        scratch_shapes=[
            pltpu.VMEM((E, D_SLICE), F32),
            pltpu.VMEM((2, D_METH, E_HALF), F32),
            pltpu.VMEM((D_SLICE, E), F32),
            pltpu.SemaphoreType.DMA((12,)),
            pltpu.SemaphoreType.DMA((12,)),
        ],
        compiler_params=pltpu.CompilerParams(vmem_limit_bytes=56 * 1024 * 1024),
        name="hand_over",
    )(d_part, m_part)


def per_device(
    dna_ids,
    meth_ids,
    pair_index,
    dna_table,
    meth_table,
    dna_proj,
    meth_proj,
    logit_scale,
    logit_bias,
):
    d_part, m_part = step_call(
        dna_ids.T,
        meth_ids.T,
        pair_index.reshape(3, 128),
        dna_table,
        meth_table,
        dna_proj,
        meth_proj,
        logit_scale,
        logit_bias,
    )
    return hand_over(d_part.reshape(E, D_SLICE), m_part)


def solution(mesh):
    placed = (
        P("blk", None),
        P("blk", None),
        P("blk"),
        P(None, "mp"),
        P(),
        P("mp", None),
        P(),
        P(),
        P(),
    )
    return jax.shard_map(
        per_device, mesh=mesh, in_specs=placed, out_specs=(P("mp", None), P()), check_vma=False
    )
```

```python
import jax
import jax.numpy as jnp
from jax import lax
from jax.experimental import pallas as pl
from jax.experimental.pallas import tpu as pltpu
from jax.sharding import PartitionSpec as P

MESH = pl.DeviceIdType.MESH
F32 = jnp.float32
BF16 = jnp.bfloat16
EPS = 1e-06

PAIR_DEV = 384
ROWS = 2 * PAIR_DEV
COLS = 8 * PAIR_DEV
E = 512
D_SLICE = 256
D_METH = 768
VOCAB_DNA = 4096
VOCAB_METH = 512
EMBED = 256
NIBBLES = 0x0F0F0F0F
LOG2E = 1.4426950408889634
E_HALF = 256
N_COPIES = 80

NT = (((1,), (1,)), ((), ()))


def place():
    blk, mp = lax.axis_index("blk"), lax.axis_index("mp")
    z = lax.div(blk, 8)
    y = lax.rem(lax.div(blk, 2), 4)
    x = lax.rem(blk, 2) * 2 + lax.div(mp, 2)
    return blk, mp, z, y, x, lax.rem(mp, 2)


def device_at(z, y, x, core):
    return (z * 8 + y * 2 + lax.div(x, 2), lax.rem(x, 2) * 2 + core)


def signal(device):
    pl.semaphore_signal(
        pltpu.get_barrier_semaphore(), inc=1, device_id=device, device_id_type=MESH
    )


def send(src, dst, send_sem, recv_sem, device):
    return pltpu.make_async_remote_copy(
        src_ref=src,
        dst_ref=dst,
        send_sem=send_sem,
        recv_sem=recv_sem,
        device_id=device,
        device_id_type=MESH,
    )


def token_counts(ids, bits, axis):
    place_of = jnp.bitwise_and(ids, 2**bits - 1)
    amount = jnp.left_shift(1, jnp.right_shift(ids, bits) * 4)
    shape = (ids.shape[0], 2**bits) if axis else (2**bits, ids.shape[1])
    spot = lax.broadcasted_iota(jnp.int32, shape, axis)
    even = odd = None
    for first in (0, 8):
        total = jnp.zeros(shape, jnp.int32)
        for t in range(first, first + 8):
            take = (slice(None), slice(t, t + 1)) if axis else (slice(t, t + 1), slice(None))
            total = total + jnp.where(spot == place_of[take], amount[take], 0)
        low = jnp.bitwise_and(total, NIBBLES)
        high = jnp.bitwise_and(jnp.right_shift(total, 4), NIBBLES)
        even, odd = (low, high) if even is None else (even + low, odd + high)
    fields = []
    for f in range(8):
        field = jnp.bitwise_and(jnp.right_shift(odd if f % 2 else even, f // 2 * 8), 255)
        fields.append(field.astype(F32).astype(BF16))
    return fields


def step_kernel(
    dna_ids_hbm,
    meth_ids_hbm,
    pairs_hbm,
    dna_table_hbm,
    meth_table_hbm,
    dna_proj_hbm,
    meth_proj_hbm,
    scale_ref,
    bias_ref,
    d_out,
    m_out,
    dna_ids,
    meth_ids,
    pairs,
    dna_proj,
    dna_table,
    meth_table,
    meth_proj,
    dna_tokens,
    ids_all,
    pair_all,
    pair_wide,
    dna_pooled,
    dna_projt,
    meth_tablet,
    meth_projt,
    meth_pooled,
    meth_unit,
    meth_rows,
    meth_inv,
    dna_unit,
    dna_inv,
    dna_rowst,
    dna_rows,
    row_acc,
    tiles,
    m_acc,
    m_low,
    m_first_in,
    m_second,
    m_second_in,
    third,
    third_in,
    third_all,
    back_all,
    back_sib,
    back_half,
    back_in,
    d_first,
    d_first_low,
    d_first_in,
    d_slab,
    m_all,
    d_fin,
    ids_send,
    ids_recv,
    send_sems,
    recv_sems,
    local_sems,
    write_sems,
):
    blk, mp, z, y, x, core = place()
    x_hi = lax.div(x, 2)
    sibling = device_at(z, y, x, 1 - core)
    ring = [device_at(z, y, lax.rem(x + o, 4), core) for o in range(4)]
    cross = [device_at(z, y, lax.rem(x + o, 4), 1 - core) for o in range(4)]
    along_y = [device_at(z, lax.rem(y + o, 4), x, core) for o in range(4)]
    cross_y = [device_at(z, lax.rem(y + o, 4), x, 1 - core) for o in range(4)]
    along_z = [device_at(lax.rem(z + o, 8), y, x, core) for o in range(8)]
    ring_place = x_hi * 4 + mp
    nearest = lax.rem(lax.div(ring_place + 1, 2), 4)

    taken = []

    def post(src, dst, device):
        n = len(taken)
        copy = send(src, dst, send_sems.at[n], recv_sems.at[n], device)
        taken.append(copy)
        return copy

    fetch = [
        pltpu.make_async_copy(src, dst, local_sems.at[1 + n])
        for n, (src, dst) in enumerate(
            (
                (dna_table_hbm, dna_table),
                (meth_table_hbm, meth_table),
                (meth_proj_hbm, meth_proj),
                (dna_ids_hbm, dna_ids),
                (meth_ids_hbm, meth_ids),
                (pairs_hbm, pairs),
                (dna_proj_hbm, dna_proj),
            )
        )
    ]
    for n in (4, 5, 6, 3, 0, 1, 2):
        fetch[n].start()

    def at_ring_place(z_of, y_of, place_of):
        return device_at(lax.rem(z_of, 8), lax.rem(y_of, 4), lax.div(place_of, 2), lax.rem(place_of, 2))

    def group(dy):
        dz = lax.rem(ring_place + 8 - 2 * dy, 8)
        return lax.rem(z + dz, 8), lax.rem(y + dy, 4)

    def source(dy, half):
        z_of, y_of = group(dy)
        return ((z_of * 4 + y_of) * 2 + half, dy)

    targets = [at_ring_place(z + 8 - s, y + 4 - mp, lax.rem(s + 2 * mp, 8)) for s in range(8)]
    sources = [source(s // 2, s % 2) for s in range(8)]

    def is_me(device):
        return jnp.logical_and(device[0] == blk, device[1] == mp)

    for s in range(8):

        @pl.when(jnp.logical_not(is_me(sources[s])))
        def _():
            signal(sources[s])

    for o in (1, 2, 3):
        signal(ring[o])
        signal(cross[o])
        signal(along_y[o])
        signal(cross_y[o])
    for o in range(1, 8):
        signal(along_z[o])
    signal(sibling)
    for n in (3, 4, 5, 6):
        fetch[n].wait()
    dna_tokens[...] = dna_ids[...].T

    def count_dna(i, carry):
        rows = pl.ds(pl.multiple_of(i * 16, 16), 16)
        fields = token_counts(dna_tokens[rows, :], 9, 1)
        for f, field in enumerate(fields):
            if f < 6:
                tiles[rows, f * 512 : (f + 1) * 512] = field
            else:
                low = pl.ds(pl.multiple_of(PAIR_DEV + i * 16, 16), 16)
                tiles[low, (f - 6) * 512 : (f - 5) * 512] = field
        return carry

    lax.fori_loop(0, PAIR_DEV // 16, count_dna, 0)
    to_self = jnp.logical_and(mp == 0, x_hi == 0).astype(jnp.int32)
    pl.semaphore_wait(pltpu.get_barrier_semaphore(), 28 - to_self)

    slot = mp * 2 + x_hi
    slot_lanes = pl.ds(pl.multiple_of(slot * PAIR_DEV, 128), PAIR_DEV)

    def ids_copy(s):
        return send(meth_ids, ids_all.at[:, slot_lanes], ids_send.at[s], ids_recv.at[slot], targets[s])

    for s in range(8):

        @pl.when(jnp.logical_not(is_me(targets[s])))
        def _():
            ids_copy(s).start()

        @pl.when(is_me(targets[s]))
        def _():
            local = pltpu.make_async_copy(meth_ids, ids_all.at[:, slot_lanes], local_sems.at[0])
            local.start()
            local.wait()

    pair_copy = post(pairs, pair_all.at[x_hi], ring[2])
    pair_copy.start()
    pair_all[x_hi] = pairs[...]

    dna_projt[:, pl.ds(pl.multiple_of(mp * D_SLICE, 128), D_SLICE)] = dna_proj[...].T
    toward = 1 + 2 * core
    far = device_at(z, y, lax.rem(x + toward, 4), core)
    other_mp = lax.rem(mp + 2, 4)

    def quarter(of):
        return dna_projt.at[:, pl.ds(pl.multiple_of(of * D_SLICE, 128), D_SLICE)]

    proj_far = post(quarter(mp), quarter(mp), far)
    proj_sib = post(quarter(mp), quarter(mp), sibling)
    proj_fwd = post(quarter(other_mp), quarter(other_mp), sibling)
    proj_far.start()
    proj_sib.start()

    fetch[0].wait()
    pooled = jnp.dot(tiles[0:PAIR_DEV, :], dna_table[0:COLS, :], preferred_element_type=F32)
    pooled = pooled + jnp.dot(
        tiles[PAIR_DEV:ROWS, 0 : VOCAB_DNA - COLS], dna_table[COLS:VOCAB_DNA, :], preferred_element_type=F32
    )
    pooled = pooled * 0.0625
    own_lanes = pl.ds(pl.multiple_of(x_hi * PAIR_DEV, 128), PAIR_DEV)
    dna_pooled[pl.ds(pl.multiple_of(mp * D_SLICE, 16), D_SLICE), own_lanes] = pooled.T.astype(BF16)

    def pool_block(x_of, core_of, low=0, count=D_SLICE):
        first = (lax.rem(x_of, 2) * 2 + core_of) * D_SLICE + low
        lanes = pl.ds(pl.multiple_of(lax.div(x_of, 2) * PAIR_DEV, 128), PAIR_DEV)
        return dna_pooled.at[pl.ds(pl.multiple_of(first, 16), count), lanes]

    own = pool_block(x, core)
    from_left = pool_block(lax.rem(x + 3, 4), core)
    from_right = pool_block(lax.rem(x + 1, 4), core)
    from_across = pool_block(lax.rem(x + 2, 4), core)
    pool_right = post(own, own, ring[1])
    pool_left = post(own, own, ring[3])
    pool_sib = post(own, own, sibling)
    pool_right.start()
    pool_left.start()
    pool_sib.start()
    half_left = pool_block(lax.rem(x + 3, 4), core, 0, 128)
    half_right = pool_block(lax.rem(x + 1, 4), core, 128, 128)
    relay_right = post(half_left, half_left, ring[1])
    relay_left = post(half_right, half_right, ring[3])
    pool_fwd = [post(part, part, sibling) for part in (from_left, from_right, from_across)]

    fetch[1].wait()
    fetch[2].wait()
    meth_tablet[...] = meth_table[...].T
    meth_projt[...] = meth_proj[...].T
    def embed_meth(i, carry):
        dy = lax.rem(nearest + i + lax.div(i, 2) * (5 - 2 * i), 4)
        for half in range(2):
            lanes = pl.ds(pl.multiple_of((dy * 2 + half) * PAIR_DEV, 128), PAIR_DEV)
            arrival = send(
                meth_ids, ids_all.at[:, lanes], ids_send.at[0], ids_recv.at[dy * 2 + half], source(dy, half)
            )

            @pl.when(jnp.logical_not(is_me(source(dy, half))))
            def _():
                arrival.wait_recv()

        for p in range(ROWS // EMBED):
            first = pl.multiple_of(dy * ROWS + p * EMBED, 128)
            lanes = pl.ds(first, EMBED)
            ids = [ids_all[:, pl.ds(pl.multiple_of(first + 128 * g, 128), 128)] for g in range(EMBED // 128)]
            tokens = jnp.concatenate(
                [jnp.concatenate(token_counts(part, 6, 0), axis=0) for part in ids], axis=1
            )
            pooled_m = jnp.dot(meth_tablet[...], tokens, preferred_element_type=F32)
            pooled_m = (pooled_m * 0.0625).astype(BF16)
            meth_pooled[:, lanes] = pooled_m
            raw = jnp.dot(meth_projt[...], pooled_m, preferred_element_type=F32)
            inverse = lax.rsqrt(jnp.sum(raw * raw, axis=0, keepdims=True) + EPS)
            unit = raw * inverse
            meth_inv[:, lanes] = inverse
            meth_unit[:, lanes] = unit
            meth_rows[:, lanes] = unit.astype(BF16)
        return carry

    lax.fori_loop(0, 2, embed_meth, 0)
    pool_right.wait_recv()
    relay_right.start()
    pool_left.wait_recv()
    relay_left.start()
    pool_fwd[0].start()
    pool_fwd[1].start()
    proj_far.wait_recv()
    proj_fwd.start()
    lax.fori_loop(2, 4, embed_meth, 0)
    relay_right.wait_recv()
    relay_left.wait_recv()
    pool_fwd[2].start()
    proj_sib.wait_recv()
    proj_fwd.wait_recv()
    pair_copy.wait_recv()
    for h in range(2):
        words = pair_all[h]
        for a in range(3):
            wide = jnp.broadcast_to(words[a : a + 1, :], (128, 128))
            first = h * PAIR_DEV + a * 128
            pair_wide[first : first + 128, :] = wide.T
    pool_sib.wait_recv()
    for copy in pool_fwd:
        copy.wait_recv()

    raw = jnp.dot(dna_projt[...], dna_pooled[...], preferred_element_type=F32)
    inverse = lax.rsqrt(jnp.sum(raw * raw, axis=0, keepdims=True) + EPS)
    unit = raw * inverse
    dna_inv[...] = inverse
    dna_unit[...] = unit
    unit_low = unit.astype(BF16)
    dna_rowst[...] = unit_low
    dna_rows[...] = unit_low.T

    scale = scale_ref[0]
    bias = bias_ref[0]
    slope, offset = scale * -LOG2E, bias * -LOG2E
    def lanes_of(c):
        return slice(c * ROWS, (c + 1) * ROWS)

    def probabilities(c, dots):
        z_of, y_of = group(c)
        partner = pair_wide[...] - (z_of * 4 + y_of) * ROWS
        lower = 1.0 + jnp.exp2(slope * dots + offset)
        prob = pl.reciprocal(lower, approx=True)
        prob = prob * (2.0 - lower * prob)
        for g in range(ROWS // 128):
            part = prob[:, g * 128 : (g + 1) * 128]
            lane = lax.broadcasted_iota(jnp.int32, (ROWS, 128), 1) + g * 128
            first = c * ROWS + g * 128
            tiles[:, first : first + 128] = jnp.where(partner == lane, part - 1.0, part).astype(BF16)

    def back_of(c, col_dots):
        up = scale * col_dots
        unit_m = meth_unit[:, lanes_of(c)]
        inner = jnp.sum(unit_m * up, axis=0, keepdims=True)
        return (meth_inv[:, lanes_of(c)] * (up - unit_m * inner)).astype(BF16)

    def add_head(c, back):
        part = lax.dot_general(meth_pooled[:, lanes_of(c)], back, NT, preferred_element_type=F32)
        m_acc[...] = part if c == 0 else m_acc[...] + part

    last = COLS // ROWS - 1
    for c in range(last + 1):
        rows_m = meth_rows[:, lanes_of(c)]
        dots = jnp.dot(dna_rows[...], rows_m, preferred_element_type=F32)
        if c > 0:
            col_dots = jnp.dot(dna_rowst[...], tiles[:, lanes_of(c - 1)], preferred_element_type=F32)
        probabilities(c, dots)
        if c > 0:
            add_head(c - 1, back_of(c - 1, col_dots))
        part = lax.dot_general(rows_m, tiles[:, lanes_of(c)], NT, preferred_element_type=F32)
        row_acc[...] = part if c == 0 else row_acc[...] + part

    other = 1 - core
    up = scale * row_acc[...]
    inner = jnp.sum(dna_unit[...] * up, axis=0, keepdims=True)
    back_all[...] = (dna_inv[...] * (up - dna_unit[...] * inner)).astype(BF16)
    back_swap = post(back_all.at[pl.ds(pl.multiple_of(other * 256, 16), 256)], back_sib, sibling)
    back_swap.start()

    col_dots = jnp.dot(dna_rowst[...], tiles[:, lanes_of(last)], preferred_element_type=F32)
    add_head(last, back_of(last, col_dots))

    back_swap.wait_recv()
    for a in range(4):
        rows = pl.ds(pl.multiple_of(core * 256 + a * 64, 16), 64)
        both = back_all[rows, :].astype(F32) + back_sib[a * 64 : (a + 1) * 64, :].astype(F32)
        back_half[a] = both.astype(BF16)
    back_x = [post(back_half.at[lax.rem(x + o, 4)], back_in.at[o - 1], ring[o]) for o in (1, 2, 3)]
    for copy in back_x:
        copy.start()
    swap = core == 1

    def pick(one, two):
        return tuple(jnp.where(swap, q, p) for p, q in zip(one, two))

    axis_a = [pick(p, q) for p, q in zip(ring, along_y)]
    axis_b = [pick(q, p) for p, q in zip(ring, along_y)]
    cross_a = [pick(q, p) for p, q in zip(cross, cross_y)]
    at_a = jnp.where(swap, y, x)
    at_b = jnp.where(swap, x, y)
    at_cross = jnp.where(swap, x, y)

    def block_rows(which, a, b):
        return pl.ds(pl.multiple_of(jnp.where(which == 1, a * 192 + b * 48, b * 192 + a * 48), 16), 48)

    def half_lanes(which):
        return pl.ds(pl.multiple_of(which * E_HALF, 128), E_HALF)

    def pack(which):
        def pack_block(i, carry):
            a, b = lax.div(i, 4), lax.rem(i, 4)
            m_low[which, a, b] = m_acc[block_rows(which, a, b), half_lanes(which)].astype(BF16)
            return carry

        lax.fori_loop(0, 16, pack_block, 0)

    pack(other)
    m_a = [
        post(m_low.at[other, lax.rem(at_cross + o, 4)], m_first_in.at[3 + o], sibling if o == 0 else cross_a[o])
        for o in range(4)
    ]
    for copy in m_a:
        copy.start()
    pack(core)
    m_own = [post(m_low.at[core, lax.rem(at_a + o, 4)], m_first_in.at[o - 1], axis_a[o]) for o in (1, 2, 3)]
    for copy in m_own:
        copy.start()
    m_a = m_a + m_own

    for copy in back_x:
        copy.wait_recv()
    back = back_half[x].astype(F32)
    for o in range(3):
        back = back + back_in[o].astype(F32)
    back = back.astype(BF16)
    for s in range(4):
        features = dna_pooled[s * D_SLICE : (s + 1) * D_SLICE, :]
        part = lax.dot_general(back, features, NT, preferred_element_type=F32)
        for a in range(4):
            d_first[a, :, s * D_SLICE : (s + 1) * D_SLICE] = part[a * 16 : (a + 1) * 16, :]
            d_first_low[a, :, s * D_SLICE : (s + 1) * D_SLICE] = part[a * 16 : (a + 1) * 16, :].astype(BF16)
    d_y = [post(d_first_low.at[lax.rem(y + o, 4)], d_first_in.at[o - 1], along_y[o]) for o in (1, 2, 3)]
    for copy in d_y:
        copy.start()

    for copy in d_y:
        copy.wait_recv()
    d_sum = d_first[y]
    for o in range(3):
        d_sum = d_sum + d_first_in[o].astype(F32)
    for s in range(8):
        third[s, 1] = d_sum[:, s * 128 : (s + 1) * 128]

    for copy in m_a:
        copy.wait_recv()
    for b in range(4):
        part = m_acc[block_rows(core, at_a, b), half_lanes(core)]
        for o in range(7):
            part = part + m_first_in[o, b].astype(F32)
        m_second[b] = part
    m_b = [post(m_second.at[lax.rem(at_b + o, 4)], m_second_in.at[o - 1], axis_b[o]) for o in (1, 2, 3)]
    for copy in m_b:
        copy.start()
    for copy in m_b:
        copy.wait_recv()
    m_sum = m_second[at_b]
    for o in range(3):
        m_sum = m_sum + m_second_in[o]
    for s in range(6):
        third[s, 0] = m_sum[s // 2 * 16 : s // 2 * 16 + 16, s % 2 * 128 : s % 2 * 128 + 128]
    third[6, 0] = jnp.zeros((16, 128), F32)
    third[7, 0] = jnp.zeros((16, 128), F32)

    z_sum = [post(third.at[lax.rem(z + o, 8)], third_in.at[o - 1], along_z[o]) for o in range(1, 8)]
    for copy in z_sum:
        copy.start()
    for copy in z_sum:
        copy.wait_recv()
    total = third[z]
    for o in range(7):
        total = total + third_in[o]
    third_all[z] = total
    z_back = [post(third_all.at[z], third_all.at[z], along_z[o]) for o in range(1, 8)]
    for copy in z_back:
        copy.start()
    for copy in z_back:
        copy.wait_recv()

    for s in range(8):
        d_slab[y, :, s * 128 : (s + 1) * 128] = third_all[s, 1]
    d_back = [post(d_slab.at[y], d_slab.at[y], along_y[o]) for o in (1, 2, 3)]
    for copy in d_back:
        copy.start()

    def rows_at(y_of, low, rows):
        return m_all.at[core, pl.ds(pl.multiple_of(lax.rem(y_of, 4) * 192 + low, 16), rows)]

    def to(part, device):
        copy = post(part, part, device)
        copy.start()
        return copy

    sub = y * 192 + x * 48
    for s in range(6):
        rows = pl.ds(pl.multiple_of(sub + s // 2 * 16, 16), 16)
        m_all[core, rows, s % 2 * 128 : s % 2 * 128 + 128] = third_all[s, 0]
    own_block = m_all.at[core, pl.ds(pl.multiple_of(sub, 16), 48)]
    m_back_x = [to(own_block, ring[o]) for o in (1, 2, 3)]
    for copy in m_back_x:
        copy.wait_recv()
    own_band = rows_at(y, 0, 192)
    up_copy = to(own_band, along_y[1])
    down_copy = to(own_band, along_y[3])
    m_last = [to(own_band, sibling)]

    for copy in d_back:
        copy.wait_recv()
    eighth = core * 4 + x

    def slice_for(device):
        return d_slab.at[:, :, pl.ds(pl.multiple_of(device[1] * D_SLICE, 128), D_SLICE)]

    d_ring = [post(slice_for(device), d_fin.at[eighth], device) for device in ring[1:] + cross[1:] + [sibling]]
    for copy in d_ring:
        copy.start()
    d_fin[eighth] = d_slab[:, :, pl.ds(pl.multiple_of(mp * D_SLICE, 128), D_SLICE)]

    written = []

    def write(src, dst):
        copy = pltpu.make_async_copy(src, dst, write_sems.at[len(written)])
        copy.start()
        written.append(copy)

    def write_band(y_of, half):
        rows = pl.ds(pl.multiple_of(lax.rem(y_of, 4) * 192, 16), 192)
        write(m_all.at[half, rows], m_out.at[half, rows])

    write_band(y, core)
    up_copy.wait_recv()
    relay_up = to(rows_at(y + 3, 0, 96), along_y[1])
    m_last.append(to(rows_at(y + 3, 0, 192), sibling))
    down_copy.wait_recv()
    relay_down = to(rows_at(y + 1, 96, 96), along_y[3])
    m_last.append(to(rows_at(y + 1, 0, 192), sibling))
    write_band(y + 3, core)
    write_band(y + 1, core)
    for copy in d_ring:
        copy.wait_recv()
    write(d_fin, d_out)
    relay_up.wait_recv()
    relay_down.wait_recv()
    m_last.append(to(rows_at(y + 2, 0, 192), sibling))
    write_band(y + 2, core)
    for copy, o in zip(m_last, (0, 3, 1, 2)):
        copy.wait_recv()
        write_band(y + o, other)
    for copy in written:
        copy.wait()

    for s in range(8):

        @pl.when(jnp.logical_not(is_me(targets[s])))
        def _():
            ids_copy(s).wait_send()

    for copy in taken:
        copy.wait_send()


def step_call(*args):
    vmem = pl.BlockSpec(memory_space=pltpu.VMEM)
    smem = pl.BlockSpec(memory_space=pltpu.SMEM)
    hbm = pl.BlockSpec(memory_space=pltpu.HBM)
    dma = pltpu.SemaphoreType.DMA
    f32 = lambda *shape: pltpu.VMEM(shape, F32)
    bf16 = lambda *shape: pltpu.VMEM(shape, BF16)
    i32 = lambda *shape: pltpu.VMEM(shape, jnp.int32)
    return pl.pallas_call(
        step_kernel,
        out_shape=(
            jax.ShapeDtypeStruct((8, 4, 16, D_SLICE), F32),
            jax.ShapeDtypeStruct((2, D_METH, E_HALF), F32),
        ),
        in_specs=[hbm] * 7 + [smem] * 2,
        out_specs=(hbm, hbm),
        scratch_shapes=[
            i32(16, PAIR_DEV),
            i32(16, PAIR_DEV),
            i32(3, 128),
            bf16(D_SLICE, E),
            bf16(VOCAB_DNA, D_SLICE),
            bf16(VOCAB_METH, D_METH),
            bf16(D_METH, E),
            i32(PAIR_DEV, 16),
            i32(16, COLS),
            i32(2, 3, 128),
            i32(ROWS, 128),
            bf16(4 * D_SLICE, ROWS),
            bf16(E, 4 * D_SLICE),
            bf16(D_METH, VOCAB_METH),
            bf16(E, D_METH),
            bf16(D_METH, COLS),
            f32(E, COLS),
            bf16(E, COLS),
            f32(1, COLS),
            f32(E, ROWS),
            f32(1, ROWS),
            bf16(E, ROWS),
            bf16(ROWS, E),
            f32(E, ROWS),
            bf16(ROWS, COLS),
            f32(D_METH, E),
            bf16(2, 4, 4, 48, E_HALF),
            bf16(7, 4, 48, E_HALF),
            f32(4, 48, E_HALF),
            f32(3, 48, E_HALF),
            f32(8, 2, 16, 128),
            f32(7, 2, 16, 128),
            f32(8, 2, 16, 128),
            bf16(E, ROWS),
            bf16(256, ROWS),
            bf16(4, 64, ROWS),
            bf16(3, 64, ROWS),
            f32(4, 16, 4 * D_SLICE),
            bf16(4, 16, 4 * D_SLICE),
            bf16(3, 16, 4 * D_SLICE),
            f32(4, 16, 4 * D_SLICE),
            f32(2, D_METH, E_HALF),
            f32(8, 4, 16, D_SLICE),
            dma((8,)),
            dma((8,)),
            dma((N_COPIES,)),
            dma((N_COPIES,)),
            dma((8,)),
            dma((9,)),
        ],
        compiler_params=pltpu.CompilerParams(
            collective_id=0, has_side_effects=True, vmem_limit_bytes=56 * 1024 * 1024
        ),
        cost_estimate=pl.CostEstimate(flops=19 * 10**9, bytes_accessed=8 * 10**6, transcendentals=5 * 10**6),
        name="contrastive_step",
    )(*args)


def hand_over_kernel(d_in, m_in, d_out, m_out, d_here, m_here, d_turned, in_sems, out_sems):
    m_parts = [(half, pl.ds(first, 192)) for half in range(2) for first in range(0, D_METH, 192)]
    d_parts = [slice(s * 128, (s + 1) * 128) for s in range(E // 128)]
    fetch = [(m_in.at[h, rows], m_here.at[h, rows]) for h, rows in m_parts]
    store = [(m_here.at[h, rows], m_out.at[rows, pl.ds(h * E_HALF, E_HALF)]) for h, rows in m_parts]
    fetch += [(d_in.at[rows], d_here.at[rows]) for rows in d_parts]
    store += [(d_turned.at[:, rows], d_out.at[:, rows]) for rows in d_parts]
    fetch = [pltpu.make_async_copy(*pair, in_sems.at[n]) for n, pair in enumerate(fetch)]
    store = [pltpu.make_async_copy(*pair, out_sems.at[n]) for n, pair in enumerate(store)]
    for copy in fetch:
        copy.start()
    for n in range(len(store)):
        fetch[n].wait()
        if n >= len(m_parts):
            rows = d_parts[n - len(m_parts)]
            d_turned[:, rows] = d_here[rows, :].T
        store[n].start()
    for copy in store:
        copy.wait()


def hand_over(d_part, m_part):
    hbm = pl.BlockSpec(memory_space=pltpu.HBM)
    return pl.pallas_call(
        hand_over_kernel,
        out_shape=(
            jax.ShapeDtypeStruct((D_SLICE, E), F32),
            jax.ShapeDtypeStruct((D_METH, E), F32),
        ),
        in_specs=[hbm, hbm],
        out_specs=(hbm, hbm),
        scratch_shapes=[
            pltpu.VMEM((E, D_SLICE), F32),
            pltpu.VMEM((2, D_METH, E_HALF), F32),
            pltpu.VMEM((D_SLICE, E), F32),
            pltpu.SemaphoreType.DMA((12,)),
            pltpu.SemaphoreType.DMA((12,)),
        ],
        compiler_params=pltpu.CompilerParams(vmem_limit_bytes=56 * 1024 * 1024),
        name="hand_over",
    )(d_part, m_part)


def per_device(
    dna_ids,
    meth_ids,
    pair_index,
    dna_table,
    meth_table,
    dna_proj,
    meth_proj,
    logit_scale,
    logit_bias,
):
    d_part, m_part = step_call(
        dna_ids.T,
        meth_ids.T,
        pair_index.reshape(3, 128),
        dna_table,
        meth_table,
        dna_proj,
        meth_proj,
        logit_scale,
        logit_bias,
    )
    return hand_over(d_part.reshape(E, D_SLICE), m_part)


def solution(mesh):
    placed = (
        P("blk", None),
        P("blk", None),
        P("blk"),
        P(None, "mp"),
        P(),
        P("mp", None),
        P(),
        P(),
        P(),
    )
    return jax.shard_map(
        per_device, mesh=mesh, in_specs=placed, out_specs=(P("mp", None), P()), check_vma=False
    )
```

```python
import jax
import jax.numpy as jnp
from jax import lax
from jax.experimental import pallas as pl
from jax.experimental.pallas import tpu as pltpu
from jax.sharding import PartitionSpec as P

MESH = pl.DeviceIdType.MESH
F32 = jnp.float32
BF16 = jnp.bfloat16
EPS = 1e-06

PAIR_DEV = 384
ROWS = 2 * PAIR_DEV
COLS = 8 * PAIR_DEV
E = 512
D_SLICE = 256
D_METH = 768
VOCAB_DNA = 4096
VOCAB_METH = 512
EMBED = 256
NIBBLES = 0x0F0F0F0F
LOG2E = 1.4426950408889634
E_HALF = 256
N_COPIES = 80

NT = (((1,), (1,)), ((), ()))


def place():
    blk, mp = lax.axis_index("blk"), lax.axis_index("mp")
    z = lax.div(blk, 8)
    y = lax.rem(lax.div(blk, 2), 4)
    x = lax.rem(blk, 2) * 2 + lax.div(mp, 2)
    return blk, mp, z, y, x, lax.rem(mp, 2)


def device_at(z, y, x, core):
    return (z * 8 + y * 2 + lax.div(x, 2), lax.rem(x, 2) * 2 + core)


def signal(device):
    pl.semaphore_signal(
        pltpu.get_barrier_semaphore(), inc=1, device_id=device, device_id_type=MESH
    )


def send(src, dst, send_sem, recv_sem, device):
    return pltpu.make_async_remote_copy(
        src_ref=src,
        dst_ref=dst,
        send_sem=send_sem,
        recv_sem=recv_sem,
        device_id=device,
        device_id_type=MESH,
    )


def token_counts(ids, bits, axis):
    place_of = jnp.bitwise_and(ids, 2**bits - 1)
    amount = jnp.left_shift(1, jnp.right_shift(ids, bits) * 4)
    shape = (ids.shape[0], 2**bits) if axis else (2**bits, ids.shape[1])
    spot = lax.broadcasted_iota(jnp.int32, shape, axis)
    even = odd = None
    for first in (0, 8):
        total = jnp.zeros(shape, jnp.int32)
        for t in range(first, first + 8):
            take = (slice(None), slice(t, t + 1)) if axis else (slice(t, t + 1), slice(None))
            total = total + jnp.where(spot == place_of[take], amount[take], 0)
        low = jnp.bitwise_and(total, NIBBLES)
        high = jnp.bitwise_and(jnp.right_shift(total, 4), NIBBLES)
        even, odd = (low, high) if even is None else (even + low, odd + high)
    fields = []
    for f in range(8):
        field = jnp.bitwise_and(jnp.right_shift(odd if f % 2 else even, f // 2 * 8), 255)
        fields.append(field.astype(F32).astype(BF16))
    return fields


def step_kernel(
    dna_ids_hbm,
    meth_ids_hbm,
    pairs_hbm,
    dna_table_hbm,
    meth_table_hbm,
    dna_proj_hbm,
    meth_proj_hbm,
    scale_ref,
    bias_ref,
    d_out,
    m_out,
    dna_ids,
    meth_ids,
    pairs,
    dna_proj,
    dna_table,
    meth_table,
    meth_proj,
    dna_tokens,
    ids_all,
    pair_all,
    pair_wide,
    dna_pooled,
    dna_projt,
    meth_tablet,
    meth_projt,
    meth_pooled,
    meth_unit,
    meth_rows,
    meth_inv,
    dna_unit,
    dna_inv,
    dna_rowst,
    dna_rows,
    row_acc,
    tiles,
    m_acc,
    m_low,
    m_first_in,
    m_second,
    m_second_in,
    third,
    third_in,
    third_all,
    back_all,
    back_sib,
    back_half,
    back_in,
    d_first,
    d_first_low,
    d_first_in,
    d_slab,
    m_all,
    d_fin,
    ids_send,
    ids_recv,
    send_sems,
    recv_sems,
    local_sems,
    write_sems,
):
    blk, mp, z, y, x, core = place()
    x_hi = lax.div(x, 2)
    sibling = device_at(z, y, x, 1 - core)
    ring = [device_at(z, y, lax.rem(x + o, 4), core) for o in range(4)]
    cross = [device_at(z, y, lax.rem(x + o, 4), 1 - core) for o in range(4)]
    along_y = [device_at(z, lax.rem(y + o, 4), x, core) for o in range(4)]
    cross_y = [device_at(z, lax.rem(y + o, 4), x, 1 - core) for o in range(4)]
    along_z = [device_at(lax.rem(z + o, 8), y, x, core) for o in range(8)]
    ring_place = x_hi * 4 + mp
    nearest = lax.rem(lax.div(ring_place + 1, 2), 4)

    taken = []

    def post(src, dst, device):
        n = len(taken)
        copy = send(src, dst, send_sems.at[n], recv_sems.at[n], device)
        taken.append(copy)
        return copy

    fetch = [
        pltpu.make_async_copy(src, dst, local_sems.at[1 + n])
        for n, (src, dst) in enumerate(
            (
                (dna_table_hbm, dna_table),
                (meth_table_hbm, meth_table),
                (meth_proj_hbm, meth_proj),
                (dna_ids_hbm, dna_ids),
                (meth_ids_hbm, meth_ids),
                (pairs_hbm, pairs),
                (dna_proj_hbm, dna_proj),
            )
        )
    ]
    for n in (4, 5, 6, 3, 0, 1, 2):
        fetch[n].start()

    def at_ring_place(z_of, y_of, place_of):
        return device_at(lax.rem(z_of, 8), lax.rem(y_of, 4), lax.div(place_of, 2), lax.rem(place_of, 2))

    def group(dy):
        dz = lax.rem(ring_place + 8 - 2 * dy, 8)
        return lax.rem(z + dz, 8), lax.rem(y + dy, 4)

    def source(dy, half):
        z_of, y_of = group(dy)
        return ((z_of * 4 + y_of) * 2 + half, dy)

    targets = [at_ring_place(z + 8 - s, y + 4 - mp, lax.rem(s + 2 * mp, 8)) for s in range(8)]
    sources = [source(s // 2, s % 2) for s in range(8)]

    def is_me(device):
        return jnp.logical_and(device[0] == blk, device[1] == mp)

    for s in range(8):

        @pl.when(jnp.logical_not(is_me(sources[s])))
        def _():
            signal(sources[s])

    for o in (1, 2, 3):
        signal(ring[o])
        signal(cross[o])
        signal(along_y[o])
        signal(cross_y[o])
    for o in range(1, 8):
        signal(along_z[o])
    signal(sibling)
    for n in (3, 4, 5, 6):
        fetch[n].wait()
    dna_tokens[...] = dna_ids[...].T

    def count_dna(i, carry):
        rows = pl.ds(pl.multiple_of(i * 16, 16), 16)
        fields = token_counts(dna_tokens[rows, :], 9, 1)
        for f, field in enumerate(fields):
            if f < 6:
                tiles[rows, f * 512 : (f + 1) * 512] = field
            else:
                low = pl.ds(pl.multiple_of(PAIR_DEV + i * 16, 16), 16)
                tiles[low, (f - 6) * 512 : (f - 5) * 512] = field
        return carry

    lax.fori_loop(0, PAIR_DEV // 16, count_dna, 0)
    to_self = jnp.logical_and(mp == 0, x_hi == 0).astype(jnp.int32)
    pl.semaphore_wait(pltpu.get_barrier_semaphore(), 28 - to_self)

    slot = mp * 2 + x_hi
    slot_lanes = pl.ds(pl.multiple_of(slot * PAIR_DEV, 128), PAIR_DEV)

    def ids_copy(s):
        return send(meth_ids, ids_all.at[:, slot_lanes], ids_send.at[s], ids_recv.at[slot], targets[s])

    for s in range(8):

        @pl.when(jnp.logical_not(is_me(targets[s])))
        def _():
            ids_copy(s).start()

        @pl.when(is_me(targets[s]))
        def _():
            local = pltpu.make_async_copy(meth_ids, ids_all.at[:, slot_lanes], local_sems.at[0])
            local.start()
            local.wait()

    pair_copy = post(pairs, pair_all.at[x_hi], ring[2])
    pair_copy.start()
    pair_all[x_hi] = pairs[...]

    dna_projt[:, pl.ds(pl.multiple_of(mp * D_SLICE, 128), D_SLICE)] = dna_proj[...].T
    toward = 1 + 2 * core
    far = device_at(z, y, lax.rem(x + toward, 4), core)
    other_mp = lax.rem(mp + 2, 4)

    def quarter(of):
        return dna_projt.at[:, pl.ds(pl.multiple_of(of * D_SLICE, 128), D_SLICE)]

    proj_far = post(quarter(mp), quarter(mp), far)
    proj_sib = post(quarter(mp), quarter(mp), sibling)
    proj_fwd = post(quarter(other_mp), quarter(other_mp), sibling)
    proj_far.start()
    proj_sib.start()

    fetch[0].wait()
    pooled = jnp.dot(tiles[0:PAIR_DEV, :], dna_table[0:COLS, :], preferred_element_type=F32)
    pooled = pooled + jnp.dot(
        tiles[PAIR_DEV:ROWS, 0 : VOCAB_DNA - COLS], dna_table[COLS:VOCAB_DNA, :], preferred_element_type=F32
    )
    pooled = pooled * 0.0625
    own_lanes = pl.ds(pl.multiple_of(x_hi * PAIR_DEV, 128), PAIR_DEV)
    dna_pooled[pl.ds(pl.multiple_of(mp * D_SLICE, 16), D_SLICE), own_lanes] = pooled.T.astype(BF16)

    def pool_block(x_of, core_of, low=0, count=D_SLICE):
        first = (lax.rem(x_of, 2) * 2 + core_of) * D_SLICE + low
        lanes = pl.ds(pl.multiple_of(lax.div(x_of, 2) * PAIR_DEV, 128), PAIR_DEV)
        return dna_pooled.at[pl.ds(pl.multiple_of(first, 16), count), lanes]

    own = pool_block(x, core)
    from_left = pool_block(lax.rem(x + 3, 4), core)
    from_right = pool_block(lax.rem(x + 1, 4), core)
    pool_right = post(own, own, ring[1])
    pool_left = post(own, own, ring[3])
    pool_sib = post(own, own, sibling)
    pool_right.start()
    pool_left.start()
    pool_sib.start()
    half_left = pool_block(lax.rem(x + 3, 4), core, 0, 128)
    half_right = pool_block(lax.rem(x + 1, 4), core, 128, 128)
    relay_right = [post(half_left, half_left, device) for device in (ring[1], cross[1])]
    relay_left = [post(half_right, half_right, device) for device in (ring[3], cross[3])]
    pool_fwd = [post(part, part, sibling) for part in (from_left, from_right)]

    fetch[1].wait()
    fetch[2].wait()
    meth_tablet[...] = meth_table[...].T
    meth_projt[...] = meth_proj[...].T
    def embed_meth(i, carry):
        dy = lax.rem(nearest + i + lax.div(i, 2) * (5 - 2 * i), 4)
        for half in range(2):
            lanes = pl.ds(pl.multiple_of((dy * 2 + half) * PAIR_DEV, 128), PAIR_DEV)
            arrival = send(
                meth_ids, ids_all.at[:, lanes], ids_send.at[0], ids_recv.at[dy * 2 + half], source(dy, half)
            )

            @pl.when(jnp.logical_not(is_me(source(dy, half))))
            def _():
                arrival.wait_recv()

        for p in range(ROWS // EMBED):
            first = pl.multiple_of(dy * ROWS + p * EMBED, 128)
            lanes = pl.ds(first, EMBED)
            ids = [ids_all[:, pl.ds(pl.multiple_of(first + 128 * g, 128), 128)] for g in range(EMBED // 128)]
            tokens = jnp.concatenate(
                [jnp.concatenate(token_counts(part, 6, 0), axis=0) for part in ids], axis=1
            )
            pooled_m = jnp.dot(meth_tablet[...], tokens, preferred_element_type=F32)
            pooled_m = (pooled_m * 0.0625).astype(BF16)
            meth_pooled[:, lanes] = pooled_m
            raw = jnp.dot(meth_projt[...], pooled_m, preferred_element_type=F32)
            inverse = lax.rsqrt(jnp.sum(raw * raw, axis=0, keepdims=True) + EPS)
            unit = raw * inverse
            meth_inv[:, lanes] = inverse
            meth_unit[:, lanes] = unit
            meth_rows[:, lanes] = unit.astype(BF16)
        return carry

    lax.fori_loop(0, 2, embed_meth, 0)
    pool_right.wait_recv()
    for copy in relay_right:
        copy.start()
    pool_left.wait_recv()
    for copy in relay_left:
        copy.start()
    pool_fwd[0].start()
    pool_fwd[1].start()
    proj_far.wait_recv()
    proj_fwd.start()
    lax.fori_loop(2, 4, embed_meth, 0)
    for copy in relay_right + relay_left:
        copy.wait_recv()
    proj_sib.wait_recv()
    proj_fwd.wait_recv()
    pair_copy.wait_recv()
    for h in range(2):
        words = pair_all[h]
        for a in range(3):
            wide = jnp.broadcast_to(words[a : a + 1, :], (128, 128))
            first = h * PAIR_DEV + a * 128
            pair_wide[first : first + 128, :] = wide.T
    pool_sib.wait_recv()
    for copy in pool_fwd:
        copy.wait_recv()

    raw = jnp.dot(dna_projt[...], dna_pooled[...], preferred_element_type=F32)
    inverse = lax.rsqrt(jnp.sum(raw * raw, axis=0, keepdims=True) + EPS)
    unit = raw * inverse
    dna_inv[...] = inverse
    dna_unit[...] = unit
    unit_low = unit.astype(BF16)
    dna_rowst[...] = unit_low
    dna_rows[...] = unit_low.T

    scale = scale_ref[0]
    bias = bias_ref[0]
    slope, offset = scale * -LOG2E, bias * -LOG2E
    def lanes_of(c):
        return slice(c * ROWS, (c + 1) * ROWS)

    def probabilities(c, dots):
        z_of, y_of = group(c)
        partner = pair_wide[...] - (z_of * 4 + y_of) * ROWS
        lower = 1.0 + jnp.exp2(slope * dots + offset)
        prob = pl.reciprocal(lower, approx=True)
        prob = prob * (2.0 - lower * prob)
        for g in range(ROWS // 128):
            part = prob[:, g * 128 : (g + 1) * 128]
            lane = lax.broadcasted_iota(jnp.int32, (ROWS, 128), 1) + g * 128
            first = c * ROWS + g * 128
            tiles[:, first : first + 128] = jnp.where(partner == lane, part - 1.0, part).astype(BF16)

    def back_of(c, col_dots):
        up = scale * col_dots
        unit_m = meth_unit[:, lanes_of(c)]
        inner = jnp.sum(unit_m * up, axis=0, keepdims=True)
        return (meth_inv[:, lanes_of(c)] * (up - unit_m * inner)).astype(BF16)

    def add_head(c, back):
        part = lax.dot_general(meth_pooled[:, lanes_of(c)], back, NT, preferred_element_type=F32)
        m_acc[...] = part if c == 0 else m_acc[...] + part

    last = COLS // ROWS - 1
    for c in range(last + 1):
        rows_m = meth_rows[:, lanes_of(c)]
        dots = jnp.dot(dna_rows[...], rows_m, preferred_element_type=F32)
        if c > 0:
            col_dots = jnp.dot(dna_rowst[...], tiles[:, lanes_of(c - 1)], preferred_element_type=F32)
        probabilities(c, dots)
        if c > 0:
            add_head(c - 1, back_of(c - 1, col_dots))
        part = lax.dot_general(rows_m, tiles[:, lanes_of(c)], NT, preferred_element_type=F32)
        row_acc[...] = part if c == 0 else row_acc[...] + part

    other = 1 - core
    up = scale * row_acc[...]
    inner = jnp.sum(dna_unit[...] * up, axis=0, keepdims=True)
    back_all[...] = (dna_inv[...] * (up - dna_unit[...] * inner)).astype(BF16)
    back_swap = post(back_all.at[pl.ds(pl.multiple_of(other * 256, 16), 256)], back_sib, sibling)
    back_swap.start()

    col_dots = jnp.dot(dna_rowst[...], tiles[:, lanes_of(last)], preferred_element_type=F32)
    add_head(last, back_of(last, col_dots))

    back_swap.wait_recv()
    for a in range(4):
        rows = pl.ds(pl.multiple_of(core * 256 + a * 64, 16), 64)
        both = back_all[rows, :].astype(F32) + back_sib[a * 64 : (a + 1) * 64, :].astype(F32)
        back_half[a] = both.astype(BF16)
    back_x = [post(back_half.at[lax.rem(x + o, 4)], back_in.at[o - 1], ring[o]) for o in (1, 2, 3)]
    for copy in back_x:
        copy.start()
    swap = core == 1

    def pick(one, two):
        return tuple(jnp.where(swap, q, p) for p, q in zip(one, two))

    axis_a = [pick(p, q) for p, q in zip(ring, along_y)]
    axis_b = [pick(q, p) for p, q in zip(ring, along_y)]
    cross_a = [pick(q, p) for p, q in zip(cross, cross_y)]
    at_a = jnp.where(swap, y, x)
    at_b = jnp.where(swap, x, y)
    at_cross = jnp.where(swap, x, y)

    def block_rows(which, a, b):
        return pl.ds(pl.multiple_of(jnp.where(which == 1, a * 192 + b * 48, b * 192 + a * 48), 16), 48)

    def half_lanes(which):
        return pl.ds(pl.multiple_of(which * E_HALF, 128), E_HALF)

    def pack(which):
        def pack_block(i, carry):
            a, b = lax.div(i, 4), lax.rem(i, 4)
            m_low[which, a, b] = m_acc[block_rows(which, a, b), half_lanes(which)].astype(BF16)
            return carry

        lax.fori_loop(0, 16, pack_block, 0)

    pack(other)
    m_a = [
        post(m_low.at[other, lax.rem(at_cross + o, 4)], m_first_in.at[3 + o], sibling if o == 0 else cross_a[o])
        for o in range(4)
    ]
    for copy in m_a:
        copy.start()
    pack(core)
    m_own = [post(m_low.at[core, lax.rem(at_a + o, 4)], m_first_in.at[o - 1], axis_a[o]) for o in (1, 2, 3)]
    for copy in m_own:
        copy.start()
    m_a = m_a + m_own

    for copy in back_x:
        copy.wait_recv()
    back = back_half[x].astype(F32)
    for o in range(3):
        back = back + back_in[o].astype(F32)
    back = back.astype(BF16)
    wide = jnp.concatenate([back, back], axis=0)
    part = lax.dot_general(dna_pooled[...], wide, NT, preferred_element_type=F32).T
    for a in range(4):
        d_first[a] = part[a * 16 : (a + 1) * 16, :]
        d_first_low[a] = part[a * 16 : (a + 1) * 16, :].astype(BF16)
    d_y = [post(d_first_low.at[lax.rem(y + o, 4)], d_first_in.at[o - 1], along_y[o]) for o in (1, 2, 3)]
    for copy in d_y:
        copy.start()

    for copy in d_y:
        copy.wait_recv()
    d_sum = d_first[y]
    for o in range(3):
        d_sum = d_sum + d_first_in[o].astype(F32)
    for s in range(8):
        third[s, 1] = d_sum[:, s * 128 : (s + 1) * 128]

    for copy in m_a:
        copy.wait_recv()
    for b in range(4):
        part = m_acc[block_rows(core, at_a, b), half_lanes(core)]
        for o in range(7):
            part = part + m_first_in[o, b].astype(F32)
        m_second[b] = part
    m_b = [post(m_second.at[lax.rem(at_b + o, 4)], m_second_in.at[o - 1], axis_b[o]) for o in (1, 2, 3)]
    for copy in m_b:
        copy.start()
    for copy in m_b:
        copy.wait_recv()
    m_sum = m_second[at_b]
    for o in range(3):
        m_sum = m_sum + m_second_in[o]
    for s in range(6):
        third[s, 0] = m_sum[s // 2 * 16 : s // 2 * 16 + 16, s % 2 * 128 : s % 2 * 128 + 128]
    third[6, 0] = jnp.zeros((16, 128), F32)
    third[7, 0] = jnp.zeros((16, 128), F32)

    z_sum = [post(third.at[lax.rem(z + o, 8)], third_in.at[o - 1], along_z[o]) for o in range(1, 8)]
    for copy in z_sum:
        copy.start()
    for copy in z_sum:
        copy.wait_recv()
    total = third[z]
    for o in range(7):
        total = total + third_in[o]
    third_all[z] = total
    z_back = [post(third_all.at[z], third_all.at[z], along_z[o]) for o in range(1, 8)]
    for copy in z_back:
        copy.start()
    for copy in z_back:
        copy.wait_recv()

    for s in range(8):
        d_slab[y, :, s * 128 : (s + 1) * 128] = third_all[s, 1]
    d_back = [post(d_slab.at[y], d_slab.at[y], along_y[o]) for o in (1, 2, 3)]
    for copy in d_back:
        copy.start()

    def rows_at(y_of, low, rows):
        return m_all.at[core, pl.ds(pl.multiple_of(lax.rem(y_of, 4) * 192 + low, 16), rows)]

    def to(part, device):
        copy = post(part, part, device)
        copy.start()
        return copy

    sub = y * 192 + x * 48
    for s in range(6):
        rows = pl.ds(pl.multiple_of(sub + s // 2 * 16, 16), 16)
        m_all[core, rows, s % 2 * 128 : s % 2 * 128 + 128] = third_all[s, 0]
    own_block = m_all.at[core, pl.ds(pl.multiple_of(sub, 16), 48)]
    m_back_x = [to(own_block, ring[o]) for o in (1, 2, 3)]
    for copy in m_back_x:
        copy.wait_recv()
    own_band = rows_at(y, 0, 192)
    up_copy = to(own_band, along_y[1])
    down_copy = to(own_band, along_y[3])
    m_last = [to(own_band, sibling)]

    for copy in d_back:
        copy.wait_recv()
    eighth = core * 4 + x

    def slice_for(device):
        return d_slab.at[:, :, pl.ds(pl.multiple_of(device[1] * D_SLICE, 128), D_SLICE)]

    d_ring = [post(slice_for(device), d_fin.at[eighth], device) for device in ring[1:] + cross[1:] + [sibling]]
    for copy in d_ring:
        copy.start()
    d_fin[eighth] = d_slab[:, :, pl.ds(pl.multiple_of(mp * D_SLICE, 128), D_SLICE)]

    written = []

    def write(src, dst):
        copy = pltpu.make_async_copy(src, dst, write_sems.at[len(written)])
        copy.start()
        written.append(copy)

    def write_band(y_of, half):
        rows = pl.ds(pl.multiple_of(lax.rem(y_of, 4) * 192, 16), 192)
        write(m_all.at[half, rows], m_out.at[half, rows])

    write_band(y, core)
    up_copy.wait_recv()
    relay_up = to(rows_at(y + 3, 0, 96), along_y[1])
    m_last.append(to(rows_at(y + 3, 0, 192), sibling))
    down_copy.wait_recv()
    relay_down = to(rows_at(y + 1, 96, 96), along_y[3])
    m_last.append(to(rows_at(y + 1, 0, 192), sibling))
    write_band(y + 3, core)
    write_band(y + 1, core)
    for copy in d_ring:
        copy.wait_recv()
    write(d_fin, d_out)
    relay_up.wait_recv()
    relay_down.wait_recv()
    m_last.append(to(rows_at(y + 2, 0, 192), sibling))
    write_band(y + 2, core)
    for copy, o in zip(m_last, (0, 3, 1, 2)):
        copy.wait_recv()
        write_band(y + o, other)
    for copy in written:
        copy.wait()

    for s in range(8):

        @pl.when(jnp.logical_not(is_me(targets[s])))
        def _():
            ids_copy(s).wait_send()

    for copy in taken:
        copy.wait_send()


def step_call(*args):
    vmem = pl.BlockSpec(memory_space=pltpu.VMEM)
    smem = pl.BlockSpec(memory_space=pltpu.SMEM)
    hbm = pl.BlockSpec(memory_space=pltpu.HBM)
    dma = pltpu.SemaphoreType.DMA
    f32 = lambda *shape: pltpu.VMEM(shape, F32)
    bf16 = lambda *shape: pltpu.VMEM(shape, BF16)
    i32 = lambda *shape: pltpu.VMEM(shape, jnp.int32)
    return pl.pallas_call(
        step_kernel,
        out_shape=(
            jax.ShapeDtypeStruct((8, 4, 16, D_SLICE), F32),
            jax.ShapeDtypeStruct((2, D_METH, E_HALF), F32),
        ),
        in_specs=[hbm] * 7 + [smem] * 2,
        out_specs=(hbm, hbm),
        scratch_shapes=[
            i32(16, PAIR_DEV),
            i32(16, PAIR_DEV),
            i32(3, 128),
            bf16(D_SLICE, E),
            bf16(VOCAB_DNA, D_SLICE),
            bf16(VOCAB_METH, D_METH),
            bf16(D_METH, E),
            i32(PAIR_DEV, 16),
            i32(16, COLS),
            i32(2, 3, 128),
            i32(ROWS, 128),
            bf16(4 * D_SLICE, ROWS),
            bf16(E, 4 * D_SLICE),
            bf16(D_METH, VOCAB_METH),
            bf16(E, D_METH),
            bf16(D_METH, COLS),
            f32(E, COLS),
            bf16(E, COLS),
            f32(1, COLS),
            f32(E, ROWS),
            f32(1, ROWS),
            bf16(E, ROWS),
            bf16(ROWS, E),
            f32(E, ROWS),
            bf16(ROWS, COLS),
            f32(D_METH, E),
            bf16(2, 4, 4, 48, E_HALF),
            bf16(7, 4, 48, E_HALF),
            f32(4, 48, E_HALF),
            f32(3, 48, E_HALF),
            f32(8, 2, 16, 128),
            f32(7, 2, 16, 128),
            f32(8, 2, 16, 128),
            bf16(E, ROWS),
            bf16(256, ROWS),
            bf16(4, 64, ROWS),
            bf16(3, 64, ROWS),
            f32(4, 16, 4 * D_SLICE),
            bf16(4, 16, 4 * D_SLICE),
            bf16(3, 16, 4 * D_SLICE),
            f32(4, 16, 4 * D_SLICE),
            f32(2, D_METH, E_HALF),
            f32(8, 4, 16, D_SLICE),
            dma((8,)),
            dma((8,)),
            dma((N_COPIES,)),
            dma((N_COPIES,)),
            dma((8,)),
            dma((9,)),
        ],
        compiler_params=pltpu.CompilerParams(
            collective_id=0, has_side_effects=True, vmem_limit_bytes=56 * 1024 * 1024
        ),
        cost_estimate=pl.CostEstimate(flops=19 * 10**9, bytes_accessed=8 * 10**6, transcendentals=5 * 10**6),
        name="contrastive_step",
    )(*args)


def hand_over_kernel(d_in, m_in, d_out, m_out, d_here, m_here, d_turned, in_sems, out_sems):
    m_parts = [(half, pl.ds(first, 192)) for half in range(2) for first in range(0, D_METH, 192)]
    d_parts = [slice(s * 128, (s + 1) * 128) for s in range(E // 128)]
    fetch = [(m_in.at[h, rows], m_here.at[h, rows]) for h, rows in m_parts]
    store = [(m_here.at[h, rows], m_out.at[rows, pl.ds(h * E_HALF, E_HALF)]) for h, rows in m_parts]
    fetch += [(d_in.at[rows], d_here.at[rows]) for rows in d_parts]
    store += [(d_turned.at[:, rows], d_out.at[:, rows]) for rows in d_parts]
    fetch = [pltpu.make_async_copy(*pair, in_sems.at[n]) for n, pair in enumerate(fetch)]
    store = [pltpu.make_async_copy(*pair, out_sems.at[n]) for n, pair in enumerate(store)]
    for copy in fetch:
        copy.start()
    for n in range(len(store)):
        fetch[n].wait()
        if n >= len(m_parts):
            rows = d_parts[n - len(m_parts)]
            d_turned[:, rows] = d_here[rows, :].T
        store[n].start()
    for copy in store:
        copy.wait()


def hand_over(d_part, m_part):
    hbm = pl.BlockSpec(memory_space=pltpu.HBM)
    return pl.pallas_call(
        hand_over_kernel,
        out_shape=(
            jax.ShapeDtypeStruct((D_SLICE, E), F32),
            jax.ShapeDtypeStruct((D_METH, E), F32),
        ),
        in_specs=[hbm, hbm],
        out_specs=(hbm, hbm),
        scratch_shapes=[
            pltpu.VMEM((E, D_SLICE), F32),
            pltpu.VMEM((2, D_METH, E_HALF), F32),
            pltpu.VMEM((D_SLICE, E), F32),
            pltpu.SemaphoreType.DMA((12,)),
            pltpu.SemaphoreType.DMA((12,)),
        ],
        compiler_params=pltpu.CompilerParams(vmem_limit_bytes=56 * 1024 * 1024),
        name="hand_over",
    )(d_part, m_part)


def per_device(
    dna_ids,
    meth_ids,
    pair_index,
    dna_table,
    meth_table,
    dna_proj,
    meth_proj,
    logit_scale,
    logit_bias,
):
    d_part, m_part = step_call(
        dna_ids.T,
        meth_ids.T,
        pair_index.reshape(3, 128),
        dna_table,
        meth_table,
        dna_proj,
        meth_proj,
        logit_scale,
        logit_bias,
    )
    return hand_over(d_part.reshape(E, D_SLICE), m_part)


def solution(mesh):
    placed = (
        P("blk", None),
        P("blk", None),
        P("blk"),
        P(None, "mp"),
        P(),
        P("mp", None),
        P(),
        P(),
        P(),
    )
    return jax.shard_map(
        per_device, mesh=mesh, in_specs=placed, out_specs=(P("mp", None), P()), check_vma=False
    )
```

```python
import jax
import jax.numpy as jnp
from jax import lax
from jax.experimental import pallas as pl
from jax.experimental.pallas import tpu as pltpu
from jax.sharding import PartitionSpec as P

MESH = pl.DeviceIdType.MESH
F32 = jnp.float32
BF16 = jnp.bfloat16
EPS = 1e-06

PAIR_DEV = 384
ROWS = 2 * PAIR_DEV
COLS = 8 * PAIR_DEV
E = 512
D_SLICE = 256
D_METH = 768
VOCAB_DNA = 4096
VOCAB_METH = 512
EMBED = 256
NIBBLES = 0x0F0F0F0F
LOG2E = 1.4426950408889634
E_HALF = 256
N_COPIES = 80

NT = (((1,), (1,)), ((), ()))


def place():
    blk, mp = lax.axis_index("blk"), lax.axis_index("mp")
    z = lax.div(blk, 8)
    y = lax.rem(lax.div(blk, 2), 4)
    x = lax.rem(blk, 2) * 2 + lax.div(mp, 2)
    return blk, mp, z, y, x, lax.rem(mp, 2)


def device_at(z, y, x, core):
    return (z * 8 + y * 2 + lax.div(x, 2), lax.rem(x, 2) * 2 + core)


def signal(device):
    pl.semaphore_signal(
        pltpu.get_barrier_semaphore(), inc=1, device_id=device, device_id_type=MESH
    )


def repeat(first, last, body):
    def step(i, carry):
        body(i)
        return carry

    lax.fori_loop(first, last, step, 0)


def send(src, dst, send_sem, recv_sem, device):
    return pltpu.make_async_remote_copy(
        src_ref=src,
        dst_ref=dst,
        send_sem=send_sem,
        recv_sem=recv_sem,
        device_id=device,
        device_id_type=MESH,
    )


def token_counts(ids, bits, axis):
    place_of = jnp.bitwise_and(ids, 2**bits - 1)
    amount = jnp.left_shift(1, jnp.right_shift(ids, bits) * 4)
    shape = (ids.shape[0], 2**bits) if axis else (2**bits, ids.shape[1])
    spot = lax.broadcasted_iota(jnp.int32, shape, axis)
    even = odd = None
    for first in (0, 8):
        total = jnp.zeros(shape, jnp.int32)
        for t in range(first, first + 8):
            take = (slice(None), slice(t, t + 1)) if axis else (slice(t, t + 1), slice(None))
            total = total + jnp.where(spot == place_of[take], amount[take], 0)
        low = jnp.bitwise_and(total, NIBBLES)
        high = jnp.bitwise_and(jnp.right_shift(total, 4), NIBBLES)
        even, odd = (low, high) if even is None else (even + low, odd + high)
    fields = []
    for f in range(8):
        field = jnp.bitwise_and(jnp.right_shift(odd if f % 2 else even, f // 2 * 8), 255)
        fields.append(field.astype(F32).astype(BF16))
    return fields


def step_kernel(
    dna_ids_hbm,
    meth_ids_hbm,
    pairs_hbm,
    dna_table_hbm,
    meth_table_hbm,
    dna_proj_hbm,
    meth_proj_hbm,
    scale_ref,
    bias_ref,
    d_out,
    m_out,
    dna_ids,
    meth_ids,
    pairs,
    dna_proj,
    dna_table,
    meth_table,
    meth_proj,
    dna_tokens,
    ids_all,
    pair_all,
    pair_wide,
    dna_pooled,
    dna_projt,
    meth_tablet,
    meth_projt,
    meth_pooled,
    meth_unit,
    meth_rows,
    meth_inv,
    dna_unit,
    dna_inv,
    dna_rowst,
    dna_rows,
    row_acc,
    tiles,
    m_acc,
    m_low,
    m_first_in,
    m_second,
    m_second_in,
    third,
    third_in,
    third_all,
    total,
    back_all,
    back_sib,
    back_half,
    back_in,
    d_first,
    d_first_low,
    d_first_in,
    d_slab,
    m_all,
    d_fin,
    ids_send,
    ids_recv,
    z_send,
    z_recv,
    send_sems,
    recv_sems,
    local_sems,
    write_sems,
):
    blk, mp, z, y, x, core = place()
    x_hi = lax.div(x, 2)
    sibling = device_at(z, y, x, 1 - core)
    ring = [device_at(z, y, lax.rem(x + o, 4), core) for o in range(4)]
    cross = [device_at(z, y, lax.rem(x + o, 4), 1 - core) for o in range(4)]
    along_y = [device_at(z, lax.rem(y + o, 4), x, core) for o in range(4)]
    cross_y = [device_at(z, lax.rem(y + o, 4), x, 1 - core) for o in range(4)]
    ring_place = x_hi * 4 + mp
    nearest = lax.rem(lax.div(ring_place + 1, 2), 4)

    taken = []

    def post(src, dst, device):
        n = len(taken)
        copy = send(src, dst, send_sems.at[n], recv_sems.at[n], device)
        taken.append(copy)
        return copy

    fetch = [
        pltpu.make_async_copy(src, dst, local_sems.at[1 + n])
        for n, (src, dst) in enumerate(
            (
                (dna_table_hbm, dna_table),
                (meth_table_hbm, meth_table),
                (meth_proj_hbm, meth_proj),
                (dna_ids_hbm, dna_ids),
                (meth_ids_hbm, meth_ids),
                (pairs_hbm, pairs),
                (dna_proj_hbm, dna_proj),
            )
        )
    ]
    for n in (4, 5, 6, 3, 0, 1, 2):
        fetch[n].start()

    def at_ring_place(z_of, y_of, place_of):
        return device_at(lax.rem(z_of, 8), lax.rem(y_of, 4), lax.div(place_of, 2), lax.rem(place_of, 2))

    def group(dy):
        dz = lax.rem(ring_place + 8 - 2 * dy, 8)
        return lax.rem(z + dz, 8), lax.rem(y + dy, 4)

    def source(dy, half):
        z_of, y_of = group(dy)
        return ((z_of * 4 + y_of) * 2 + half, dy)

    def target(s):
        return at_ring_place(z + 8 - s, y + 4 - mp, lax.rem(s + 2 * mp, 8))

    def is_me(device):
        return jnp.logical_and(device[0] == blk, device[1] == mp)

    def greet(s):
        device = source(lax.div(s, 2), lax.rem(s, 2))

        @pl.when(jnp.logical_not(is_me(device)))
        def _():
            signal(device)

    repeat(0, 8, greet)

    for o in (1, 2, 3):
        signal(ring[o])
        signal(cross[o])
        signal(along_y[o])
        signal(cross_y[o])
    repeat(1, 8, lambda o: signal(device_at(lax.rem(z + o, 8), y, x, core)))
    signal(sibling)
    for n in (3, 4, 5, 6):
        fetch[n].wait()
    dna_tokens[...] = dna_ids[...].T

    def count_dna(i, carry):
        rows = pl.ds(pl.multiple_of(i * 16, 16), 16)
        fields = token_counts(dna_tokens[rows, :], 9, 1)
        for f, field in enumerate(fields):
            if f < 6:
                tiles[rows, f * 512 : (f + 1) * 512] = field
            else:
                low = pl.ds(pl.multiple_of(PAIR_DEV + i * 16, 16), 16)
                tiles[low, (f - 6) * 512 : (f - 5) * 512] = field
        return carry

    lax.fori_loop(0, PAIR_DEV // 16, count_dna, 0)
    to_self = jnp.logical_and(mp == 0, x_hi == 0).astype(jnp.int32)
    pl.semaphore_wait(pltpu.get_barrier_semaphore(), 28 - to_self)

    slot = mp * 2 + x_hi
    slot_lanes = pl.ds(pl.multiple_of(slot * PAIR_DEV, 128), PAIR_DEV)

    def ids_copy(s):
        return send(meth_ids, ids_all.at[:, slot_lanes], ids_send.at[s], ids_recv.at[slot], target(s))

    def give_ids(s):
        @pl.when(jnp.logical_not(is_me(target(s))))
        def _():
            ids_copy(s).start()

        @pl.when(is_me(target(s)))
        def _():
            local = pltpu.make_async_copy(meth_ids, ids_all.at[:, slot_lanes], local_sems.at[0])
            local.start()
            local.wait()

    repeat(0, 8, give_ids)

    pair_copy = post(pairs, pair_all.at[x_hi], ring[2])
    pair_copy.start()
    pair_all[x_hi] = pairs[...]

    dna_projt[:, pl.ds(pl.multiple_of(mp * D_SLICE, 128), D_SLICE)] = dna_proj[...].T
    toward = 1 + 2 * core
    far = device_at(z, y, lax.rem(x + toward, 4), core)
    other_mp = lax.rem(mp + 2, 4)

    def quarter(of):
        return dna_projt.at[:, pl.ds(pl.multiple_of(of * D_SLICE, 128), D_SLICE)]

    proj_far = post(quarter(mp), quarter(mp), far)
    proj_sib = post(quarter(mp), quarter(mp), sibling)
    proj_fwd = post(quarter(other_mp), quarter(other_mp), sibling)
    proj_far.start()
    proj_sib.start()

    fetch[0].wait()
    pooled = jnp.dot(tiles[0:PAIR_DEV, :], dna_table[0:COLS, :], preferred_element_type=F32)
    pooled = pooled + jnp.dot(
        tiles[PAIR_DEV:ROWS, 0 : VOCAB_DNA - COLS], dna_table[COLS:VOCAB_DNA, :], preferred_element_type=F32
    )
    pooled = pooled * 0.0625
    own_lanes = pl.ds(pl.multiple_of(x_hi * PAIR_DEV, 128), PAIR_DEV)
    dna_pooled[pl.ds(pl.multiple_of(mp * D_SLICE, 16), D_SLICE), own_lanes] = pooled.T.astype(BF16)

    def pool_block(x_of, core_of, low=0, count=D_SLICE):
        first = (lax.rem(x_of, 2) * 2 + core_of) * D_SLICE + low
        lanes = pl.ds(pl.multiple_of(lax.div(x_of, 2) * PAIR_DEV, 128), PAIR_DEV)
        return dna_pooled.at[pl.ds(pl.multiple_of(first, 16), count), lanes]

    own = pool_block(x, core)
    from_left = pool_block(lax.rem(x + 3, 4), core)
    from_right = pool_block(lax.rem(x + 1, 4), core)
    pool_right = post(own, own, ring[1])
    pool_left = post(own, own, ring[3])
    pool_sib = post(own, own, sibling)
    pool_right.start()
    pool_left.start()
    pool_sib.start()
    half_left = pool_block(lax.rem(x + 3, 4), core, 0, 128)
    half_right = pool_block(lax.rem(x + 1, 4), core, 128, 128)
    relay_right = [post(half_left, half_left, device) for device in (ring[1], cross[1])]
    relay_left = [post(half_right, half_right, device) for device in (ring[3], cross[3])]
    pool_fwd = [post(part, part, sibling) for part in (from_left, from_right)]

    fetch[1].wait()
    fetch[2].wait()
    meth_tablet[...] = meth_table[...].T
    meth_projt[...] = meth_proj[...].T
    def embed_meth(i, carry):
        dy = lax.rem(nearest + i + lax.div(i, 2) * (5 - 2 * i), 4)
        for half in range(2):
            lanes = pl.ds(pl.multiple_of((dy * 2 + half) * PAIR_DEV, 128), PAIR_DEV)
            arrival = send(
                meth_ids, ids_all.at[:, lanes], ids_send.at[0], ids_recv.at[dy * 2 + half], source(dy, half)
            )

            @pl.when(jnp.logical_not(is_me(source(dy, half))))
            def _():
                arrival.wait_recv()

        def tokens_of(p):
            first = dy * ROWS + p * EMBED
            ids = [ids_all[:, pl.ds(pl.multiple_of(first + 128 * g, 128), 128)] for g in range(EMBED // 128)]
            return jnp.concatenate([jnp.concatenate(token_counts(part, 6, 0), axis=0) for part in ids], axis=1)

        tokens = tokens_of(0)
        for p in range(ROWS // EMBED):
            lanes = pl.ds(pl.multiple_of(dy * ROWS + p * EMBED, 128), EMBED)
            pooled_m = jnp.dot(meth_tablet[...], tokens, preferred_element_type=F32)
            if p + 1 < ROWS // EMBED:
                tokens = tokens_of(p + 1)
            pooled_m = (pooled_m * 0.0625).astype(BF16)
            meth_pooled[:, lanes] = pooled_m
            raw = jnp.dot(meth_projt[...], pooled_m, preferred_element_type=F32)
            inverse = lax.rsqrt(jnp.sum(raw * raw, axis=0, keepdims=True) + EPS)
            unit = raw * inverse
            meth_inv[:, lanes] = inverse
            meth_unit[:, lanes] = unit
            meth_rows[:, lanes] = unit.astype(BF16)
        return carry

    lax.fori_loop(0, 2, embed_meth, 0)
    pool_right.wait_recv()
    for copy in relay_right:
        copy.start()
    pool_left.wait_recv()
    for copy in relay_left:
        copy.start()
    pool_fwd[0].start()
    pool_fwd[1].start()
    proj_far.wait_recv()
    proj_fwd.start()
    lax.fori_loop(2, 4, embed_meth, 0)
    for copy in relay_right + relay_left:
        copy.wait_recv()
    proj_sib.wait_recv()
    proj_fwd.wait_recv()
    pair_copy.wait_recv()
    for h in range(2):
        words = pair_all[h]
        for a in range(3):
            wide = jnp.broadcast_to(words[a : a + 1, :], (128, 128))
            first = h * PAIR_DEV + a * 128
            pair_wide[first : first + 128, :] = wide.T
    pool_sib.wait_recv()
    for copy in pool_fwd:
        copy.wait_recv()

    raw = jnp.dot(dna_projt[...], dna_pooled[...], preferred_element_type=F32)
    inverse = lax.rsqrt(jnp.sum(raw * raw, axis=0, keepdims=True) + EPS)
    unit = raw * inverse
    dna_inv[...] = inverse
    dna_unit[...] = unit
    unit_low = unit.astype(BF16)
    dna_rowst[...] = unit_low
    dna_rows[...] = unit_low.T

    scale = scale_ref[0]
    bias = bias_ref[0]
    slope, offset = scale * -LOG2E, bias * -LOG2E
    def lanes_of(c):
        return slice(c * ROWS, (c + 1) * ROWS)

    def probabilities(c, dots):
        z_of, y_of = group(c)
        partner = pair_wide[...] - (z_of * 4 + y_of) * ROWS
        lower = 1.0 + jnp.exp2(slope * dots + offset)
        prob = pl.reciprocal(lower, approx=True)
        prob = prob * (2.0 - lower * prob)
        for g in range(ROWS // 128):
            part = prob[:, g * 128 : (g + 1) * 128]
            lane = lax.broadcasted_iota(jnp.int32, (ROWS, 128), 1) + g * 128
            first = c * ROWS + g * 128
            tiles[:, first : first + 128] = jnp.where(partner == lane, part - 1.0, part).astype(BF16)

    def back_of(c, col_dots):
        up = scale * col_dots
        unit_m = meth_unit[:, lanes_of(c)]
        inner = jnp.sum(unit_m * up, axis=0, keepdims=True)
        return (meth_inv[:, lanes_of(c)] * (up - unit_m * inner)).astype(BF16)

    def add_head(c, back):
        part = lax.dot_general(meth_pooled[:, lanes_of(c)], back, NT, preferred_element_type=F32)
        m_acc[...] = part if c == 0 else m_acc[...] + part

    last = COLS // ROWS - 1
    for c in range(last + 1):
        rows_m = meth_rows[:, lanes_of(c)]
        dots = jnp.dot(dna_rows[...], rows_m, preferred_element_type=F32)
        if c > 0:
            col_dots = jnp.dot(dna_rowst[...], tiles[:, lanes_of(c - 1)], preferred_element_type=F32)
        probabilities(c, dots)
        if c > 0:
            add_head(c - 1, back_of(c - 1, col_dots))
        part = lax.dot_general(rows_m, tiles[:, lanes_of(c)], NT, preferred_element_type=F32)
        row_acc[...] = part if c == 0 else row_acc[...] + part

    other = 1 - core
    up = scale * row_acc[...]
    inner = jnp.sum(dna_unit[...] * up, axis=0, keepdims=True)
    back_all[...] = (dna_inv[...] * (up - dna_unit[...] * inner)).astype(BF16)
    back_swap = post(back_all.at[pl.ds(pl.multiple_of(other * 256, 16), 256)], back_sib, sibling)
    back_swap.start()

    col_dots = jnp.dot(dna_rowst[...], tiles[:, lanes_of(last)], preferred_element_type=F32)
    add_head(last, back_of(last, col_dots))

    back_swap.wait_recv()
    for a in range(4):
        rows = pl.ds(pl.multiple_of(core * 256 + a * 64, 16), 64)
        both = back_all[rows, :].astype(F32) + back_sib[a * 64 : (a + 1) * 64, :].astype(F32)
        back_half[a] = both.astype(BF16)
    back_x = [post(back_half.at[lax.rem(x + o, 4)], back_in.at[o - 1], ring[o]) for o in (1, 2, 3)]
    for copy in back_x:
        copy.start()
    swap = core == 1

    def pick(one, two):
        return tuple(jnp.where(swap, q, p) for p, q in zip(one, two))

    axis_a = [pick(p, q) for p, q in zip(ring, along_y)]
    axis_b = [pick(q, p) for p, q in zip(ring, along_y)]
    cross_a = [pick(q, p) for p, q in zip(cross, cross_y)]
    at_a = jnp.where(swap, y, x)
    at_b = jnp.where(swap, x, y)
    at_cross = jnp.where(swap, x, y)

    def block_rows(which, a, b):
        return pl.ds(pl.multiple_of(jnp.where(which == 1, a * 192 + b * 48, b * 192 + a * 48), 16), 48)

    def half_lanes(which):
        return pl.ds(pl.multiple_of(which * E_HALF, 128), E_HALF)

    def pack(which):
        def pack_block(i, carry):
            a, b = lax.div(i, 4), lax.rem(i, 4)
            m_low[which, a, b] = m_acc[block_rows(which, a, b), half_lanes(which)].astype(BF16)
            return carry

        lax.fori_loop(0, 16, pack_block, 0)

    pack(other)
    m_a = [
        post(m_low.at[other, lax.rem(at_cross + o, 4)], m_first_in.at[3 + o], sibling if o == 0 else cross_a[o])
        for o in range(4)
    ]
    for copy in m_a:
        copy.start()
    pack(core)
    m_own = [post(m_low.at[core, lax.rem(at_a + o, 4)], m_first_in.at[o - 1], axis_a[o]) for o in (1, 2, 3)]
    for copy in m_own:
        copy.start()
    m_a = m_a + m_own

    for copy in back_x:
        copy.wait_recv()
    back = back_half[x].astype(F32)
    for o in range(3):
        back = back + back_in[o].astype(F32)
    back = back.astype(BF16)
    wide = jnp.concatenate([back, back], axis=0)
    part = lax.dot_general(dna_pooled[...], wide, NT, preferred_element_type=F32).T
    for a in range(4):
        d_first[a] = part[a * 16 : (a + 1) * 16, :]
        d_first_low[a] = part[a * 16 : (a + 1) * 16, :].astype(BF16)
    d_y = [post(d_first_low.at[lax.rem(y + o, 4)], d_first_in.at[o - 1], along_y[o]) for o in (1, 2, 3)]
    for copy in d_y:
        copy.start()

    for copy in d_y:
        copy.wait_recv()
    d_sum = d_first[y]
    for o in range(3):
        d_sum = d_sum + d_first_in[o].astype(F32)
    for s in range(8):
        third[s, 1] = d_sum[:, s * 128 : (s + 1) * 128]

    for copy in m_a:
        copy.wait_recv()

    def add_first(b):
        part = m_acc[block_rows(core, at_a, b), half_lanes(core)]
        for o in range(7):
            part = part + m_first_in[o, b].astype(F32)
        m_second[b] = part

    repeat(0, 4, add_first)
    m_b = [post(m_second.at[lax.rem(at_b + o, 4)], m_second_in.at[o - 1], axis_b[o]) for o in (1, 2, 3)]
    for copy in m_b:
        copy.start()
    for copy in m_b:
        copy.wait_recv()
    m_sum = m_second[at_b]
    for o in range(3):
        m_sum = m_sum + m_second_in[o]
    for s in range(6):
        third[s, 0] = m_sum[s // 2 * 16 : s // 2 * 16 + 16, s % 2 * 128 : s % 2 * 128 + 128]
    third[6, 0] = jnp.zeros((16, 128), F32)
    third[7, 0] = jnp.zeros((16, 128), F32)

    def z_sum(o):
        at = lax.rem(z + o, 8)
        return send(third.at[at], third_in.at[o - 1], z_send.at[o - 1], z_recv.at[o - 1], device_at(at, y, x, core))

    def z_back(o):
        device = device_at(lax.rem(z + o, 8), y, x, core)
        return send(third_all.at[z], third_all.at[z], z_send.at[6 + o], z_recv.at[6 + o], device)

    def add_z(o):
        z_sum(o).wait_recv()
        total[...] = total[...] + third_in[o - 1]

    repeat(1, 8, lambda o: z_sum(o).start())
    total[...] = third[z]
    repeat(1, 8, add_z)
    third_all[z] = total[...]
    repeat(1, 8, lambda o: z_back(o).start())
    repeat(1, 8, lambda o: z_back(o).wait_recv())

    for s in range(8):
        d_slab[y, :, s * 128 : (s + 1) * 128] = third_all[s, 1]
    d_back = [post(d_slab.at[y], d_slab.at[y], along_y[o]) for o in (1, 2, 3)]
    for copy in d_back:
        copy.start()

    def rows_at(y_of, low, rows):
        return m_all.at[core, pl.ds(pl.multiple_of(lax.rem(y_of, 4) * 192 + low, 16), rows)]

    def to(part, device):
        copy = post(part, part, device)
        copy.start()
        return copy

    sub = y * 192 + x * 48
    for s in range(6):
        rows = pl.ds(pl.multiple_of(sub + s // 2 * 16, 16), 16)
        m_all[core, rows, s % 2 * 128 : s % 2 * 128 + 128] = third_all[s, 0]
    own_block = m_all.at[core, pl.ds(pl.multiple_of(sub, 16), 48)]
    m_back_x = [to(own_block, ring[o]) for o in (1, 2, 3)]
    for copy in m_back_x:
        copy.wait_recv()
    own_band = rows_at(y, 0, 192)
    up_copy = to(own_band, along_y[1])
    down_copy = to(own_band, along_y[3])
    m_last = [to(own_band, sibling)]

    for copy in d_back:
        copy.wait_recv()
    eighth = core * 4 + x

    def slice_for(device):
        return d_slab.at[:, :, pl.ds(pl.multiple_of(device[1] * D_SLICE, 128), D_SLICE)]

    d_ring = [post(slice_for(device), d_fin.at[eighth], device) for device in ring[1:] + cross[1:] + [sibling]]
    for copy in d_ring:
        copy.start()
    d_fin[eighth] = d_slab[:, :, pl.ds(pl.multiple_of(mp * D_SLICE, 128), D_SLICE)]

    written = []

    def write(src, dst):
        copy = pltpu.make_async_copy(src, dst, write_sems.at[len(written)])
        copy.start()
        written.append(copy)

    def write_band(y_of, half):
        rows = pl.ds(pl.multiple_of(lax.rem(y_of, 4) * 192, 16), 192)
        write(m_all.at[half, rows], m_out.at[half, rows])

    write_band(y, core)
    up_copy.wait_recv()
    relay_up = to(rows_at(y + 3, 0, 96), along_y[1])
    m_last.append(to(rows_at(y + 3, 0, 192), sibling))
    down_copy.wait_recv()
    relay_down = to(rows_at(y + 1, 96, 96), along_y[3])
    m_last.append(to(rows_at(y + 1, 0, 192), sibling))
    write_band(y + 3, core)
    write_band(y + 1, core)
    for copy in d_ring:
        copy.wait_recv()
    write(d_fin, d_out)
    relay_up.wait_recv()
    relay_down.wait_recv()
    m_last.append(to(rows_at(y + 2, 0, 192), sibling))
    write_band(y + 2, core)
    for copy, o in zip(m_last, (0, 3, 1, 2)):
        copy.wait_recv()
        write_band(y + o, other)
    for copy in written:
        copy.wait()

    def ids_left(s):
        @pl.when(jnp.logical_not(is_me(target(s))))
        def _():
            ids_copy(s).wait_send()

    repeat(0, 8, ids_left)

    for copy in taken:
        copy.wait_send()
    repeat(1, 8, lambda o: z_sum(o).wait_send())
    repeat(1, 8, lambda o: z_back(o).wait_send())


def step_call(*args):
    vmem = pl.BlockSpec(memory_space=pltpu.VMEM)
    smem = pl.BlockSpec(memory_space=pltpu.SMEM)
    hbm = pl.BlockSpec(memory_space=pltpu.HBM)
    dma = pltpu.SemaphoreType.DMA
    f32 = lambda *shape: pltpu.VMEM(shape, F32)
    bf16 = lambda *shape: pltpu.VMEM(shape, BF16)
    i32 = lambda *shape: pltpu.VMEM(shape, jnp.int32)
    return pl.pallas_call(
        step_kernel,
        out_shape=(
            jax.ShapeDtypeStruct((8, 4, 16, D_SLICE), F32),
            jax.ShapeDtypeStruct((2, D_METH, E_HALF), F32),
        ),
        in_specs=[hbm] * 7 + [smem] * 2,
        out_specs=(hbm, hbm),
        scratch_shapes=[
            i32(16, PAIR_DEV),
            i32(16, PAIR_DEV),
            i32(3, 128),
            bf16(D_SLICE, E),
            bf16(VOCAB_DNA, D_SLICE),
            bf16(VOCAB_METH, D_METH),
            bf16(D_METH, E),
            i32(PAIR_DEV, 16),
            i32(16, COLS),
            i32(2, 3, 128),
            i32(ROWS, 128),
            bf16(4 * D_SLICE, ROWS),
            bf16(E, 4 * D_SLICE),
            bf16(D_METH, VOCAB_METH),
            bf16(E, D_METH),
            bf16(D_METH, COLS),
            f32(E, COLS),
            bf16(E, COLS),
            f32(1, COLS),
            f32(E, ROWS),
            f32(1, ROWS),
            bf16(E, ROWS),
            bf16(ROWS, E),
            f32(E, ROWS),
            bf16(ROWS, COLS),
            f32(D_METH, E),
            bf16(2, 4, 4, 48, E_HALF),
            bf16(7, 4, 48, E_HALF),
            f32(4, 48, E_HALF),
            f32(3, 48, E_HALF),
            f32(8, 2, 16, 128),
            f32(7, 2, 16, 128),
            f32(8, 2, 16, 128),
            f32(2, 16, 128),
            bf16(E, ROWS),
            bf16(256, ROWS),
            bf16(4, 64, ROWS),
            bf16(3, 64, ROWS),
            f32(4, 16, 4 * D_SLICE),
            bf16(4, 16, 4 * D_SLICE),
            bf16(3, 16, 4 * D_SLICE),
            f32(4, 16, 4 * D_SLICE),
            f32(2, D_METH, E_HALF),
            f32(8, 4, 16, D_SLICE),
            dma((8,)),
            dma((8,)),
            dma((14,)),
            dma((14,)),
            dma((N_COPIES,)),
            dma((N_COPIES,)),
            dma((8,)),
            dma((9,)),
        ],
        compiler_params=pltpu.CompilerParams(
            collective_id=0, has_side_effects=True, vmem_limit_bytes=56 * 1024 * 1024
        ),
        cost_estimate=pl.CostEstimate(flops=19 * 10**9, bytes_accessed=8 * 10**6, transcendentals=5 * 10**6),
        name="contrastive_step",
    )(*args)


def hand_over_kernel(d_in, m_in, d_out, m_out, d_here, m_here, d_turned, in_sems, out_sems):
    m_parts = [(half, pl.ds(first, 192)) for half in range(2) for first in range(0, D_METH, 192)]
    d_parts = [slice(s * 128, (s + 1) * 128) for s in range(E // 128)]
    fetch = [(m_in.at[h, rows], m_here.at[h, rows]) for h, rows in m_parts]
    store = [(m_here.at[h, rows], m_out.at[rows, pl.ds(h * E_HALF, E_HALF)]) for h, rows in m_parts]
    fetch += [(d_in.at[rows], d_here.at[rows]) for rows in d_parts]
    store += [(d_turned.at[:, rows], d_out.at[:, rows]) for rows in d_parts]
    fetch = [pltpu.make_async_copy(*pair, in_sems.at[n]) for n, pair in enumerate(fetch)]
    store = [pltpu.make_async_copy(*pair, out_sems.at[n]) for n, pair in enumerate(store)]
    for copy in fetch:
        copy.start()
    for n in range(len(store)):
        fetch[n].wait()
        if n >= len(m_parts):
            rows = d_parts[n - len(m_parts)]
            d_turned[:, rows] = d_here[rows, :].T
        store[n].start()
    for copy in store:
        copy.wait()


def hand_over(d_part, m_part):
    hbm = pl.BlockSpec(memory_space=pltpu.HBM)
    return pl.pallas_call(
        hand_over_kernel,
        out_shape=(
            jax.ShapeDtypeStruct((D_SLICE, E), F32),
            jax.ShapeDtypeStruct((D_METH, E), F32),
        ),
        in_specs=[hbm, hbm],
        out_specs=(hbm, hbm),
        scratch_shapes=[
            pltpu.VMEM((E, D_SLICE), F32),
            pltpu.VMEM((2, D_METH, E_HALF), F32),
            pltpu.VMEM((D_SLICE, E), F32),
            pltpu.SemaphoreType.DMA((12,)),
            pltpu.SemaphoreType.DMA((12,)),
        ],
        compiler_params=pltpu.CompilerParams(vmem_limit_bytes=56 * 1024 * 1024),
        name="hand_over",
    )(d_part, m_part)


def per_device(
    dna_ids,
    meth_ids,
    pair_index,
    dna_table,
    meth_table,
    dna_proj,
    meth_proj,
    logit_scale,
    logit_bias,
):
    d_part, m_part = step_call(
        dna_ids.T,
        meth_ids.T,
        pair_index.reshape(3, 128),
        dna_table,
        meth_table,
        dna_proj,
        meth_proj,
        logit_scale,
        logit_bias,
    )
    return hand_over(d_part.reshape(E, D_SLICE), m_part)


def solution(mesh):
    placed = (
        P("blk", None),
        P("blk", None),
        P("blk"),
        P(None, "mp"),
        P(),
        P("mp", None),
        P(),
        P(),
        P(),
    )
    return jax.shard_map(
        per_device, mesh=mesh, in_specs=placed, out_specs=(P("mp", None), P()), check_vma=False
    )
```

```python
import jax
import jax.numpy as jnp
from jax import lax
from jax.experimental import pallas as pl
from jax.experimental.pallas import tpu as pltpu
from jax.sharding import PartitionSpec as P

MESH = pl.DeviceIdType.MESH
F32 = jnp.float32
BF16 = jnp.bfloat16
EPS = 1e-06

PAIR_DEV = 384
ROWS = 2 * PAIR_DEV
COLS = 8 * PAIR_DEV
E = 512
D_SLICE = 256
D_METH = 768
VOCAB_DNA = 4096
VOCAB_METH = 512
EMBED = 256
PART = 256
NIBBLES = 0x0F0F0F0F
LOG2E = 1.4426950408889634
E_HALF = 256
N_COPIES = 80

NT = (((1,), (1,)), ((), ()))


def place():
    blk, mp = lax.axis_index("blk"), lax.axis_index("mp")
    z = lax.div(blk, 8)
    y = lax.rem(lax.div(blk, 2), 4)
    x = lax.rem(blk, 2) * 2 + lax.div(mp, 2)
    return blk, mp, z, y, x, lax.rem(mp, 2)


def device_at(z, y, x, core):
    return (z * 8 + y * 2 + lax.div(x, 2), lax.rem(x, 2) * 2 + core)


def signal(device):
    pl.semaphore_signal(
        pltpu.get_barrier_semaphore(), inc=1, device_id=device, device_id_type=MESH
    )


def send(src, dst, send_sem, recv_sem, device):
    return pltpu.make_async_remote_copy(
        src_ref=src,
        dst_ref=dst,
        send_sem=send_sem,
        recv_sem=recv_sem,
        device_id=device,
        device_id_type=MESH,
    )


def token_counts(ids, bits, axis):
    place_of = jnp.bitwise_and(ids, 2**bits - 1)
    amount = jnp.left_shift(1, jnp.right_shift(ids, bits) * 4)
    shape = (ids.shape[0], 2**bits) if axis else (2**bits, ids.shape[1])
    spot = lax.broadcasted_iota(jnp.int32, shape, axis)
    even = odd = None
    for first in (0, 8):
        total = jnp.zeros(shape, jnp.int32)
        for t in range(first, first + 8):
            take = (slice(None), slice(t, t + 1)) if axis else (slice(t, t + 1), slice(None))
            total = total + jnp.where(spot == place_of[take], amount[take], 0)
        low = jnp.bitwise_and(total, NIBBLES)
        high = jnp.bitwise_and(jnp.right_shift(total, 4), NIBBLES)
        even, odd = (low, high) if even is None else (even + low, odd + high)
    fields = []
    for f in range(8):
        field = jnp.bitwise_and(jnp.right_shift(odd if f % 2 else even, f // 2 * 8), 255)
        fields.append(field.astype(F32).astype(BF16))
    return fields


def step_kernel(
    dna_ids_hbm,
    meth_ids_hbm,
    pairs_hbm,
    dna_table_hbm,
    meth_table_hbm,
    dna_proj_hbm,
    meth_proj_hbm,
    scale_ref,
    bias_ref,
    d_out,
    m_out,
    dna_ids,
    meth_ids,
    pairs,
    dna_proj,
    dna_table,
    meth_table,
    meth_proj,
    dna_tokens,
    ids_all,
    pair_all,
    pair_wide,
    dna_pooled,
    dna_projt,
    meth_tablet,
    meth_projt,
    meth_pooled,
    meth_unit,
    meth_rows,
    meth_inv,
    dna_unit,
    dna_inv,
    dna_rowst,
    dna_rows,
    row_acc,
    tiles,
    m_acc,
    m_low,
    m_first_in,
    m_second,
    m_second_in,
    third,
    third_in,
    third_all,
    back_all,
    back_sib,
    back_half,
    back_in,
    d_first,
    d_first_low,
    d_first_in,
    d_slab,
    m_all,
    d_fin,
    ids_send,
    ids_recv,
    send_sems,
    recv_sems,
    local_sems,
    write_sems,
):
    blk, mp, z, y, x, core = place()
    x_hi = lax.div(x, 2)
    sibling = device_at(z, y, x, 1 - core)
    ring = [device_at(z, y, lax.rem(x + o, 4), core) for o in range(4)]
    cross = [device_at(z, y, lax.rem(x + o, 4), 1 - core) for o in range(4)]
    along_y = [device_at(z, lax.rem(y + o, 4), x, core) for o in range(4)]
    cross_y = [device_at(z, lax.rem(y + o, 4), x, 1 - core) for o in range(4)]
    along_z = [device_at(lax.rem(z + o, 8), y, x, core) for o in range(8)]
    ring_place = x_hi * 4 + mp
    nearest = lax.rem(lax.div(ring_place + 1, 2), 4)

    taken = []

    def post(src, dst, device):
        n = len(taken)
        copy = send(src, dst, send_sems.at[n], recv_sems.at[n], device)
        taken.append(copy)
        return copy

    fetch = [
        pltpu.make_async_copy(src, dst, local_sems.at[1 + n])
        for n, (src, dst) in enumerate(
            (
                (dna_table_hbm, dna_table),
                (meth_table_hbm, meth_table),
                (meth_proj_hbm, meth_proj),
                (dna_ids_hbm, dna_ids),
                (meth_ids_hbm, meth_ids),
                (pairs_hbm, pairs),
                (dna_proj_hbm, dna_proj),
            )
        )
    ]
    for n in (4, 5, 6, 3, 0, 1, 2):
        fetch[n].start()

    def at_ring_place(z_of, y_of, place_of):
        return device_at(lax.rem(z_of, 8), lax.rem(y_of, 4), lax.div(place_of, 2), lax.rem(place_of, 2))

    def group(dy):
        dz = lax.rem(ring_place + 8 - 2 * dy, 8)
        return lax.rem(z + dz, 8), lax.rem(y + dy, 4)

    def source(dy, half):
        z_of, y_of = group(dy)
        return ((z_of * 4 + y_of) * 2 + half, dy)

    targets = [at_ring_place(z + 8 - s, y + 4 - mp, lax.rem(s + 2 * mp, 8)) for s in range(8)]
    sources = [source(s // 2, s % 2) for s in range(8)]

    def is_me(device):
        return jnp.logical_and(device[0] == blk, device[1] == mp)

    for s in range(8):

        @pl.when(jnp.logical_not(is_me(sources[s])))
        def _():
            signal(sources[s])

    for o in (1, 2, 3):
        signal(ring[o])
        signal(cross[o])
        signal(along_y[o])
        signal(cross_y[o])
    for o in range(1, 8):
        signal(along_z[o])
    signal(sibling)
    for n in (3, 4, 5, 6):
        fetch[n].wait()
    dna_tokens[...] = dna_ids[...].T

    def count_dna(i, carry):
        rows = pl.ds(pl.multiple_of(i * 16, 16), 16)
        fields = token_counts(dna_tokens[rows, :], 9, 1)
        for f, field in enumerate(fields):
            if f < 6:
                tiles[rows, f * 512 : (f + 1) * 512] = field
            else:
                low = pl.ds(pl.multiple_of(PAIR_DEV + i * 16, 16), 16)
                tiles[low, (f - 6) * 512 : (f - 5) * 512] = field
        return carry

    lax.fori_loop(0, PAIR_DEV // 16, count_dna, 0)
    to_self = jnp.logical_and(mp == 0, x_hi == 0).astype(jnp.int32)
    pl.semaphore_wait(pltpu.get_barrier_semaphore(), 28 - to_self)

    slot = mp * 2 + x_hi
    slot_lanes = pl.ds(pl.multiple_of(slot * PAIR_DEV, 128), PAIR_DEV)

    def ids_copy(s):
        return send(meth_ids, ids_all.at[:, slot_lanes], ids_send.at[s], ids_recv.at[slot], targets[s])

    for s in range(8):

        @pl.when(jnp.logical_not(is_me(targets[s])))
        def _():
            ids_copy(s).start()

        @pl.when(is_me(targets[s]))
        def _():
            local = pltpu.make_async_copy(meth_ids, ids_all.at[:, slot_lanes], local_sems.at[0])
            local.start()
            local.wait()

    pair_copy = post(pairs, pair_all.at[x_hi], ring[2])
    pair_copy.start()
    pair_all[x_hi] = pairs[...]

    dna_projt[:, pl.ds(pl.multiple_of(mp * D_SLICE, 128), D_SLICE)] = dna_proj[...].T
    toward = 1 + 2 * core
    far = device_at(z, y, lax.rem(x + toward, 4), core)
    other_mp = lax.rem(mp + 2, 4)

    def quarter(of):
        return dna_projt.at[:, pl.ds(pl.multiple_of(of * D_SLICE, 128), D_SLICE)]

    proj_far = post(quarter(mp), quarter(mp), far)
    proj_sib = post(quarter(mp), quarter(mp), sibling)
    proj_fwd = post(quarter(other_mp), quarter(other_mp), sibling)
    proj_far.start()
    proj_sib.start()

    fetch[0].wait()
    pooled = jnp.dot(tiles[0:PAIR_DEV, :], dna_table[0:COLS, :], preferred_element_type=F32)
    pooled = pooled + jnp.dot(
        tiles[PAIR_DEV:ROWS, 0 : VOCAB_DNA - COLS], dna_table[COLS:VOCAB_DNA, :], preferred_element_type=F32
    )
    pooled = pooled * 0.0625
    own_lanes = pl.ds(pl.multiple_of(x_hi * PAIR_DEV, 128), PAIR_DEV)
    dna_pooled[pl.ds(pl.multiple_of(mp * D_SLICE, 16), D_SLICE), own_lanes] = pooled.T.astype(BF16)

    def pool_block(x_of, core_of, low=0, count=D_SLICE):
        first = (lax.rem(x_of, 2) * 2 + core_of) * D_SLICE + low
        lanes = pl.ds(pl.multiple_of(lax.div(x_of, 2) * PAIR_DEV, 128), PAIR_DEV)
        return dna_pooled.at[pl.ds(pl.multiple_of(first, 16), count), lanes]

    own = pool_block(x, core)
    from_left = pool_block(lax.rem(x + 3, 4), core)
    from_right = pool_block(lax.rem(x + 1, 4), core)
    pool_right = post(own, own, ring[1])
    pool_left = post(own, own, ring[3])
    pool_sib = post(own, own, sibling)
    pool_right.start()
    pool_left.start()
    pool_sib.start()
    half_left = pool_block(lax.rem(x + 3, 4), core, 0, 128)
    half_right = pool_block(lax.rem(x + 1, 4), core, 128, 128)
    relay_right = [post(half_left, half_left, device) for device in (ring[1], cross[1])]
    relay_left = [post(half_right, half_right, device) for device in (ring[3], cross[3])]
    pool_fwd = [post(part, part, sibling) for part in (from_left, from_right)]

    fetch[1].wait()
    fetch[2].wait()
    meth_tablet[...] = meth_table[...].T
    meth_projt[...] = meth_proj[...].T
    def embed_meth(i, carry):
        dy = lax.rem(nearest + i + lax.div(i, 2) * (5 - 2 * i), 4)
        for half in range(2):
            lanes = pl.ds(pl.multiple_of((dy * 2 + half) * PAIR_DEV, 128), PAIR_DEV)
            arrival = send(
                meth_ids, ids_all.at[:, lanes], ids_send.at[0], ids_recv.at[dy * 2 + half], source(dy, half)
            )

            @pl.when(jnp.logical_not(is_me(source(dy, half))))
            def _():
                arrival.wait_recv()

        for p in range(ROWS // EMBED):
            first = pl.multiple_of(dy * ROWS + p * EMBED, 128)
            lanes = pl.ds(first, EMBED)
            ids = [ids_all[:, pl.ds(pl.multiple_of(first + 128 * g, 128), 128)] for g in range(EMBED // 128)]
            tokens = jnp.concatenate(
                [jnp.concatenate(token_counts(part, 6, 0), axis=0) for part in ids], axis=1
            )
            pooled_m = jnp.dot(meth_tablet[...], tokens, preferred_element_type=F32)
            pooled_m = (pooled_m * 0.0625).astype(BF16)
            meth_pooled[:, lanes] = pooled_m
            raw = jnp.dot(meth_projt[...], pooled_m, preferred_element_type=F32)
            inverse = lax.rsqrt(jnp.sum(raw * raw, axis=0, keepdims=True) + EPS)
            unit = raw * inverse
            meth_inv[:, lanes] = inverse
            meth_unit[:, lanes] = unit
            meth_rows[:, lanes] = unit.astype(BF16)
        return carry

    lax.fori_loop(0, 2, embed_meth, 0)
    pool_right.wait_recv()
    for copy in relay_right:
        copy.start()
    pool_left.wait_recv()
    for copy in relay_left:
        copy.start()
    pool_fwd[0].start()
    pool_fwd[1].start()
    proj_far.wait_recv()
    proj_fwd.start()
    lax.fori_loop(2, 4, embed_meth, 0)
    for copy in relay_right + relay_left:
        copy.wait_recv()
    proj_sib.wait_recv()
    proj_fwd.wait_recv()
    pair_copy.wait_recv()
    for h in range(2):
        words = pair_all[h]
        for a in range(3):
            wide = jnp.broadcast_to(words[a : a + 1, :], (128, 128))
            first = h * PAIR_DEV + a * 128
            pair_wide[first : first + 128, :] = wide.T
    pool_sib.wait_recv()
    for copy in pool_fwd:
        copy.wait_recv()

    raw = jnp.dot(dna_projt[...], dna_pooled[...], preferred_element_type=F32)
    inverse = lax.rsqrt(jnp.sum(raw * raw, axis=0, keepdims=True) + EPS)
    unit = raw * inverse
    dna_inv[...] = inverse
    dna_unit[...] = unit
    unit_low = unit.astype(BF16)
    dna_rowst[...] = unit_low
    dna_rows[...] = unit_low.T

    scale = scale_ref[0]
    bias = bias_ref[0]
    slope, offset = scale * -LOG2E, bias * -LOG2E
    def lanes_of(c):
        return slice(c * ROWS, (c + 1) * ROWS)

    def part_of(c, p):
        return slice(c * ROWS + p * PART, c * ROWS + (p + 1) * PART)

    def logit_dots(c, p):
        return jnp.dot(dna_rows[...], meth_rows[:, part_of(c, p)], preferred_element_type=F32)

    def probabilities(c, p, partner, dots):
        lower = 1.0 + jnp.exp2(slope * dots + offset)
        prob = pl.reciprocal(lower, approx=True)
        prob = prob * (2.0 - lower * prob)
        for g in range(PART // 128):
            part = prob[:, g * 128 : (g + 1) * 128]
            low = p * PART + g * 128
            lane = lax.broadcasted_iota(jnp.int32, (ROWS, 128), 1) + low
            first = c * ROWS + low
            tiles[:, first : first + 128] = jnp.where(partner == lane, part - 1.0, part).astype(BF16)

    def col_dots(c, p):
        return jnp.dot(dna_rowst[...], tiles[:, part_of(c, p)], preferred_element_type=F32)

    def back_of(c, p, dots):
        up = scale * dots
        unit_m = meth_unit[:, part_of(c, p)]
        inner = jnp.sum(unit_m * up, axis=0, keepdims=True)
        return (meth_inv[:, part_of(c, p)] * (up - unit_m * inner)).astype(BF16)

    def add_head(c, parts):
        back = jnp.concatenate(parts, axis=1)
        part = lax.dot_general(meth_pooled[:, lanes_of(c)], back, NT, preferred_element_type=F32)
        m_acc[...] = part if c == 0 else m_acc[...] + part

    def add_rows(c):
        part = lax.dot_general(meth_rows[:, lanes_of(c)], tiles[:, lanes_of(c)], NT, preferred_element_type=F32)
        row_acc[...] = part if c == 0 else row_acc[...] + part

    last = COLS // ROWS - 1
    n_parts = ROWS // PART
    dots = logit_dots(0, 0)
    for c in range(last + 1):
        z_of, y_of = group(c)
        partner = pair_wide[...] - (z_of * 4 + y_of) * ROWS
        parts = []
        for p in range(n_parts):
            here = dots
            if c > 0:
                cols = col_dots(c - 1, p)
            if p + 1 < n_parts:
                dots = logit_dots(c, p + 1)
            probabilities(c, p, partner, here)
            if c > 0:
                parts.append(back_of(c - 1, p, cols))
        if c < last:
            dots = logit_dots(c + 1, 0)
        if c > 0:
            add_head(c - 1, parts)
        add_rows(c)

    other = 1 - core
    up = scale * row_acc[...]
    inner = jnp.sum(dna_unit[...] * up, axis=0, keepdims=True)
    back_all[...] = (dna_inv[...] * (up - dna_unit[...] * inner)).astype(BF16)
    back_swap = post(back_all.at[pl.ds(pl.multiple_of(other * 256, 16), 256)], back_sib, sibling)
    back_swap.start()

    add_head(last, [back_of(last, p, col_dots(last, p)) for p in range(n_parts)])

    back_swap.wait_recv()
    for a in range(4):
        rows = pl.ds(pl.multiple_of(core * 256 + a * 64, 16), 64)
        both = back_all[rows, :].astype(F32) + back_sib[a * 64 : (a + 1) * 64, :].astype(F32)
        back_half[a] = both.astype(BF16)
    back_x = [post(back_half.at[lax.rem(x + o, 4)], back_in.at[o - 1], ring[o]) for o in (1, 2, 3)]
    for copy in back_x:
        copy.start()
    swap = core == 1

    def pick(one, two):
        return tuple(jnp.where(swap, q, p) for p, q in zip(one, two))

    axis_a = [pick(p, q) for p, q in zip(ring, along_y)]
    axis_b = [pick(q, p) for p, q in zip(ring, along_y)]
    cross_a = [pick(q, p) for p, q in zip(cross, cross_y)]
    at_a = jnp.where(swap, y, x)
    at_b = jnp.where(swap, x, y)
    at_cross = jnp.where(swap, x, y)

    def block_rows(which, a, b):
        return pl.ds(pl.multiple_of(jnp.where(which == 1, a * 192 + b * 48, b * 192 + a * 48), 16), 48)

    def half_lanes(which):
        return pl.ds(pl.multiple_of(which * E_HALF, 128), E_HALF)

    def pack(which):
        def pack_block(i, carry):
            a, b = lax.div(i, 4), lax.rem(i, 4)
            m_low[which, a, b] = m_acc[block_rows(which, a, b), half_lanes(which)].astype(BF16)
            return carry

        lax.fori_loop(0, 16, pack_block, 0)

    pack(other)
    m_a = [
        post(m_low.at[other, lax.rem(at_cross + o, 4)], m_first_in.at[3 + o], sibling if o == 0 else cross_a[o])
        for o in range(4)
    ]
    for copy in m_a:
        copy.start()
    pack(core)
    m_own = [post(m_low.at[core, lax.rem(at_a + o, 4)], m_first_in.at[o - 1], axis_a[o]) for o in (1, 2, 3)]
    for copy in m_own:
        copy.start()
    m_a = m_a + m_own

    for copy in back_x:
        copy.wait_recv()
    back = back_half[x].astype(F32)
    for o in range(3):
        back = back + back_in[o].astype(F32)
    back = back.astype(BF16)
    wide = jnp.concatenate([back, back], axis=0)
    part = lax.dot_general(dna_pooled[...], wide, NT, preferred_element_type=F32).T
    for a in range(4):
        d_first[a] = part[a * 16 : (a + 1) * 16, :]
        d_first_low[a] = part[a * 16 : (a + 1) * 16, :].astype(BF16)
    d_y = [post(d_first_low.at[lax.rem(y + o, 4)], d_first_in.at[o - 1], along_y[o]) for o in (1, 2, 3)]
    for copy in d_y:
        copy.start()

    for copy in d_y:
        copy.wait_recv()
    d_sum = d_first[y]
    for o in range(3):
        d_sum = d_sum + d_first_in[o].astype(F32)
    for s in range(8):
        third[s, 1] = d_sum[:, s * 128 : (s + 1) * 128]

    for copy in m_a:
        copy.wait_recv()
    for b in range(4):
        part = m_acc[block_rows(core, at_a, b), half_lanes(core)]
        for o in range(7):
            part = part + m_first_in[o, b].astype(F32)
        m_second[b] = part
    m_b = [post(m_second.at[lax.rem(at_b + o, 4)], m_second_in.at[o - 1], axis_b[o]) for o in (1, 2, 3)]
    for copy in m_b:
        copy.start()
    for copy in m_b:
        copy.wait_recv()
    m_sum = m_second[at_b]
    for o in range(3):
        m_sum = m_sum + m_second_in[o]
    for s in range(6):
        third[s, 0] = m_sum[s // 2 * 16 : s // 2 * 16 + 16, s % 2 * 128 : s % 2 * 128 + 128]
    third[6, 0] = jnp.zeros((16, 128), F32)
    third[7, 0] = jnp.zeros((16, 128), F32)

    z_sum = [post(third.at[lax.rem(z + o, 8)], third_in.at[o - 1], along_z[o]) for o in range(1, 8)]
    for copy in z_sum:
        copy.start()
    for copy in z_sum:
        copy.wait_recv()
    total = third[z]
    for o in range(7):
        total = total + third_in[o]
    third_all[z] = total
    z_back = [post(third_all.at[z], third_all.at[z], along_z[o]) for o in range(1, 8)]
    for copy in z_back:
        copy.start()
    for copy in z_back:
        copy.wait_recv()

    for s in range(8):
        d_slab[y, :, s * 128 : (s + 1) * 128] = third_all[s, 1]
    d_back = [post(d_slab.at[y], d_slab.at[y], along_y[o]) for o in (1, 2, 3)]
    for copy in d_back:
        copy.start()

    def rows_at(y_of, low, rows):
        return m_all.at[core, pl.ds(pl.multiple_of(lax.rem(y_of, 4) * 192 + low, 16), rows)]

    def to(part, device):
        copy = post(part, part, device)
        copy.start()
        return copy

    sub = y * 192 + x * 48
    for s in range(6):
        rows = pl.ds(pl.multiple_of(sub + s // 2 * 16, 16), 16)
        m_all[core, rows, s % 2 * 128 : s % 2 * 128 + 128] = third_all[s, 0]
    own_block = m_all.at[core, pl.ds(pl.multiple_of(sub, 16), 48)]
    m_back_x = [to(own_block, ring[o]) for o in (1, 2, 3)]
    for copy in m_back_x:
        copy.wait_recv()
    own_band = rows_at(y, 0, 192)
    up_copy = to(own_band, along_y[1])
    down_copy = to(own_band, along_y[3])
    m_last = [to(own_band, sibling)]

    for copy in d_back:
        copy.wait_recv()
    eighth = core * 4 + x

    def slice_for(device):
        return d_slab.at[:, :, pl.ds(pl.multiple_of(device[1] * D_SLICE, 128), D_SLICE)]

    d_ring = [post(slice_for(device), d_fin.at[eighth], device) for device in ring[1:] + cross[1:] + [sibling]]
    for copy in d_ring:
        copy.start()
    d_fin[eighth] = d_slab[:, :, pl.ds(pl.multiple_of(mp * D_SLICE, 128), D_SLICE)]

    written = []

    def write(src, dst):
        copy = pltpu.make_async_copy(src, dst, write_sems.at[len(written)])
        copy.start()
        written.append(copy)

    def write_band(y_of, half):
        rows = pl.ds(pl.multiple_of(lax.rem(y_of, 4) * 192, 16), 192)
        write(m_all.at[half, rows], m_out.at[half, rows])

    write_band(y, core)
    up_copy.wait_recv()
    relay_up = to(rows_at(y + 3, 0, 96), along_y[1])
    m_last.append(to(rows_at(y + 3, 0, 192), sibling))
    down_copy.wait_recv()
    relay_down = to(rows_at(y + 1, 96, 96), along_y[3])
    m_last.append(to(rows_at(y + 1, 0, 192), sibling))
    write_band(y + 3, core)
    write_band(y + 1, core)
    for copy in d_ring:
        copy.wait_recv()
    write(d_fin, d_out)
    relay_up.wait_recv()
    relay_down.wait_recv()
    m_last.append(to(rows_at(y + 2, 0, 192), sibling))
    write_band(y + 2, core)
    for copy, o in zip(m_last, (0, 3, 1, 2)):
        copy.wait_recv()
        write_band(y + o, other)
    for copy in written:
        copy.wait()

    for s in range(8):

        @pl.when(jnp.logical_not(is_me(targets[s])))
        def _():
            ids_copy(s).wait_send()

    for copy in taken:
        copy.wait_send()


def step_call(*args):
    vmem = pl.BlockSpec(memory_space=pltpu.VMEM)
    smem = pl.BlockSpec(memory_space=pltpu.SMEM)
    hbm = pl.BlockSpec(memory_space=pltpu.HBM)
    dma = pltpu.SemaphoreType.DMA
    f32 = lambda *shape: pltpu.VMEM(shape, F32)
    bf16 = lambda *shape: pltpu.VMEM(shape, BF16)
    i32 = lambda *shape: pltpu.VMEM(shape, jnp.int32)
    return pl.pallas_call(
        step_kernel,
        out_shape=(
            jax.ShapeDtypeStruct((8, 4, 16, D_SLICE), F32),
            jax.ShapeDtypeStruct((2, D_METH, E_HALF), F32),
        ),
        in_specs=[hbm] * 7 + [smem] * 2,
        out_specs=(hbm, hbm),
        scratch_shapes=[
            i32(16, PAIR_DEV),
            i32(16, PAIR_DEV),
            i32(3, 128),
            bf16(D_SLICE, E),
            bf16(VOCAB_DNA, D_SLICE),
            bf16(VOCAB_METH, D_METH),
            bf16(D_METH, E),
            i32(PAIR_DEV, 16),
            i32(16, COLS),
            i32(2, 3, 128),
            i32(ROWS, 128),
            bf16(4 * D_SLICE, ROWS),
            bf16(E, 4 * D_SLICE),
            bf16(D_METH, VOCAB_METH),
            bf16(E, D_METH),
            bf16(D_METH, COLS),
            f32(E, COLS),
            bf16(E, COLS),
            f32(1, COLS),
            f32(E, ROWS),
            f32(1, ROWS),
            bf16(E, ROWS),
            bf16(ROWS, E),
            f32(E, ROWS),
            bf16(ROWS, COLS),
            f32(D_METH, E),
            bf16(2, 4, 4, 48, E_HALF),
            bf16(7, 4, 48, E_HALF),
            f32(4, 48, E_HALF),
            f32(3, 48, E_HALF),
            f32(8, 2, 16, 128),
            f32(7, 2, 16, 128),
            f32(8, 2, 16, 128),
            bf16(E, ROWS),
            bf16(256, ROWS),
            bf16(4, 64, ROWS),
            bf16(3, 64, ROWS),
            f32(4, 16, 4 * D_SLICE),
            bf16(4, 16, 4 * D_SLICE),
            bf16(3, 16, 4 * D_SLICE),
            f32(4, 16, 4 * D_SLICE),
            f32(2, D_METH, E_HALF),
            f32(8, 4, 16, D_SLICE),
            dma((8,)),
            dma((8,)),
            dma((N_COPIES,)),
            dma((N_COPIES,)),
            dma((8,)),
            dma((9,)),
        ],
        compiler_params=pltpu.CompilerParams(
            collective_id=0, has_side_effects=True, vmem_limit_bytes=56 * 1024 * 1024
        ),
        cost_estimate=pl.CostEstimate(flops=19 * 10**9, bytes_accessed=8 * 10**6, transcendentals=5 * 10**6),
        name="contrastive_step",
    )(*args)


def hand_over_kernel(d_in, m_in, d_out, m_out, d_here, m_here, d_turned, in_sems, out_sems):
    m_parts = [(half, pl.ds(first, 192)) for half in range(2) for first in range(0, D_METH, 192)]
    d_parts = [slice(s * 128, (s + 1) * 128) for s in range(E // 128)]
    fetch = [(m_in.at[h, rows], m_here.at[h, rows]) for h, rows in m_parts]
    store = [(m_here.at[h, rows], m_out.at[rows, pl.ds(h * E_HALF, E_HALF)]) for h, rows in m_parts]
    fetch += [(d_in.at[rows], d_here.at[rows]) for rows in d_parts]
    store += [(d_turned.at[:, rows], d_out.at[:, rows]) for rows in d_parts]
    fetch = [pltpu.make_async_copy(*pair, in_sems.at[n]) for n, pair in enumerate(fetch)]
    store = [pltpu.make_async_copy(*pair, out_sems.at[n]) for n, pair in enumerate(store)]
    for copy in fetch:
        copy.start()
    for n in range(len(store)):
        fetch[n].wait()
        if n >= len(m_parts):
            rows = d_parts[n - len(m_parts)]
            d_turned[:, rows] = d_here[rows, :].T
        store[n].start()
    for copy in store:
        copy.wait()


def hand_over(d_part, m_part):
    hbm = pl.BlockSpec(memory_space=pltpu.HBM)
    return pl.pallas_call(
        hand_over_kernel,
        out_shape=(
            jax.ShapeDtypeStruct((D_SLICE, E), F32),
            jax.ShapeDtypeStruct((D_METH, E), F32),
        ),
        in_specs=[hbm, hbm],
        out_specs=(hbm, hbm),
        scratch_shapes=[
            pltpu.VMEM((E, D_SLICE), F32),
            pltpu.VMEM((2, D_METH, E_HALF), F32),
            pltpu.VMEM((D_SLICE, E), F32),
            pltpu.SemaphoreType.DMA((12,)),
            pltpu.SemaphoreType.DMA((12,)),
        ],
        compiler_params=pltpu.CompilerParams(vmem_limit_bytes=56 * 1024 * 1024),
        name="hand_over",
    )(d_part, m_part)


def per_device(
    dna_ids,
    meth_ids,
    pair_index,
    dna_table,
    meth_table,
    dna_proj,
    meth_proj,
    logit_scale,
    logit_bias,
):
    d_part, m_part = step_call(
        dna_ids.T,
        meth_ids.T,
        pair_index.reshape(3, 128),
        dna_table,
        meth_table,
        dna_proj,
        meth_proj,
        logit_scale,
        logit_bias,
    )
    return hand_over(d_part.reshape(E, D_SLICE), m_part)


def solution(mesh):
    placed = (
        P("blk", None),
        P("blk", None),
        P("blk"),
        P(None, "mp"),
        P(),
        P("mp", None),
        P(),
        P(),
        P(),
    )
    return jax.shard_map(
        per_device, mesh=mesh, in_specs=placed, out_specs=(P("mp", None), P()), check_vma=False
    )
```
